32 devices in a mesh: blk: 4 (over x, core), dp: 8 (over z, y).
Axes of the slice: x: 2, y: 2, z: 4, core: 2. Of those that a mesh axis runs over, the one named last changes fastest.
Arguments:
- hidden_in: bfloat16 [8, 4, 320, 2048], P('dp', 'blk'), may hold values from -6 to 6
- cotangent: bfloat16 [8, 4, 320, 2048], P('dp', 'blk'), may hold values from -6 to 6
- seq_lengths: int32 [8, 2], P('dp'), may hold values from 128 to 1024, as said below
- block_order: int32 [2, 4], replicated, may hold values from 0 to 3, each once within a row
- w_qkv: bfloat16 [2048, 6144], P(('blk', 'dp')), may hold values from -0.1875 to 0.1875
- w_out: bfloat16 [2048, 2048], P(('blk', 'dp')), may hold values from -0.5 to 0.5
- w_up: bfloat16 [2048, 8192], P(('blk', 'dp')), may hold values from -0.125 to 0.125
- w_down: bfloat16 [8192, 2048], P(('blk', 'dp')), may hold values from -0.09375 to 0.09375
- norm_gains: float32 [2, 2048], replicated, may hold values from 0.5 to 1.5
- norm_biases: float32 [2, 2048], replicated, may hold values from -4 to 4
- hidden_bias: float32 [8192], replicated, may hold values from -6 to 6
Outputs:
- layer_out: bfloat16 [8, 4, 320, 2048], P('dp', 'blk')
- grad_input: bfloat16 [8, 4, 320, 2048], P('dp', 'blk')
- grad_w_qkv: float32 [2048, 6144], P(('blk', 'dp'))
- grad_w_out: float32 [2048, 2048], P(('blk', 'dp'))
- grad_w_up: float32 [2048, 8192], P(('blk', 'dp'))
- grad_w_down: float32 [8192, 2048], P(('blk', 'dp'))
- grad_norm_gains: float32 [2, 2048], P(None, ('blk', 'dp'))
- grad_norm_biases: float32 [2, 2048], P(None, ('blk', 'dp'))
- grad_hidden_bias: float32 [8192], P(('blk', 'dp'))
The draws below stay inside these ranges and needn't reach their ends.
Inputs may be any that keep to these rules, and one draw needn't show every extreme that they name: `seq_lengths`: column 0 lies from 512 to 1024, column 1 from 128 to 256; in each row one of the two equals its bucket length, and column 0 does in at least one row. `block_order`: each row holds every block number once.
All inputs are finite; a program needn't handle non-finite values.
Results may differ from the reference program's by a relative error of at most 0.015.
Values may be sent and summed in bfloat16 or wider, within the bound.
No kernel may reach another device: no remote copies, remote signals or barrier semaphores. Data moves between devices by JAX's collectives and lax.ppermute only.
A program may use at most 768 MiB of HBM per device.

```python
import math
import jax
import jax.numpy as jnp
from jax import lax

D = 2048
HEADS = 16
HEAD = 128
FF = 8192
BLK_A = 256
BLK_B = 64
NBLOCKS = 4
NSEQ = 8
LEN_A = 1024
LEN_B = 256
ROWS = 320


def draw_seq_lengths(key, part):
    key = jax.random.fold_in(key, 11)
    first_key, second_key, pick_key, forced_key = jax.random.split(key, 4)
    column_a = jax.random.randint(first_key, (NSEQ,), LEN_A // 2, LEN_A + 1)
    column_b = jax.random.randint(second_key, (NSEQ,), LEN_B // 2, LEN_B + 1)
    picked = jax.random.randint(pick_key, (NSEQ,), 0, 2)
    forced = jax.random.randint(forced_key, (), 0, NSEQ)
    full_first = (picked == 0) | (jnp.arange(NSEQ) == forced)
    column_a = jnp.where(full_first, LEN_A, column_a)
    column_b = jnp.where(full_first, column_b, LEN_B)
    return jnp.stack([column_a, column_b], axis=1).astype(jnp.int32)


def shard_levels(stream_key, shape, shards, low, top_value):
    def one(position, shards_of):
        steps = jax.random.uniform(jax.random.fold_in(jax.random.fold_in(stream_key, 6), position), (shards_of,), jnp.float32, low / len(shards), top_value / len(shards))
        return jnp.repeat(jnp.exp(steps), shape[position] // shards_of).reshape((-1,) + (1,) * (len(shape) - position - 1))

    level = one(*shards[0])
    for cut in shards[1:]:
        level = level * one(*cut)
    return level


def normal_values(rng, dims, scale, reach, shards=(), kind=jnp.bfloat16):
    values = jax.random.normal(rng, dims, jnp.float32) * scale
    if len(shards) > 0:
        values = shard_levels(rng, dims, shards, -0.22, 0.18) * values
    return jnp.clip(values, min=-reach, max=reach).astype(kind)


def setup_inputs(seed: int = 0) -> dict:
    splits = jax.random.split(jax.random.key(seed), 12)
    hidden_in = normal_values(splits[0], (NSEQ, NBLOCKS, ROWS, D), 1.0, 6.0, ((0, 8), (1, 4)))
    cotangent = normal_values(splits[1], (NSEQ, NBLOCKS, ROWS, D), 1.0, 6.0, ((0, 8), (1, 4)))
    seq_lengths = draw_seq_lengths(jax.random.fold_in(splits[11], 71), 0)
    block_order = jax.vmap(lambda own: jax.random.permutation(own, NBLOCKS))(jax.random.split(splits[3], 2)).reshape((2, NBLOCKS)).astype(jnp.int32)
    w_qkv = normal_values(splits[4], (D, 3 * D), (D // 2) ** -0.5, 0.1875, ((0, 32),))
    w_out = normal_values(splits[5], (D, D), (D // 16) ** -0.5, 0.5, ((0, 32),))
    w_up = normal_values(splits[6], (D, FF), D ** -0.5, 0.125, ((0, 32),))
    w_down = normal_values(splits[7], (FF, D), (FF // 2) ** -0.5, 0.09375, ((0, 32),))
    norm_gains = jnp.clip(1.0 + 0.1 * jax.random.normal(splits[8], (2, D), jnp.float32), 0.5, 1.5)
    norm_biases = normal_values(splits[9], (2, D), 0.3, 4.0, (), jnp.float32)
    hidden_bias = normal_values(splits[10], (FF,), 0.5, 6.0, (), jnp.float32)
    return {"hidden_in": hidden_in, "cotangent": cotangent, "seq_lengths": seq_lengths, "block_order": block_order, "w_qkv": w_qkv, "w_out": w_out, "w_up": w_up, "w_down": w_down, "norm_gains": norm_gains, "norm_biases": norm_biases, "hidden_bias": hidden_bias}


EPSILON = 1e-05
NEGATIVE = -1e+30
HIGHEST = lax.Precision.HIGHEST

@jax.custom_vjp
def low(v):
    return lax.optimization_barrier(v.astype(jnp.bfloat16)).astype(jnp.float32)

@jax.custom_vjp
def low_back(v):
    return v

def low_keep(v):
    return (low(v), None)

def low_pass(kept, grad):
    return (grad,)

def back_keep(v):
    return (v, None)

def back_low(kept, grad):
    return (low(grad),)
low.defvjp(low_keep, low_pass)
low_back.defvjp(back_keep, back_low)

def layer_norm(value, gain, bias):
    center = value - lax.optimization_barrier(jnp.mean(value, axis=-1, keepdims=True))
    spread = lax.optimization_barrier(jnp.mean(center * center, axis=-1, keepdims=True))
    return center * lax.rsqrt(spread + EPSILON) * gain + bias

def attend(queries, keys, values, query_places, key_places, length):
    scores = jnp.einsum('qhd,khd->hqk', queries, keys, precision=HIGHEST) * (1.0 / math.sqrt(HEAD))
    scores = low_back(scores)
    allowed = (key_places[None, :] <= query_places[:, None]) & (key_places[None, :] < length)
    scores = jnp.where(allowed[None], scores, NEGATIVE)
    probs = low(jax.nn.softmax(scores, axis=-1))
    return jnp.einsum('hqk,khd->qhd', probs, values, precision=HIGHEST)

def layer(inputs, w_qkv, w_out, w_up, w_down, gains, biases, hidden_bias, places, length):
    count = inputs.shape[0]
    width = inputs.shape[1]
    normed = low(layer_norm(inputs, gains[0], biases[0]))
    projected = low(low_back(jnp.dot(normed, w_qkv, precision=HIGHEST)))
    queries = projected[:, :width].reshape(count, HEADS, HEAD)
    keys = projected[:, width:2 * width].reshape(count, HEADS, HEAD)
    values = projected[:, 2 * width:].reshape(count, HEADS, HEAD)
    block = min(512, count)
    blocks = count // block
    query_blocks = queries.reshape(blocks, block, HEADS, HEAD)
    place_blocks = places.reshape(blocks, block)

    def one_block(record):
        return attend(record[0], keys, values, record[1], places, length)
    attended = lax.map(jax.checkpoint(one_block), (query_blocks, place_blocks)).reshape(count, width)
    attended = low(low_back(attended))
    mixed = inputs + low_back(jnp.dot(attended, w_out, precision=HIGHEST))
    second = low(layer_norm(mixed, gains[1], biases[1]))
    hidden_pre = low_back(jnp.dot(second, w_up, precision=HIGHEST) + hidden_bias)
    activated = low(jax.nn.gelu(hidden_pre, approximate=True))
    return mixed + low_back(jnp.dot(activated, w_down, precision=HIGHEST))

def micro_batch(hidden_in, cotangent, seq_lengths, block_order, params, first, block_rows, column):
    total = NBLOCKS * block_rows
    inputs = hidden_in[:, :, first:first + block_rows, :].astype(jnp.float32).reshape(NSEQ, total, D)
    grads_out = cotangent[:, :, first:first + block_rows, :].astype(jnp.float32).reshape(NSEQ, total, D)
    places = (block_order[column][:, None] * block_rows + jnp.arange(block_rows, dtype=jnp.int32)[None, :]).reshape(total).astype(jnp.int32)
    lengths = seq_lengths[:, column]

    def one_sequence(running, record):
        seq_in, seq_cot, length = record

        def forward(seq_x, w_qkv, w_out, w_up, w_down, gains, biases, hidden_bias):
            return layer(seq_x, w_qkv, w_out, w_up, w_down, gains, biases, hidden_bias, places, length)
        result, pull = jax.vjp(forward, seq_in, *params)
        grads = pull(seq_cot)
        running = tuple((held + new for held, new in zip(running, grads[1:])))
        return (running, (result, grads[0]))
    start = tuple((jnp.zeros_like(param) for param in params))
    sums, (results, grad_inputs) = lax.scan(one_sequence, start, (inputs, grads_out, lengths))
    return (sums, results.reshape(NSEQ, NBLOCKS, block_rows, D), grad_inputs.reshape(NSEQ, NBLOCKS, block_rows, D))

def reference(hidden_in, cotangent, seq_lengths, block_order, w_qkv, w_out, w_up, w_down, norm_gains, norm_biases, hidden_bias):
    params = (w_qkv.astype(jnp.float32), w_out.astype(jnp.float32), w_up.astype(jnp.float32), w_down.astype(jnp.float32), norm_gains.astype(jnp.float32), norm_biases.astype(jnp.float32), hidden_bias.astype(jnp.float32))
    sums_a, out_a, grad_a = micro_batch(hidden_in, cotangent, seq_lengths, block_order, params, 0, BLK_A, 0)
    sums_b, out_b, grad_b = micro_batch(hidden_in, cotangent, seq_lengths, block_order, params, BLK_A, BLK_B, 1)
    sums = tuple((first + later for first, later in zip(sums_a, sums_b)))
    layer_out = jnp.concatenate([out_a, out_b], axis=2).astype(jnp.bfloat16)
    grad_input = jnp.concatenate([grad_a, grad_b], axis=2).astype(jnp.bfloat16)
    return (layer_out, grad_input, sums[0], sums[1], sums[2], sums[3], sums[4], sums[5], sums[6])
```

```python
import jax
import jax.numpy as jnp
from jax import lax
from jax.sharding import PartitionSpec as P

HEAD = 128
BLK_A = 256
BLK_B = 64

EPSILON = 1e-05
NEGATIVE = -1e30
BF16 = jnp.bfloat16
F32 = jnp.float32


def inner_size(count):
    inner = 1
    while (inner * 2) ** 2 <= count:
        inner *= 2
    return inner


def layer_norm(value, gain, bias):
    center = value - jnp.mean(value, axis=-1, keepdims=True)
    spread = jnp.mean(center * center, axis=-1, keepdims=True)
    return center * lax.rsqrt(spread + EPSILON) * gain + bias


def contract_last(left, right):
    return lax.dot_general(
        left, right, (((1,), (1,)), ((), ())), preferred_element_type=F32
    )


def contract_first(left, right):
    return lax.dot_general(
        left, right, (((0,), (0,)), ((), ())), preferred_element_type=F32
    )


def flip(block, bits):
    count = lax.axis_size("blk")
    return lax.ppermute(block, "blk", [(i ^ bits, i) for i in range(count)])


def outer_shift(block, distance):
    count = lax.axis_size("dp")
    inner = inner_size(count)
    outer = count // inner
    route = [
        (z * inner + y, ((z + distance) % outer) * inner + y)
        for z in range(outer)
        for y in range(inner)
    ]
    return lax.ppermute(block, "dp", route)


def inner_shift(block, distance):
    count = lax.axis_size("dp")
    inner = inner_size(count)
    route = [
        (z * inner + y, z * inner + (y + distance) % inner)
        for z in range(count // inner)
        for y in range(inner)
    ]
    return lax.ppermute(block, "dp", route)


def pick(array, index, axis):
    return lax.dynamic_index_in_dim(array, index, axis, keepdims=False)


def place(whole, part, index, axis):
    return lax.dynamic_update_index_in_dim(whole, part, index, axis)


def exchange_blk(parts):
    count = lax.axis_size("blk")
    index = lax.axis_index("blk")
    out = parts
    for bits in range(1, count):
        out = place(out, flip(pick(parts, index ^ bits, 0), bits), index ^ bits, 0)
    return out


def gather_dp(part):
    count = lax.axis_size("dp")
    inner = inner_size(count)
    outer = count // inner
    index = lax.axis_index("dp")
    z, y = index // inner, index % inner
    groups, rows, columns = part.shape
    whole = jnp.zeros((groups, count, rows, columns), part.dtype)
    for far in range(outer):
        from_z = part if far == 0 else outer_shift(part, far)
        for near in range(inner):
            piece = from_z if near == 0 else inner_shift(from_z, near)
            source = ((z - far) % outer) * inner + (y - near) % inner
            whole = place(whole, piece, source, 1)
    return whole.reshape(groups * count * rows, columns)


def scatter_dp(total, groups):
    count = lax.axis_size("dp")
    inner = inner_size(count)
    outer = count // inner
    index = lax.axis_index("dp")
    z, y = index // inner, index % inner
    columns = total.shape[1]
    parts = total.astype(BF16).reshape(groups, outer, inner, -1, columns)
    held = pick(parts, y, 2).astype(F32)
    for near in range(1, inner):
        held = held + inner_shift(pick(parts, (y + near) % inner, 2), near).astype(F32)
    low = held.astype(BF16)
    out = pick(low, z, 1).astype(F32)
    for far in range(1, outer):
        out = out + outer_shift(pick(low, (z + far) % outer, 1), far).astype(F32)
    return out


def gather_blk(part):
    count = lax.axis_size("blk")
    index = lax.axis_index("blk")
    whole = jnp.zeros((count,) + part.shape, part.dtype)
    for far in range(0, count, 2):
        piece = part if far == 0 else flip(part, far)
        whole = place(whole, piece, index ^ far, 0)
        whole = place(whole, flip(piece, 1), index ^ far ^ 1, 0)
    return whole


def scatter_blk(total):
    count = lax.axis_size("blk")
    index = lax.axis_index("blk")
    far_index, core = index // 2, index % 2
    parts = total.astype(BF16).reshape((count // 2, 2) + total.shape[1:])
    held = pick(parts, core, 1).astype(F32) + flip(pick(parts, core ^ 1, 1), 1).astype(F32)
    low = held.astype(BF16)
    out = pick(low, far_index, 0).astype(F32)
    for far in range(1, count // 2):
        out = out + flip(pick(low, far_index ^ far, 0), far * 2).astype(F32)
    return out


def sum_small(total):
    blk, dp = lax.axis_size("blk"), lax.axis_size("dp")
    count, width = total.shape
    parts = total.reshape(count, blk, dp, -1).transpose(1, 2, 0, 3)
    got = jnp.sum(lax.all_to_all(parts, "blk", 0, 0), axis=0)
    return jnp.sum(lax.all_to_all(got, "dp", 0, 0), axis=0)


def allowed_of(places, length):
    return (places[None, :] <= places[:, None]) & (places[None, :] < length)


def scores_of(queries, keys, allowed):
    scores = jnp.einsum("qhd,khd->hqk", queries, keys, preferred_element_type=F32) * HEAD ** (-0.5)
    return jnp.where(allowed[None], scores, NEGATIVE)


def attention_forward(queries, keys, values, allowed):
    scores = scores_of(queries, keys, allowed)
    peak = jnp.max(scores, axis=-1, keepdims=True)
    log_total = peak + jnp.log(jnp.sum(jnp.exp(scores - peak), axis=-1, keepdims=True))
    probs = jnp.where(allowed[None], jnp.exp(scores - log_total), 0.0).astype(BF16)
    attended = jnp.einsum("hqk,khd->qhd", probs, values, preferred_element_type=F32)
    return attended, log_total


def attention_backward(queries, keys, values, attended, grad_attended, log_total, allowed):
    scale = HEAD ** (-0.5)
    delta = jnp.einsum("qhd,qhd->hq", grad_attended.astype(F32), attended)
    scores = scores_of(queries, keys, allowed)
    probs = jnp.where(allowed[None], jnp.exp(scores - log_total), 0.0)
    grad_values = jnp.einsum(
        "hqk,qhd->khd", probs.astype(BF16), grad_attended, preferred_element_type=F32
    )
    grad_probs = jnp.einsum("qhd,khd->hqk", grad_attended, values, preferred_element_type=F32)
    grad_scores = (probs * (grad_probs - delta[..., None])).astype(BF16)
    grad_queries = scale * jnp.einsum("hqk,khd->qhd", grad_scores, keys, preferred_element_type=F32)
    grad_keys = scale * jnp.einsum("hqk,qhd->khd", grad_scores, queries, preferred_element_type=F32)
    return grad_queries, grad_keys, grad_values


def body(
    hidden_in,
    cotangent,
    seq_lengths,
    block_order,
    w_qkv,
    w_out,
    w_up,
    w_down,
    norm_gains,
    norm_biases,
    hidden_bias,
):
    blk = lax.axis_size("blk")
    index = lax.axis_index("blk")
    rows, width = hidden_in.shape[2:]
    heads = width // HEAD // blk
    part = width // blk
    x = hidden_in.reshape(rows, width).astype(F32)
    cot_low = cotangent.reshape(rows, width)
    splits = ((0, BLK_A), (BLK_A, BLK_A + BLK_B))

    shard = w_qkv.shape[0]
    hidden = hidden_bias.shape[0] // blk
    out_full = gather_dp(w_out[None])
    qkv_part = exchange_blk(w_qkv.reshape(shard, 3, blk, part).transpose(2, 0, 1, 3).reshape(blk, shard, 3 * part))
    qkv_full = gather_dp(qkv_part)
    up_part = exchange_blk(w_up.reshape(shard, blk, hidden).transpose(1, 0, 2))
    up_full = gather_dp(up_part)
    down_full = gather_dp(w_down[None])

    normed, first_pull = jax.vjp(layer_norm, x, norm_gains[0], norm_biases[0])
    normed_all = gather_blk(normed.astype(BF16)).reshape(blk * rows, width)
    projected = jnp.dot(normed_all, qkv_full, preferred_element_type=F32).astype(BF16)
    projected = projected.reshape(blk, rows, 3, heads, HEAD)

    attended_parts, saved = [], []
    for column, (first, last) in enumerate(splits):
        count = last - first
        places = (
            block_order[column][:, None] * count + jnp.arange(count, dtype=jnp.int32)[None, :]
        ).reshape(blk * count)
        allowed = allowed_of(places, seq_lengths[0, column])
        mine = projected[:, first:last].reshape(blk * count, 3, heads, HEAD)
        queries, keys, values = mine[:, 0], mine[:, 1], mine[:, 2]
        attended, log_total = attention_forward(queries, keys, values, allowed)
        attended_parts.append(attended.astype(BF16).reshape(blk, count, part))
        saved.append((queries, keys, values, attended, log_total, allowed))
    attended_low = jnp.concatenate(attended_parts, axis=1).reshape(blk * rows, part)
    mixed = x + scatter_blk(
        jnp.dot(attended_low, out_full, preferred_element_type=F32).reshape(blk, rows, width)
    )
    second, second_pull = jax.vjp(layer_norm, mixed, norm_gains[1], norm_biases[1])
    second_all = gather_blk(second.astype(BF16)).reshape(blk * rows, width)
    bias_part = lax.dynamic_slice_in_dim(hidden_bias, index * hidden, hidden)
    hidden_pre = jnp.dot(second_all, up_full, preferred_element_type=F32) + bias_part
    activated, gelu_pull = jax.vjp(lambda v: jax.nn.gelu(v, approximate=True), hidden_pre)
    activated_low = activated.astype(BF16)
    result = mixed + scatter_blk(
        jnp.dot(activated_low, down_full, preferred_element_type=F32).reshape(blk, rows, width)
    )

    cot_all = gather_blk(cot_low).reshape(blk * rows, width)
    down_sum = scatter_dp(contract_first(activated_low, cot_all), 1)
    (grad_hidden,) = gelu_pull(contract_last(cot_all, down_full))
    grad_hidden_low = grad_hidden.astype(BF16)
    hidden_sum = jnp.sum(grad_hidden_low.astype(F32), axis=0)
    grad_second = scatter_blk(contract_last(grad_hidden_low, up_full).reshape(blk, rows, width))
    up_sum = scatter_dp(contract_first(second_all, grad_hidden_low), blk)
    grad_mixed_norm, gain_two, bias_two = second_pull(grad_second)
    grad_mixed = cot_low.astype(F32) + grad_mixed_norm
    mixed_all = gather_blk(grad_mixed.astype(BF16)).reshape(blk * rows, width)
    grad_attended = contract_last(mixed_all, out_full).astype(BF16).reshape(blk, rows, heads, HEAD)
    out_sum = scatter_dp(contract_first(attended_low, mixed_all), 1)
    grad_parts = []
    for (first, last), (queries, keys, values, attended, log_total, allowed) in zip(splits, saved):
        grads = attention_backward(
            queries,
            keys,
            values,
            attended,
            grad_attended[:, first:last].reshape(-1, heads, HEAD),
            log_total,
            allowed,
        )
        grads = jnp.concatenate([g.astype(BF16).reshape(-1, part) for g in grads], axis=1)
        grad_parts.append(grads.reshape(blk, last - first, 3 * part))
    grad_projected = jnp.concatenate(grad_parts, axis=1).reshape(blk * rows, 3 * part)
    qkv_sum = scatter_dp(contract_first(normed_all, grad_projected), blk)
    grad_normed = scatter_blk(contract_last(grad_projected, qkv_full).reshape(blk, rows, width))
    grad_input_norm, gain_one, bias_one = first_pull(grad_normed)
    grad_input = (grad_mixed + grad_input_norm).astype(BF16)

    grad_qkv = exchange_blk(qkv_sum.astype(BF16)).astype(F32)
    grad_qkv = grad_qkv.reshape(blk, shard, 3, part).transpose(1, 2, 0, 3).reshape(shard, 3 * width)
    grad_up = exchange_blk(up_sum.astype(BF16)).astype(F32).transpose(1, 0, 2).reshape(shard, -1)
    norms = sum_small(jnp.stack([gain_one, gain_two, bias_one, bias_two]))
    dp = lax.axis_size("dp")
    grad_hidden_bias = jnp.sum(lax.all_to_all(hidden_sum.reshape(dp, -1), "dp", 0, 0), axis=0)
    return (
        result.astype(BF16).reshape(1, 1, rows, width),
        grad_input.reshape(1, 1, rows, width),
        grad_qkv,
        out_sum[0],
        grad_up,
        down_sum[0],
        norms[:2],
        norms[2:],
        grad_hidden_bias,
    )


def solution(mesh):
    return jax.shard_map(
        body,
        mesh=mesh,
        in_specs=(
            P("dp", "blk", None, None),
            P("dp", "blk", None, None),
            P("dp", None),
            P(),
            P(("blk", "dp"), None),
            P(("blk", "dp"), None),
            P(("blk", "dp"), None),
            P(("blk", "dp"), None),
            P(),
            P(),
            P(),
        ),
        out_specs=(
            P("dp", "blk", None, None),
            P("dp", "blk", None, None),
            P(("blk", "dp"), None),
            P(("blk", "dp"), None),
            P(("blk", "dp"), None),
            P(("blk", "dp"), None),
            P(None, ("blk", "dp")),
            P(None, ("blk", "dp")),
            P(("blk", "dp")),
        ),
        check_vma=False,
    )
```

```python
import jax
import jax.numpy as jnp
from jax import lax
from jax.sharding import PartitionSpec as P

HEAD = 128
BLK_A = 256
BLK_B = 64

EPSILON = 1e-05
NEGATIVE = -1e30
BF16 = jnp.bfloat16
F32 = jnp.float32


def after(value, *others):
    return lax.optimization_barrier((value, others))[0]


def layer_norm(value, gain, bias):
    center = value - jnp.mean(value, axis=-1, keepdims=True)
    spread = jnp.mean(center * center, axis=-1, keepdims=True)
    return center * lax.rsqrt(spread + EPSILON) * gain + bias


def contract_last(left, right):
    return lax.dot_general(
        left, right, (((1,), (1,)), ((), ())), preferred_element_type=F32
    )


def contract_first(left, right):
    return lax.dot_general(
        left, right, (((0,), (0,)), ((), ())), preferred_element_type=F32
    )


def flip(axis, bits, block):
    count = lax.axis_size(axis)
    return lax.ppermute(block, axis, [(i ^ bits, i) for i in range(count)])


def flip_core(block):
    return flip("blk", 1, block)


def flip_x(block):
    return flip("blk", 2, block)


def flip_y(block):
    return flip("dp", 1, block)


def lines():
    count = lax.axis_size("dp")
    return [[z * 2 + y for z in range(count // 2)] for y in range(2)]


def gather_z(part, axis):
    return lax.all_gather(part, "dp", axis_index_groups=lines(), axis=axis, tiled=True)


def scatter_z(total, axis):
    return lax.psum_scatter(
        total, "dp", axis_index_groups=lines(), scatter_dimension=axis, tiled=True
    )


def by_y(own, other):
    y = lax.axis_index("dp") % 2
    return jnp.where(y == 0, own, other), jnp.where(y == 0, other, own)


def exchange(cut):
    y = lax.axis_index("dp") % 2
    other = flip_y(cut(1 - y))
    both = jnp.stack(by_y(cut(y), other), axis=1)
    return lax.all_to_all(both, "blk", 0, 0)


def gather_plane(part):
    half = part.shape[0] // 2
    from_x, from_y, from_core = flip_x(part), flip_y(part), flip_core(part)
    diagonal = jnp.concatenate([flip_y(from_x[:half]), flip_x(from_y[half:])], axis=0)
    mine = [part, from_x, from_y, diagonal]
    return jnp.concatenate(
        mine + [from_core] + [flip_core(piece) for piece in mine[1:]], axis=0
    )


def scatter_plane(product, rows):
    half = rows // 2
    got = flip_core(product(4, 8).astype(BF16))
    held = product(0, 4) + got.astype(F32)
    own, to_x, to_y, across = [held[i * rows : (i + 1) * rows] for i in range(4)]
    across = across.astype(BF16)
    x_across, y_across = flip_x(across[:half]), flip_y(across[half:])
    x_top = flip_x(to_x[:half].astype(BF16))
    y_bottom = flip_y(to_y[half:].astype(BF16))
    y_top = flip_y((to_y[:half] + x_across.astype(F32)).astype(BF16))
    x_bottom = flip_x((to_x[half:] + y_across.astype(F32)).astype(BF16))
    top = own[:half] + x_top.astype(F32) + y_top.astype(F32)
    bottom = own[half:] + x_bottom.astype(F32) + y_bottom.astype(F32)
    return jnp.concatenate([top, bottom], axis=0)


def sum_over(total, axis, bits):
    while bits < lax.axis_size(axis):
        total = total + flip(axis, bits, total)
        bits *= 2
    return total


def allowed_of(places, length):
    return (places[None, :] <= places[:, None]) & (places[None, :] < length)


def scores_of(queries, keys, allowed):
    scores = jnp.einsum("qhd,khd->hqk", queries, keys, preferred_element_type=F32) * HEAD ** (-0.5)
    return jnp.where(allowed[None], scores, NEGATIVE)


def attention_forward(queries, keys, values, allowed):
    scores = scores_of(queries, keys, allowed)
    peak = jnp.max(scores, axis=-1, keepdims=True)
    log_total = peak + jnp.log(jnp.sum(jnp.exp(scores - peak), axis=-1, keepdims=True))
    probs = jnp.where(allowed[None], jnp.exp(scores - log_total), 0.0).astype(BF16)
    attended = jnp.einsum("hqk,khd->qhd", probs, values, preferred_element_type=F32)
    return attended, log_total


def attention_backward(queries, keys, values, attended, grad_attended, log_total, allowed):
    scale = HEAD ** (-0.5)
    delta = jnp.einsum("qhd,qhd->hq", grad_attended.astype(F32), attended)
    scores = scores_of(queries, keys, allowed)
    probs = jnp.where(allowed[None], jnp.exp(scores - log_total), 0.0)
    grad_values = jnp.einsum(
        "hqk,qhd->khd", probs.astype(BF16), grad_attended, preferred_element_type=F32
    )
    grad_probs = jnp.einsum("qhd,khd->hqk", grad_attended, values, preferred_element_type=F32)
    grad_scores = (probs * (grad_probs - delta[..., None])).astype(BF16)
    grad_queries = scale * jnp.einsum("hqk,khd->qhd", grad_scores, keys, preferred_element_type=F32)
    grad_keys = scale * jnp.einsum("hqk,qhd->khd", grad_scores, queries, preferred_element_type=F32)
    return grad_queries, grad_keys, grad_values


def body(
    hidden_in,
    cotangent,
    seq_lengths,
    block_order,
    w_qkv,
    w_out,
    w_up,
    w_down,
    norm_gains,
    norm_biases,
    hidden_bias,
):
    blk, dp = lax.axis_size("blk"), lax.axis_size("dp")
    lanes = dp // 2
    b, d = lax.axis_index("blk"), lax.axis_index("dp")
    z, y = d // 2, d % 2
    rows, width = hidden_in.shape[2:]
    pairs = width // HEAD // blk // 2
    part = pairs * HEAD
    shard = w_qkv.shape[0]
    units = w_down.shape[0]
    x = hidden_in.reshape(rows, width).astype(F32)
    cot_low = cotangent.reshape(rows, width)
    splits = ((0, BLK_A), (BLK_A, BLK_A + BLK_B))

    def cut_qkv(to_y):
        view = w_qkv.reshape(shard, 3, blk, pairs, 2, HEAD)
        view = lax.dynamic_index_in_dim(view, to_y, 4, keepdims=False)
        return view.transpose(2, 0, 1, 3, 4).reshape(blk, shard, 3 * part)

    def cut_up(to_y):
        view = w_up.reshape(shard, blk, lanes, 2, units)
        view = lax.dynamic_index_in_dim(view, to_y, 3, keepdims=False)
        return view.transpose(1, 0, 2, 3).reshape(blk, shard, lanes * units)

    pieces = [[p for p in range(dp) if (p * shard // HEAD) % 2 == to_y] for to_y in range(2)]
    route = [(pieces[to_y][lane], lane * 2 + to_y) for to_y in range(2) for lane in range(lanes)]

    out_full = gather_z(lax.ppermute(w_out, "dp", route), 0)
    qkv_part = exchange(cut_qkv).reshape(blk, 2 * shard, 3 * part)
    qkv_full = gather_z(qkv_part, 1).reshape(width, 3 * part)
    up_part = exchange(cut_up).reshape(blk, 2 * shard, lanes * units)
    up_full = gather_z(up_part, 1).reshape(width, lanes * units)
    down_full = gather_z(w_down, 0)

    normed, first_pull = jax.vjp(layer_norm, x, norm_gains[0], norm_biases[0])
    normed_all = gather_plane(normed.astype(BF16))
    cot_all = gather_plane(after(cot_low, normed_all))
    projected = jnp.dot(normed_all, qkv_full, preferred_element_type=F32).astype(BF16)
    held = projected.reshape(2, 2, 2, rows, 3, pairs, HEAD)
    lengths = [seq_lengths, flip_y(seq_lengths)]

    def sequences(array, select):
        return [select(array[:, s, :, first:last]) for first, last in splits for s in range(2)]

    def back(parts):
        joined = []
        for column, (first, last) in enumerate(splits):
            pair = [p.reshape(2, 2, last - first, -1) for p in parts[2 * column : 2 * column + 2]]
            joined.append(jnp.stack(pair, axis=1))
        return jnp.concatenate(joined, axis=3).reshape(8 * rows, -1)

    states = []
    for index, mine in enumerate(sequences(held, lambda v: v.reshape(-1, 3, pairs, HEAD))):
        column, s = index // 2, index % 2
        count = splits[column][1] - splits[column][0]
        blocks = jnp.stack(
            [
                lax.dynamic_index_in_dim(block_order[column], b ^ (far * 2 + core), 0, keepdims=False)
                for core in range(2)
                for far in range(2)
            ]
        )
        places = (
            blocks[:, None] * count + jnp.arange(count, dtype=jnp.int32)[None, :]
        ).reshape(4 * count)
        allowed = allowed_of(places, lengths[s][0, column])
        queries, keys, values = mine[:, 0], mine[:, 1], mine[:, 2]
        attended, log_total = attention_forward(queries, keys, values, allowed)
        states.append((queries, keys, values, attended, log_total, allowed))
    attended_low = back([state[3].astype(BF16).reshape(-1, part) for state in states])

    def times(left, right):
        return lambda first, last: jnp.dot(
            left[first * rows : last * rows], right, preferred_element_type=F32
        )

    def times_transposed(left, right):
        return lambda first, last: contract_last(left[first * rows : last * rows], right)

    mixed = x + scatter_plane(times(attended_low, out_full), rows)
    second, second_pull = jax.vjp(layer_norm, mixed, norm_gains[1], norm_biases[1])
    second_all = gather_plane(second.astype(BF16))
    bias_part = lax.dynamic_slice_in_dim(
        hidden_bias.reshape(blk, lanes, 2, units), b, 1, 0
    )
    bias_part = lax.dynamic_index_in_dim(bias_part, y, 2, keepdims=False).reshape(-1)
    hidden_pre = jnp.dot(second_all, up_full, preferred_element_type=F32) + bias_part
    activated, gelu_pull = jax.vjp(lambda v: jax.nn.gelu(v, approximate=True), hidden_pre)
    activated_low = activated.astype(BF16)

    down_sum = scatter_z(contract_first(activated_low, cot_all).astype(BF16), 0)
    (grad_hidden,) = gelu_pull(contract_last(cot_all, down_full))
    grad_hidden_low = grad_hidden.astype(BF16)
    hidden_sum = jnp.sum(grad_hidden_low.astype(F32), axis=0)
    grad_second = scatter_plane(times_transposed(grad_hidden_low, up_full), rows)
    up_sum = contract_first(second_all, grad_hidden_low).astype(BF16)
    up_sum = scatter_z(up_sum.reshape(blk, -1, lanes * units), 1)
    grad_mixed_norm, gain_two, bias_two = second_pull(grad_second)
    grad_mixed = cot_low.astype(F32) + grad_mixed_norm
    mixed_all = gather_plane(grad_mixed.astype(BF16))
    result = mixed + scatter_plane(times(after(activated_low, mixed_all), down_full), rows)
    grad_attended = contract_last(mixed_all, out_full).astype(BF16)
    out_sum = contract_first(attended_low, mixed_all).astype(BF16)
    grad_parts = []
    grad_views = sequences(
        grad_attended.reshape(2, 2, 2, rows, pairs, HEAD), lambda v: v.reshape(-1, pairs, HEAD)
    )
    for grad_view, (queries, keys, values, attended, log_total, allowed) in zip(grad_views, states):
        grads = attention_backward(
            queries, keys, values, attended, grad_view, log_total, allowed
        )
        grad_parts.append(
            jnp.concatenate([g.astype(BF16).reshape(-1, part) for g in grads], axis=1)
        )
    grad_projected = back(grad_parts)
    qkv_sum = contract_first(normed_all, grad_projected).astype(BF16)
    qkv_sum = scatter_z(qkv_sum.reshape(blk, -1, 3 * part), 1)
    out_sum = scatter_z(out_sum, 0)
    grad_normed = scatter_plane(times_transposed(grad_projected, qkv_full), rows)
    grad_input_norm, gain_one, bias_one = first_pull(grad_normed)
    grad_input = (grad_mixed + grad_input_norm).astype(BF16)

    def give_back(total):
        parts = total.reshape(blk, 2, shard, -1)
        return exchange(lambda to_y: lax.dynamic_index_in_dim(parts, to_y, 1, keepdims=False))

    grad_up = give_back(up_sum).reshape(blk, 2, shard, lanes, units).astype(F32)
    grad_up = grad_up.transpose(2, 0, 3, 1, 4).reshape(shard, -1)
    grad_qkv = give_back(qkv_sum).reshape(blk, 2, shard, 3, pairs, HEAD).astype(F32)
    grad_qkv = grad_qkv.transpose(2, 3, 0, 4, 1, 5).reshape(shard, -1)
    grad_out = lax.ppermute(out_sum, "dp", [(j, i) for i, j in route]).astype(F32)
    small = jnp.concatenate([gain_one, gain_two, bias_one, bias_two, hidden_sum])
    small = sum_over(small, "dp", 2)
    norms = small[: 4 * width].reshape(4, width)
    norms = sum_over(norms + flip_y(norms), "blk", 1)
    norms = lax.dynamic_slice_in_dim(norms, (b * dp + d) * shard, shard, 1)
    grad_hidden_bias = lax.dynamic_slice_in_dim(small, 4 * width + z * units, units)
    return (
        result.astype(BF16).reshape(1, 1, rows, width),
        grad_input.reshape(1, 1, rows, width),
        grad_qkv,
        grad_out,
        grad_up,
        down_sum.astype(F32),
        norms[:2],
        norms[2:],
        grad_hidden_bias,
    )


def solution(mesh):
    return jax.shard_map(
        body,
        mesh=mesh,
        in_specs=(
            P("dp", "blk", None, None),
            P("dp", "blk", None, None),
            P("dp", None),
            P(),
            P(("blk", "dp"), None),
            P(("blk", "dp"), None),
            P(("blk", "dp"), None),
            P(("blk", "dp"), None),
            P(),
            P(),
            P(),
        ),
        out_specs=(
            P("dp", "blk", None, None),
            P("dp", "blk", None, None),
            P(("blk", "dp"), None),
            P(("blk", "dp"), None),
            P(("blk", "dp"), None),
            P(("blk", "dp"), None),
            P(None, ("blk", "dp")),
            P(None, ("blk", "dp")),
            P(("blk", "dp")),
        ),
        check_vma=False,
    )
```

```python
import jax
import jax.numpy as jnp
from jax import lax
from jax.experimental import pallas as pl
from jax.experimental.pallas import tpu as pltpu
from jax.sharding import PartitionSpec as P

HEAD = 128
BLK_A = 256
BLK_B = 64
SPLITS = ((0, BLK_A), (BLK_A, BLK_A + BLK_B))

EPSILON = 1e-05
NEGATIVE = -1e30
SCALE = HEAD ** (-0.5)
BF16 = jnp.bfloat16
F32 = jnp.float32


def after(value, *others):
    return lax.optimization_barrier((value, others))[0]


def layer_norm(value, gain, bias):
    center = value - jnp.mean(value, axis=-1, keepdims=True)
    spread = jnp.mean(center * center, axis=-1, keepdims=True)
    return center * lax.rsqrt(spread + EPSILON) * gain + bias


def contract_last(left, right):
    return lax.dot_general(
        left, right, (((1,), (1,)), ((), ())), preferred_element_type=F32
    )


def contract_first(left, right):
    return lax.dot_general(
        left, right, (((0,), (0,)), ((), ())), preferred_element_type=F32
    )


def flip(axis, bits, block):
    count = lax.axis_size(axis)
    return lax.ppermute(block, axis, [(i ^ bits, i) for i in range(count)])


def flip_core(block):
    return flip("blk", 1, block)


def flip_x(block):
    return flip("blk", 2, block)


def flip_y(block):
    return flip("dp", 1, block)


def lines():
    count = lax.axis_size("dp")
    return [[z * 2 + y for z in range(count // 2)] for y in range(2)]


def gather_z(part, axis):
    return lax.all_gather(part, "dp", axis_index_groups=lines(), axis=axis, tiled=True)


def scatter_z(total, axis):
    return lax.psum_scatter(
        total, "dp", axis_index_groups=lines(), scatter_dimension=axis, tiled=True
    )


def by_y(own, other):
    y = lax.axis_index("dp") % 2
    return jnp.where(y == 0, own, other), jnp.where(y == 0, other, own)


def exchange(cut):
    y = lax.axis_index("dp") % 2
    other = flip_y(cut(1 - y))
    both = jnp.stack(by_y(cut(y), other), axis=1)
    return lax.all_to_all(both, "blk", 0, 0)


def gather_plane(part):
    half = part.shape[0] // 2
    from_x, from_y, from_core = flip_x(part), flip_y(part), flip_core(part)
    diagonal = jnp.concatenate([flip_y(from_x[:half]), flip_x(from_y[half:])], axis=0)
    mine = [part, from_x, from_y, diagonal]
    return jnp.concatenate(
        mine + [from_core] + [flip_core(piece) for piece in mine[1:]], axis=0
    )


def scatter_plane(product, rows):
    half = rows // 2
    got = flip_core(product(4, 8).astype(BF16))
    held = product(0, 4).astype(F32) + got.astype(F32)
    own, to_x, to_y, across = [held[i * rows : (i + 1) * rows] for i in range(4)]
    across = across.astype(BF16)
    x_across, y_across = flip_x(across[:half]), flip_y(across[half:])
    x_top = flip_x(to_x[:half].astype(BF16))
    y_bottom = flip_y(to_y[half:].astype(BF16))
    sent = [
        (to_y[:half] + x_across.astype(F32)).astype(BF16),
        (to_x[half:] + y_across.astype(F32)).astype(BF16),
    ]
    y_top = flip_y(sent[0])
    x_bottom = flip_x(sent[1])
    top = own[:half] + x_top.astype(F32) + y_top.astype(F32)
    bottom = own[half:] + x_bottom.astype(F32) + y_bottom.astype(F32)
    return jnp.concatenate([top, bottom], axis=0), sent


def sum_over(total, axis, bits):
    while bits < lax.axis_size(axis):
        total = total + flip(axis, bits, total)
        bits *= 2
    return total


def part_of(slots_ref, column, block):
    slot = slots_ref[column, block]
    first, last = SPLITS[column]
    return slot // 2, 0, slot % 2, slice(first, last)


def scores_of(queries, keys, first, length):
    scores = contract_last(queries, keys) * SCALE
    key_places = lax.broadcasted_iota(jnp.int32, scores.shape, 1)
    query_places = first + lax.broadcasted_iota(jnp.int32, scores.shape, 0)
    allowed = (key_places <= query_places) & (key_places < length)
    return jnp.where(allowed, scores, NEGATIVE)


def attention_steps():
    for column, (first, last) in enumerate(SPLITS):
        size = last - first
        step = 1 if size * 4 > 512 else 4
        yield column, size, [(p, step, (p + step) * size) for p in range(0, 4, step)]


def attention_forward_kernel(slots_ref, lengths_ref, in_ref, out_ref, log_ref, q_ref, k_ref, v_ref):
    sequence = pl.program_id(0)
    heads = in_ref.shape[-1] // (3 * HEAD)
    for column, size, runs in attention_steps():
        length = lengths_ref[sequence, column]
        for head in range(heads):
            for third, ref in enumerate((q_ref, k_ref, v_ref)):
                lanes = slice((third * heads + head) * HEAD, (third * heads + head + 1) * HEAD)
                for block in range(4):
                    ref[block * size : (block + 1) * size] = in_ref[
                        (*part_of(slots_ref, column, block), lanes)
                    ]
            lanes = slice(head * HEAD, (head + 1) * HEAD)
            for start, step, keys in runs:
                rows = slice(start * size, (start + step) * size)
                scores = scores_of(q_ref[rows], k_ref[:keys], start * size, length)
                peak = jnp.max(scores, axis=-1, keepdims=True)
                weights = jnp.exp(scores - peak)
                total = jnp.sum(weights, axis=-1, keepdims=True)
                attended = jnp.dot(weights.astype(BF16), v_ref[:keys], preferred_element_type=F32)
                attended = (attended / total).astype(BF16)
                log_total = jnp.broadcast_to(peak + jnp.log(total), (step * size, HEAD))
                for i in range(step):
                    where = part_of(slots_ref, column, start + i)
                    out_ref[(*where, lanes)] = attended[i * size : (i + 1) * size]
                    log_ref[(*where, lanes)] = log_total[i * size : (i + 1) * size]


def attention_backward_kernel(
    slots_ref, lengths_ref, in_ref, grad_ref, log_ref, out_ref, q_ref, k_ref, v_ref, g_ref, dk_ref, dv_ref
):
    sequence = pl.program_id(0)
    heads = in_ref.shape[-1] // (3 * HEAD)
    for column, size, runs in attention_steps():
        length = lengths_ref[sequence, column]
        for head in range(heads):
            columns = [
                slice((third * heads + head) * HEAD, (third * heads + head + 1) * HEAD)
                for third in range(3)
            ]
            lanes = slice(head * HEAD, (head + 1) * HEAD)
            for block in range(4):
                here = slice(block * size, (block + 1) * size)
                where = part_of(slots_ref, column, block)
                q_ref[here] = in_ref[(*where, columns[0])]
                k_ref[here] = in_ref[(*where, columns[1])]
                v_ref[here] = in_ref[(*where, columns[2])]
                g_ref[here] = grad_ref[(*where, lanes)]
            dk_ref[...] = jnp.zeros_like(dk_ref)
            dv_ref[...] = jnp.zeros_like(dv_ref)
            for start, step, keys in runs:
                rows = slice(start * size, (start + step) * size)
                queries, grads = q_ref[rows], g_ref[rows]
                log_total = jnp.concatenate(
                    [
                        log_ref[(*part_of(slots_ref, column, start + i), lanes)][:, :1]
                        for i in range(step)
                    ],
                    axis=0,
                )
                scores = scores_of(queries, k_ref[:keys], start * size, length)
                probs = jnp.exp(scores - log_total)
                grad_probs = contract_last(grads, v_ref[:keys])
                delta = jnp.sum(probs * grad_probs, axis=-1, keepdims=True)
                grad_scores = (probs * (grad_probs - delta)).astype(BF16)
                dv_ref[:keys] += contract_first(probs.astype(BF16), grads)
                dk_ref[:keys] += contract_first(grad_scores, queries)
                dq = jnp.dot(grad_scores, k_ref[:keys], preferred_element_type=F32) * SCALE
                dq = dq.astype(BF16)
                for i in range(step):
                    where = part_of(slots_ref, column, start + i)
                    out_ref[(*where, columns[0])] = dq[i * size : (i + 1) * size]
            for block in range(4):
                here = slice(block * size, (block + 1) * size)
                where = part_of(slots_ref, column, block)
                out_ref[(*where, columns[1])] = (dk_ref[here] * SCALE).astype(BF16)
                out_ref[(*where, columns[2])] = dv_ref[here].astype(BF16)


def attention_call(kernel, arrays, outs, scratch, slots, lengths, matmuls):
    count = 4 * BLK_A
    rows = arrays[0].shape[0] // 8

    def spec(columns):
        return pl.BlockSpec((2, 1, 2, rows, columns), lambda s, *_: (0, s, 0, 0, 0))

    heads = arrays[0].shape[1] // (3 * HEAD)
    results = pl.pallas_call(
        kernel,
        grid_spec=pltpu.PrefetchScalarGridSpec(
            num_scalar_prefetch=2,
            grid=(2,),
            in_specs=[spec(a.shape[1]) for a in arrays],
            out_specs=[spec(columns) for columns, _ in outs],
            scratch_shapes=[pltpu.VMEM((count, HEAD), dtype) for dtype in scratch],
        ),
        out_shape=[jax.ShapeDtypeStruct((2, 2, 2, rows, c), dtype) for c, dtype in outs],
        compiler_params=pltpu.CompilerParams(vmem_limit_bytes=48 * 2**20),
        cost_estimate=pl.CostEstimate(
            flops=matmuls * 2 * heads * count * count * HEAD * 2,
            bytes_accessed=8 * rows * HEAD * heads * 2 * 4,
            transcendentals=2 * heads * count * count,
        ),
    )(slots, lengths, *[a.reshape(2, 2, 2, rows, -1) for a in arrays])
    return [r.reshape(8 * rows, -1) for r in results]


def body(
    hidden_in,
    cotangent,
    seq_lengths,
    block_order,
    w_qkv,
    w_out,
    w_up,
    w_down,
    norm_gains,
    norm_biases,
    hidden_bias,
):
    blk, dp = lax.axis_size("blk"), lax.axis_size("dp")
    lanes = dp // 2
    b, d = lax.axis_index("blk"), lax.axis_index("dp")
    z, y = d // 2, d % 2
    rows, width = hidden_in.shape[2:]
    pairs = width // HEAD // blk // 2
    part = pairs * HEAD
    shard = w_qkv.shape[0]
    units = w_down.shape[0]
    x = hidden_in.reshape(rows, width).astype(F32)
    cot_low = cotangent.reshape(rows, width)

    def cut_qkv(to_y):
        view = w_qkv.reshape(shard, 3, blk, pairs, 2, HEAD)
        view = lax.dynamic_index_in_dim(view, to_y, 4, keepdims=False)
        return view.transpose(2, 0, 1, 3, 4).reshape(blk, shard, 3 * part)

    def cut_up(to_y):
        view = late_up.reshape(shard, blk, lanes, 2, units)
        view = lax.dynamic_index_in_dim(view, to_y, 3, keepdims=False)
        return view.transpose(1, 0, 2, 3).reshape(blk, shard, lanes * units)

    pieces = [[p for p in range(dp) if (p * shard // HEAD) % 2 == to_y] for to_y in range(2)]
    route = [(pieces[to_y][lane], lane * 2 + to_y) for to_y in range(2) for lane in range(lanes)]

    holders = jnp.stack(
        [jnp.take(block_order, b ^ (far * 2 + core), axis=1) for core in range(2) for far in range(2)],
        axis=1,
    )
    found = holders[:, None, :] == jnp.arange(4, dtype=jnp.int32)[None, :, None]
    slots = jnp.sum(jnp.where(found, jnp.arange(4, dtype=jnp.int32), 0), axis=2)
    lengths = jnp.concatenate([seq_lengths, flip_y(seq_lengths)], axis=0)

    out_full = gather_z(lax.ppermute(w_out, "dp", route), 0)
    qkv_part = exchange(cut_qkv).reshape(blk, 2 * shard, 3 * part)
    qkv_full = gather_z(after(qkv_part, out_full), 1).reshape(width, 3 * part)

    normed, first_pull = jax.vjp(layer_norm, x, norm_gains[0], norm_biases[0])
    normed_all = gather_plane(after(normed.astype(BF16), qkv_part))
    late_up = after(w_up, normed_all)
    up_part = exchange(cut_up).reshape(blk, 2 * shard, lanes * units)
    up_full = gather_z(up_part, 1).reshape(width, lanes * units)
    down_full = gather_z(after(w_down, up_part), 0)
    cot_all = gather_plane(after(cot_low, up_part))
    projected = jnp.dot(normed_all, qkv_full, preferred_element_type=F32).astype(BF16)
    attended_low, log_total = attention_call(
        attention_forward_kernel,
        [projected],
        [(part, BF16), (part, F32)],
        [BF16] * 3,
        slots,
        lengths,
        2,
    )

    def times(left, right):
        return lambda first, last: jnp.dot(
            left[first * rows : last * rows], right, preferred_element_type=F32
        )

    def times_transposed(left, right):
        return lambda first, last: contract_last(left[first * rows : last * rows], right)

    mixed = x + scatter_plane(times(attended_low, out_full), rows)[0]
    second, second_pull = jax.vjp(layer_norm, mixed, norm_gains[1], norm_biases[1])
    second_all = gather_plane(second.astype(BF16))
    bias_part = lax.dynamic_slice_in_dim(
        hidden_bias.reshape(blk, lanes, 2, units), b, 1, 0
    )
    bias_part = lax.dynamic_index_in_dim(bias_part, y, 2, keepdims=False).reshape(-1)
    hidden_pre = jnp.dot(second_all, up_full, preferred_element_type=F32) + bias_part
    activated, gelu_pull = jax.vjp(lambda v: jax.nn.gelu(v, approximate=True), hidden_pre)
    activated_low = activated.astype(BF16)

    down_sum = contract_first(activated_low, cot_all).astype(BF16)
    down_full = after(down_full, down_sum)
    down_sum = scatter_z(down_sum, 0)
    (grad_hidden,) = gelu_pull(contract_last(cot_all, down_full))
    grad_hidden_low = grad_hidden.astype(BF16)
    hidden_sum = jnp.sum(grad_hidden_low.astype(F32), axis=0)
    grad_second, sent = scatter_plane(times_transposed(grad_hidden_low, up_full), rows)
    up_sum = contract_first(second_all, after(grad_hidden_low, *sent)).astype(BF16)
    up_sum = scatter_z(up_sum.reshape(blk, -1, lanes * units), 1)
    grad_mixed_norm, gain_two, bias_two = second_pull(grad_second)
    grad_mixed = cot_low.astype(F32) + grad_mixed_norm
    mixed_low = grad_mixed.astype(BF16)
    mixed_all = gather_plane(mixed_low)
    product = jnp.dot(
        after(activated_low, mixed_low), down_full, preferred_element_type=F32
    ).astype(BF16)
    product = after(product, mixed_all)
    result = mixed + scatter_plane(lambda first, last: product[first * rows : last * rows], rows)[0]
    grad_attended = contract_last(mixed_all, out_full).astype(BF16)
    (grad_projected,) = attention_call(
        attention_backward_kernel,
        [projected, grad_attended, log_total],
        [(3 * part, BF16)],
        [BF16] * 4 + [F32] * 2,
        slots,
        lengths,
        5,
    )
    qkv_sum = contract_first(normed_all, grad_projected).astype(BF16)
    grad_projected = after(grad_projected, qkv_sum)
    qkv_sum = scatter_z(qkv_sum.reshape(blk, -1, 3 * part), 1)
    grad_normed, sent = scatter_plane(times_transposed(grad_projected, qkv_full), rows)
    out_sum = contract_first(after(attended_low, *sent), mixed_all).astype(BF16)
    out_sum = scatter_z(after(out_sum, qkv_sum), 0)
    grad_input_norm, gain_one, bias_one = first_pull(grad_normed)
    grad_input = (grad_mixed + grad_input_norm).astype(BF16)

    def give_back(total):
        parts = total.reshape(blk, 2, shard, -1)
        return exchange(lambda to_y: lax.dynamic_index_in_dim(parts, to_y, 1, keepdims=False))

    grad_up = give_back(up_sum).reshape(blk, 2, shard, lanes, units).astype(F32)
    grad_up = grad_up.transpose(2, 0, 3, 1, 4).reshape(shard, -1)
    grad_qkv = give_back(qkv_sum).reshape(blk, 2, shard, 3, pairs, HEAD).astype(F32)
    grad_qkv = grad_qkv.transpose(2, 3, 0, 4, 1, 5).reshape(shard, -1)
    grad_out = lax.ppermute(out_sum, "dp", [(j, i) for i, j in route]).astype(F32)
    small = jnp.concatenate([gain_one, gain_two, bias_one, bias_two, hidden_sum])
    small = sum_over(small, "dp", 2)
    norms = small[: 4 * width].reshape(4, width)
    norms = sum_over(norms + flip_y(norms), "blk", 1)
    norms = lax.dynamic_slice_in_dim(norms, (b * dp + d) * shard, shard, 1)
    grad_hidden_bias = lax.dynamic_slice_in_dim(small, 4 * width + z * units, units)
    return (
        result.astype(BF16).reshape(1, 1, rows, width),
        grad_input.reshape(1, 1, rows, width),
        grad_qkv,
        grad_out,
        grad_up,
        down_sum.astype(F32),
        norms[:2],
        norms[2:],
        grad_hidden_bias,
    )


def solution(mesh):
    return jax.shard_map(
        body,
        mesh=mesh,
        in_specs=(
            P("dp", "blk", None, None),
            P("dp", "blk", None, None),
            P("dp", None),
            P(),
            P(("blk", "dp"), None),
            P(("blk", "dp"), None),
            P(("blk", "dp"), None),
            P(("blk", "dp"), None),
            P(),
            P(),
            P(),
        ),
        out_specs=(
            P("dp", "blk", None, None),
            P("dp", "blk", None, None),
            P(("blk", "dp"), None),
            P(("blk", "dp"), None),
            P(("blk", "dp"), None),
            P(("blk", "dp"), None),
            P(None, ("blk", "dp")),
            P(None, ("blk", "dp")),
            P(("blk", "dp")),
        ),
        check_vma=False,
    )
```

```python
import jax
import jax.numpy as jnp
from jax import lax
from jax.experimental import pallas as pl
from jax.experimental.pallas import tpu as pltpu
from jax.sharding import PartitionSpec as P

HEAD = 128
BLK_A = 256
BLK_B = 64
SPLITS = ((0, BLK_A), (BLK_A, BLK_A + BLK_B))
BLOCK_HALF = (BLK_A + BLK_B) // 2

EPSILON = 1e-05
NEGATIVE = -1e30
SCALE = HEAD ** (-0.5)
BF16 = jnp.bfloat16
F32 = jnp.float32


def after(value, *others):
    return lax.optimization_barrier((value, others))[0]


def layer_norm(value, gain, bias):
    center = value - jnp.mean(value, axis=-1, keepdims=True)
    spread = jnp.mean(center * center, axis=-1, keepdims=True)
    return center * lax.rsqrt(spread + EPSILON) * gain + bias


def gelu(v):
    rate = (2.0 / 3.141592653589793) ** 0.5
    squared = v * v
    bend = jnp.tanh(rate * v * (1.0 + 0.044715 * squared))
    rise = 0.5 * (1.0 + bend)
    slope = rise + 0.5 * v * (1.0 - bend * bend) * rate * (1.0 + 3 * 0.044715 * squared)
    return v * rise, slope


def contract_last(left, right):
    return lax.dot_general(
        left, right, (((1,), (1,)), ((), ())), preferred_element_type=F32
    )


def contract_first(left, right):
    return lax.dot_general(
        left, right, (((0,), (0,)), ((), ())), preferred_element_type=F32
    )


def flip(axis, bits, block):
    count = lax.axis_size(axis)
    return lax.ppermute(block, axis, [(i ^ bits, i) for i in range(count)])


def flip_core(block):
    return flip("blk", 1, block)


def flip_x(block):
    return flip("blk", 2, block)


def flip_y(block):
    return flip("dp", 1, block)


def lines():
    count = lax.axis_size("dp")
    return [[z * 2 + y for z in range(count // 2)] for y in range(2)]


def gather_z(part, axis):
    return lax.all_gather(part, "dp", axis_index_groups=lines(), axis=axis, tiled=True)


def scatter_z(total, axis):
    return lax.psum_scatter(
        total, "dp", axis_index_groups=lines(), scatter_dimension=axis, tiled=True
    )


def column(groups, blk, runs, width, group, b, run, y):
    return (((group * blk + b) * runs + run) * 2 + y) * width


def split_columns(shard, groups, blk, runs, width):
    rows = shard.shape[0]
    count = groups * runs * width

    def kernel(y_ref, in_ref, out_ref):
        b = pl.program_id(1)
        y = jnp.where(pl.program_id(0) == 0, 1 - y_ref[0], y_ref[0])
        for group in range(groups):
            for run in range(runs):
                start = column(groups, blk, runs, width, group, b, run, y)
                to = (group * runs + run) * width
                out_ref[0, 0, :, to : to + width] = in_ref[:, pl.ds(pl.multiple_of(start, 128), width)]

    return pl.pallas_call(
        kernel,
        grid_spec=pltpu.PrefetchScalarGridSpec(
            num_scalar_prefetch=1,
            grid=(2, blk),
            in_specs=[pl.BlockSpec(shard.shape, lambda i, j, *_: (0, 0))],
            out_specs=pl.BlockSpec((1, 1, rows, count), lambda i, j, *_: (i, j, 0, 0)),
        ),
        out_shape=jax.ShapeDtypeStruct((2, blk, rows, count), shard.dtype),
        compiler_params=pltpu.CompilerParams(vmem_limit_bytes=16 * 2**20),
        cost_estimate=pl.CostEstimate(flops=0, bytes_accessed=4 * shard.size, transcendentals=0),
    )((lax.axis_index("dp") % 2).reshape(1), shard)


def join_y(own, other):
    blk, rows, count = own.shape

    def kernel(y_ref, own_ref, other_ref, out_ref):
        out_ref[0, y_ref[0]] = own_ref[0]
        out_ref[0, 1 - y_ref[0]] = other_ref[0]

    piece = pl.BlockSpec((1, rows, count), lambda i, *_: (i, 0, 0))
    return pl.pallas_call(
        kernel,
        grid_spec=pltpu.PrefetchScalarGridSpec(
            num_scalar_prefetch=1,
            grid=(blk,),
            in_specs=[piece, piece],
            out_specs=pl.BlockSpec((1, 2, rows, count), lambda i, *_: (i, 0, 0, 0)),
        ),
        out_shape=jax.ShapeDtypeStruct((blk, 2, rows, count), own.dtype),
        compiler_params=pltpu.CompilerParams(vmem_limit_bytes=16 * 2**20),
        cost_estimate=pl.CostEstimate(flops=0, bytes_accessed=8 * own.size, transcendentals=0),
    )((lax.axis_index("dp") % 2).reshape(1), own, other)


def merge_columns(parts, groups, blk, runs, width):
    _, _, rows, count = parts.shape

    def kernel(in_ref, out_ref):
        b = pl.program_id(0)
        for y in range(2):
            for group in range(groups):
                for run in range(runs):
                    start = column(groups, blk, runs, width, group, b, run, y)
                    at = (group * runs + run) * width
                    out_ref[:, pl.ds(pl.multiple_of(start, 128), width)] = in_ref[
                        0, y, :, at : at + width
                    ].astype(F32)

    return pl.pallas_call(
        kernel,
        grid=(blk,),
        in_specs=[pl.BlockSpec((1, 2, rows, count), lambda i: (i, 0, 0, 0))],
        out_specs=pl.BlockSpec((rows, blk * 2 * count), lambda i: (0, 0)),
        out_shape=jax.ShapeDtypeStruct((rows, blk * 2 * count), F32),
        compiler_params=pltpu.CompilerParams(vmem_limit_bytes=16 * 2**20),
        cost_estimate=pl.CostEstimate(flops=0, bytes_accessed=6 * parts.size, transcendentals=0),
    )(parts)


def exchange(own, other):
    return lax.all_to_all(join_y(own, other), "blk", 0, 0)


TOPS = ((0, 5), (3, 4))
BOTTOMS = ((1, 2), (7, 6))


def gather_first(part, y_others=(), x_others=()):
    return part, flip_x(after(part, x_others)), flip_y(after(part, y_others)), flip_core(after(part, x_others))


def gather_second(part, from_x, from_y, from_core):
    half = part.shape[0] // 2
    diagonal = [flip_y(from_x[:half]), flip_x(from_y[half:])]
    return [part, from_x, from_y], diagonal, [from_core, flip_core(from_x), flip_core(from_y)]


def gather_third(mine, diagonal, others):
    most = assemble([*mine, *others], [(0, 0, 2, 0), (1, 0, 1, 5), (1, 1, 1, 2), (2, 0, 1, 3), (2, 1, 1, 7)])
    diagonal = after(diagonal, most)
    both = [*diagonal, *[flip_core(piece) for piece in diagonal]]
    return assemble(both, [(0, 0, 1, 4), (1, 0, 1, 6)], most)


def assemble(pieces, runs, whole=None):
    half = BLOCK_HALF
    columns = pieces[0].shape[1]
    side_pieces = len(pieces) // 2
    copies, total = [], 0
    for side in range(2):
        for piece, start, count, to in runs:
            copies.append(
                (side * side_pieces + piece, start * half, count * half, (side * 8 + to) * half, total)
            )
            total += count * half

    def kernel(*refs):
        out_ref, held_ref, in_sems, out_sems = refs[-4:]
        reads, writes = [], []
        for i, (piece, start, count, to, at) in enumerate(copies):
            there = held_ref.at[pl.ds(at, count)]
            source = refs[piece].at[pl.ds(start, count)]
            reads.append(pltpu.make_async_copy(source, there, in_sems.at[i]))
            writes.append(pltpu.make_async_copy(there, out_ref.at[pl.ds(to, count)], out_sems.at[i]))
        for read in reads:
            read.start()
        for read, write in zip(reads, writes):
            read.wait()
            write.start()
        for write in writes:
            write.wait()

    inputs = [*pieces] if whole is None else [*pieces, whole]
    return pl.pallas_call(
        kernel,
        in_specs=[pl.BlockSpec(memory_space=pl.ANY)] * len(inputs),
        out_specs=pl.BlockSpec(memory_space=pltpu.HBM),
        out_shape=jax.ShapeDtypeStruct((16 * half, columns), pieces[0].dtype),
        input_output_aliases={} if whole is None else {len(inputs) - 1: 0},
        scratch_shapes=[pltpu.VMEM((total, columns), pieces[0].dtype)]
        + [pltpu.SemaphoreType.DMA((len(copies),))] * 2,
        compiler_params=pltpu.CompilerParams(vmem_limit_bytes=56 * 2**20),
        cost_estimate=pl.CostEstimate(flops=0, bytes_accessed=4 * total * columns, transcendentals=0),
    )(*inputs)


def scatter_core(product):
    far, near = product(12, 16).astype(BF16), product(8, 12).astype(BF16)
    return scatter_pair(product, flip_core(far), flip_core(near))


def scatter_pair(product, far, near):
    middle = far.shape[0] // 2
    to_x = (product(4, 6).astype(F32) + far[:middle].astype(F32)).astype(BF16)
    to_y = (product(6, 8).astype(F32) + far[middle:].astype(F32)).astype(BF16)
    return (to_x, to_y), (product(0, 4, to_x, to_y), near)


def scatter_first(held, *others):
    to_x, to_y = held[0]
    return flip_x(after(to_x, *others)), flip_y(after(to_y, *others))


def scatter_second(held, from_x, from_y):
    half = from_x.shape[0] // 2
    product, got = held[1]
    to_x = product[2 * half : 3 * half].astype(F32) + got[2 * half : 3 * half].astype(F32)
    to_y = product[3 * half :].astype(F32) + got[3 * half :].astype(F32)
    to_x = (to_x + from_y[:half].astype(F32)).astype(BF16)
    to_y = (to_y + from_x[:half].astype(F32)).astype(BF16)
    return to_x, to_y


def scatter_third(held, from_x, from_y, to_x, to_y):
    half = from_x.shape[0] // 2
    product, got = held[1]
    own = product[: 2 * half].astype(F32) + got[: 2 * half].astype(F32)
    top = from_x[half:].astype(F32) + flip_y(to_y).astype(F32)
    bottom = from_y[half:].astype(F32) + flip_x(to_x).astype(F32)
    return own + jnp.concatenate([top, bottom], axis=0)


def sum_small(norms, hidden):
    blk, dp = lax.axis_size("blk"), lax.axis_size("dp")
    count = norms.shape[0]
    parts = norms.reshape(count, blk, -1).transpose(1, 0, 2)
    parts = jnp.sum(lax.all_to_all(parts, "blk", 0, 0), axis=0)
    parts = parts.reshape(count, dp, -1).transpose(1, 0, 2)
    share = parts.shape[2]
    hidden = jnp.repeat(hidden.reshape(dp // 2, -1), 2, axis=0)
    both = jnp.concatenate([parts.reshape(dp, -1), hidden], axis=1)
    both = lax.all_to_all(both, "dp", 0, 0)
    mine = jnp.arange(dp) % 2 == lax.axis_index("dp") % 2
    return (
        jnp.sum(both[:, : count * share], axis=0).reshape(count, share),
        jnp.sum(jnp.where(mine[:, None], both[:, count * share :], 0.0), axis=0),
    )


def runs_of(places_ref, sequence, column, block, half):
    first, last = SPLITS[column]
    if first < half:
        top = min(last, half)
        yield places_ref[sequence, column, block], slice(first, top), slice(0, top - first)
    if last > half:
        start = max(first, half)
        yield (
            places_ref[sequence, column, 4 + block],
            slice(start - half, last - half),
            slice(start - first, last - first),
        )


def load_block(places_ref, sequence, column, block, ref, lanes, to_ref, row):
    for which, here, there in runs_of(places_ref, sequence, column, block, ref.shape[1]):
        to_ref[row + there.start : row + there.stop] = ref[which, here, lanes]


def store_block(places_ref, sequence, column, block, ref, lanes, value):
    for which, here, there in runs_of(places_ref, sequence, column, block, ref.shape[1]):
        ref[which, here, lanes] = value[there]


def scores_of(queries, keys, first, length):
    scores = contract_last(queries, keys) * SCALE
    key_places = lax.broadcasted_iota(jnp.int32, scores.shape, 1)
    query_places = first + lax.broadcasted_iota(jnp.int32, scores.shape, 0)
    allowed = (key_places <= query_places) & (key_places < length)
    return jnp.where(allowed, scores, NEGATIVE)


def attention_steps():
    for column, (first, last) in enumerate(SPLITS):
        size = last - first
        step = 1 if size * 4 > 512 else 4
        yield column, size, [(p, step, (p + step) * size) for p in range(0, 4, step)]


def attention_forward_kernel(places_ref, lengths_ref, in_ref, out_ref, log_ref, q_ref, k_ref, v_ref):
    sequence = pl.program_id(0)
    heads = in_ref.shape[-1] // (3 * HEAD)
    for column, size, runs in attention_steps():
        length = lengths_ref[sequence, column]
        for head in range(heads):
            for third, ref in enumerate((q_ref, k_ref, v_ref)):
                lanes = slice((third * heads + head) * HEAD, (third * heads + head + 1) * HEAD)
                for block in range(4):
                    load_block(places_ref, sequence, column, block, in_ref, lanes, ref, block * size)
            lanes = slice(head * HEAD, (head + 1) * HEAD)
            for start, step, keys in runs:
                rows = slice(start * size, (start + step) * size)
                scores = scores_of(q_ref[rows], k_ref[:keys], start * size, length)
                peak = jnp.max(scores, axis=-1, keepdims=True)
                weights = jnp.exp(scores - peak)
                total = jnp.sum(weights, axis=-1, keepdims=True)
                attended = jnp.dot(weights.astype(BF16), v_ref[:keys], preferred_element_type=F32)
                attended = (attended / total).astype(BF16)
                log_total = jnp.broadcast_to(peak + jnp.log(total), (step * size, HEAD))
                for i in range(step):
                    here = slice(i * size, (i + 1) * size)
                    at = (places_ref, sequence, column, start + i)
                    store_block(*at, out_ref, lanes, attended[here])
                    store_block(*at, log_ref, lanes, log_total[here])


def attention_backward_kernel(
    places_ref,
    lengths_ref,
    in_ref,
    grad_ref,
    log_ref,
    out_ref,
    q_ref,
    k_ref,
    v_ref,
    g_ref,
    log_rows_ref,
    dk_ref,
    dv_ref,
):
    sequence = pl.program_id(0)
    heads = in_ref.shape[-1] // (3 * HEAD)
    for column, size, runs in attention_steps():
        length = lengths_ref[sequence, column]
        for head in range(heads):
            columns = [
                slice((third * heads + head) * HEAD, (third * heads + head + 1) * HEAD)
                for third in range(3)
            ]
            lanes = slice(head * HEAD, (head + 1) * HEAD)
            for block in range(4):
                at = (places_ref, sequence, column, block)
                load_block(*at, in_ref, columns[0], q_ref, block * size)
                load_block(*at, in_ref, columns[1], k_ref, block * size)
                load_block(*at, in_ref, columns[2], v_ref, block * size)
                load_block(*at, grad_ref, lanes, g_ref, block * size)
                load_block(*at, log_ref, lanes, log_rows_ref, block * size)
            dk_ref[...] = jnp.zeros_like(dk_ref)
            dv_ref[...] = jnp.zeros_like(dv_ref)
            for start, step, keys in runs:
                rows = slice(start * size, (start + step) * size)
                queries, grads = q_ref[rows], g_ref[rows]
                scores = scores_of(queries, k_ref[:keys], start * size, length)
                probs = jnp.exp(scores - log_rows_ref[rows, :1])
                grad_probs = contract_last(grads, v_ref[:keys])
                delta = jnp.sum(probs * grad_probs, axis=-1, keepdims=True)
                grad_scores = (probs * (grad_probs - delta)).astype(BF16)
                dv_ref[:keys] += contract_first(probs.astype(BF16), grads)
                dk_ref[:keys] += contract_first(grad_scores, queries)
                dq = jnp.dot(grad_scores, k_ref[:keys], preferred_element_type=F32) * SCALE
                dq = dq.astype(BF16)
                for i in range(step):
                    at = (places_ref, sequence, column, start + i)
                    store_block(*at, out_ref, columns[0], dq[i * size : (i + 1) * size])
            for block in range(4):
                here = slice(block * size, (block + 1) * size)
                at = (places_ref, sequence, column, block)
                store_block(*at, out_ref, columns[1], (dk_ref[here] * SCALE).astype(BF16))
                store_block(*at, out_ref, columns[2], dv_ref[here].astype(BF16))


def attention_call(kernel, arrays, outs, scratch, places, lengths, matmuls):
    count = 4 * BLK_A
    half = arrays[0].shape[0] // 16

    def spec(columns):
        return pl.BlockSpec((16, half, columns), lambda s, *_: (0, 0, 0))

    heads = arrays[0].shape[1] // (3 * HEAD)
    results = pl.pallas_call(
        kernel,
        grid_spec=pltpu.PrefetchScalarGridSpec(
            num_scalar_prefetch=2,
            grid=(2,),
            in_specs=[spec(a.shape[1]) for a in arrays],
            out_specs=[spec(columns) for columns, _ in outs],
            scratch_shapes=[pltpu.VMEM((count, HEAD), dtype) for dtype in scratch],
        ),
        out_shape=[jax.ShapeDtypeStruct((16, half, c), dtype) for c, dtype in outs],
        compiler_params=pltpu.CompilerParams(vmem_limit_bytes=48 * 2**20),
        cost_estimate=pl.CostEstimate(
            flops=matmuls * 2 * heads * count * count * HEAD * 2,
            bytes_accessed=16 * half * HEAD * heads * 2 * 4,
            transcendentals=2 * heads * count * count,
        ),
    )(places, lengths, *[a.reshape(16, half, -1) for a in arrays])
    return [r.reshape(16 * half, -1) for r in results]


def body(
    hidden_in,
    cotangent,
    seq_lengths,
    block_order,
    w_qkv,
    w_out,
    w_up,
    w_down,
    norm_gains,
    norm_biases,
    hidden_bias,
):
    blk, dp = lax.axis_size("blk"), lax.axis_size("dp")
    lanes = dp // 2
    b, d = lax.axis_index("blk"), lax.axis_index("dp")
    z, y = d // 2, d % 2
    rows, width = hidden_in.shape[2:]
    pairs = width // HEAD // blk // 2
    part = pairs * HEAD
    half = rows // 2
    shard = w_qkv.shape[0]
    units = w_down.shape[0]
    x = hidden_in.reshape(rows, width).astype(F32)
    cot_low = cotangent.reshape(rows, width)

    qkv_cut = (3, blk, pairs, HEAD)
    up_cut = (1, blk, lanes, units)

    pieces = [[p for p in range(dp) if (p * shard // HEAD) % 2 == to_y] for to_y in range(2)]
    route = [(pieces[to_y][lane], lane * 2 + to_y) for to_y in range(2) for lane in range(lanes)]

    near = [(core, far) for core in range(2) for far in range(2)]
    holders = jnp.stack(
        [jnp.take(block_order, b ^ (far * 2 + core), axis=1) for core, far in near], axis=1
    )
    found = holders[:, None, :] == jnp.arange(4, dtype=jnp.int32)[None, :, None]
    tables = jnp.array(
        [[[core * 8 + t[s][far] for core, far in near] for t in (TOPS, BOTTOMS)] for s in range(2)],
        jnp.int32,
    )
    places = jnp.sum(jnp.where(found[None, :, None], tables[:, None, :, None], 0), axis=-1)
    places = places.reshape(2, 2, 8)

    out_full = gather_z(lax.ppermute(w_out, "dp", route), 0)
    normed, first_pull = jax.vjp(layer_norm, x, norm_gains[0], norm_biases[0])
    lengths = jnp.concatenate([seq_lengths, flip_y(seq_lengths)], axis=0)
    qkv_pair = split_columns(w_qkv, *qkv_cut)
    qkv_other = flip_y(after(qkv_pair[0], lengths))
    steps = gather_first(normed.astype(BF16))
    qkv_part = exchange(after(qkv_pair[1], steps), qkv_other).reshape(blk, 2 * shard, 3 * part)
    qkv_full = gather_z(after(qkv_part, out_full), 1).reshape(width, 3 * part)
    down_full = gather_z(after(w_down, qkv_part), 0)
    steps = gather_second(*after(steps, qkv_part))
    cot_low = after(cot_low, qkv_part)
    cot_steps = gather_second(*gather_first(cot_low))
    normed_all = gather_third(*steps)
    up_pair = split_columns(after(w_up, qkv_part), *up_cut)
    up_other = flip_y(after(up_pair[0], cot_steps[1]))
    up_part = exchange(up_pair[1], up_other).reshape(blk, 2 * shard, lanes * units)
    up_full = gather_z(after(up_part, qkv_full), 1).reshape(width, lanes * units)

    def split_sum(total):
        parts = total.reshape(blk, 2, shard, -1)
        other = flip_y(lax.dynamic_index_in_dim(parts, 1 - y, 1, keepdims=False))
        return lax.dynamic_index_in_dim(parts, y, 1, keepdims=False), other

    def times(left, right):
        return lambda first, last, *others: jnp.dot(
            after(left, *others)[first * half : last * half], right, preferred_element_type=F32
        )

    def times_transposed(left, right):
        return lambda first, last, *others: contract_last(
            after(left, *others)[first * half : last * half], right
        )

    projected = jnp.dot(
        after(normed_all, up_other), qkv_full, preferred_element_type=F32
    ).astype(BF16)
    attended_low, log_total = attention_call(
        attention_forward_kernel,
        [projected],
        [(part, BF16), (part, F32)],
        [BF16] * 3,
        places,
        lengths,
        2,
    )
    attended_low = after(attended_low, up_part)
    held = scatter_core(times(attended_low, out_full))
    got = scatter_first(held)
    cot_all = gather_third(*after(cot_steps, held))
    mixed = x + scatter_third(held, *got, *scatter_second(held, *got))
    second, second_pull = jax.vjp(layer_norm, mixed, norm_gains[1], norm_biases[1])
    second_low = second.astype(BF16)
    steps = gather_first(second_low)
    grad_activated = contract_last(after(cot_all, second_low), down_full)
    steps = gather_second(*after(steps, grad_activated))
    second_all = gather_third(*steps)
    bias_part = lax.dynamic_slice_in_dim(
        hidden_bias.reshape(blk, lanes, 2, units), b, 1, 0
    )
    bias_part = lax.dynamic_index_in_dim(bias_part, y, 2, keepdims=False).reshape(-1)
    hidden_pre = jnp.dot(second_all, up_full, preferred_element_type=F32) + bias_part
    activated, slope = gelu(hidden_pre)
    activated_low = activated.astype(BF16)
    grad_hidden_low = (grad_activated * slope).astype(BF16)

    held = scatter_core(times_transposed(grad_hidden_low, up_full))
    got = scatter_first(held)
    down_term = contract_first(after(activated_low, held), cot_all).astype(BF16)
    down_sum = scatter_z(down_term, 0)
    hidden_sum = jnp.sum(after(grad_hidden_low, down_term).astype(F32), axis=0)
    last = scatter_second(held, *after(got, hidden_sum))
    product = times(after(activated_low, last), down_full)
    result_high = product(12, 16).astype(BF16), product(8, 12).astype(BF16)
    grad_second = scatter_third(held, *got, *last)
    grad_mixed_norm, gain_two, bias_two = second_pull(grad_second)
    grad_mixed = cot_low.astype(F32) + grad_mixed_norm
    mixed_low = grad_mixed.astype(BF16)
    steps = gather_first(mixed_low)
    up_term = contract_first(second_all, after(grad_hidden_low, mixed_low)).astype(BF16)
    up_sum = scatter_z(up_term.reshape(blk, -1, lanes * units), 1)
    steps = gather_second(*after(steps, up_term))
    product = times(after(activated_low, up_term), down_full)
    result_low = product(0, 8).astype(BF16)
    mixed_all = gather_third(*after(steps, result_low))
    result_held = scatter_pair(
        lambda first, last, *others: result_low[first * half : last * half],
        *[flip_core(piece) for piece in result_high],
    )
    grad_attended = contract_last(mixed_all, out_full).astype(BF16)
    result_got = scatter_first(result_held, mixed_all)
    (grad_projected,) = attention_call(
        attention_backward_kernel,
        [projected, grad_attended, log_total],
        [(3 * part, BF16)],
        [BF16] * 4 + [F32] * 3,
        places,
        lengths,
        5,
    )
    result_last = scatter_second(result_held, *after(result_got, grad_projected))
    qkv_term = contract_first(
        normed_all, after(grad_projected, up_sum, down_sum, *result_last)
    ).astype(BF16)
    qkv_sum = scatter_z(qkv_term.reshape(blk, -1, 3 * part), 1)
    result = mixed + scatter_third(result_held, *after(result_got, qkv_term), *result_last)
    up_pair = split_sum(after(up_sum, *result_last))
    held = scatter_core(times_transposed(after(grad_projected, qkv_term, result), qkv_full))
    got = scatter_first(held, up_pair)
    out_term = contract_first(after(attended_low, held), mixed_all).astype(BF16)
    grad_normed = scatter_third(held, *got, *scatter_second(held, *got))
    grad_input_norm, gain_one, bias_one = first_pull(grad_normed)
    qkv_pair = split_sum(qkv_sum)
    grad_input = (grad_mixed + grad_input_norm).astype(BF16)

    qkv_got = exchange(*qkv_pair)
    up_got = exchange(up_pair[0], after(up_pair[1], gain_one))
    grad_up = merge_columns(up_got, *up_cut)
    grad_qkv = merge_columns(qkv_got, *qkv_cut)
    norms, hidden_sum = sum_small(
        after(jnp.stack([gain_one, gain_two, bias_one, bias_two]), qkv_got), hidden_sum
    )
    out_sum = after(scatter_z(out_term, 0), norms)
    grad_out = lax.ppermute(out_sum, "dp", [(j, i) for i, j in route]).astype(F32)
    return (
        result.astype(BF16).reshape(1, 1, rows, width),
        grad_input.reshape(1, 1, rows, width),
        grad_qkv,
        grad_out,
        grad_up,
        down_sum.astype(F32),
        norms[:2],
        norms[2:],
        hidden_sum,
    )


def solution(mesh):
    return jax.shard_map(
        body,
        mesh=mesh,
        in_specs=(
            P("dp", "blk", None, None),
            P("dp", "blk", None, None),
            P("dp", None),
            P(),
            P(("blk", "dp"), None),
            P(("blk", "dp"), None),
            P(("blk", "dp"), None),
            P(("blk", "dp"), None),
            P(),
            P(),
            P(),
        ),
        out_specs=(
            P("dp", "blk", None, None),
            P("dp", "blk", None, None),
            P(("blk", "dp"), None),
            P(("blk", "dp"), None),
            P(("blk", "dp"), None),
            P(("blk", "dp"), None),
            P(None, ("blk", "dp")),
            P(None, ("blk", "dp")),
            P(("blk", "dp")),
        ),
        check_vma=False,
    )
```

```python
import jax
import jax.numpy as jnp
from jax import lax
from jax.experimental import pallas as pl
from jax.experimental.pallas import tpu as pltpu
from jax.sharding import PartitionSpec as P

HEAD = 128
BLK_A = 256
BLK_B = 64
SPLITS = ((0, BLK_A), (BLK_A, BLK_A + BLK_B))
BLOCK_HALF = (BLK_A + BLK_B) // 2

EPSILON = 1e-05
NEGATIVE = -1e30
SCALE = HEAD ** (-0.5)
BF16 = jnp.bfloat16
F32 = jnp.float32


def after(value, *others):
    return lax.optimization_barrier((value, others))[0]


def layer_norm(value, gain, bias):
    center = value - jnp.mean(value, axis=-1, keepdims=True)
    spread = jnp.mean(center * center, axis=-1, keepdims=True)
    return center * lax.rsqrt(spread + EPSILON) * gain + bias


def gelu(v):
    rate = (2.0 / 3.141592653589793) ** 0.5
    squared = v * v
    bend = jnp.tanh(rate * v * (1.0 + 0.044715 * squared))
    rise = 0.5 * (1.0 + bend)
    slope = rise + 0.5 * v * (1.0 - bend * bend) * rate * (1.0 + 3 * 0.044715 * squared)
    return v * rise, slope


def contract_last(left, right):
    return lax.dot_general(
        left, right, (((1,), (1,)), ((), ())), preferred_element_type=F32
    )


def contract_first(left, right):
    return lax.dot_general(
        left, right, (((0,), (0,)), ((), ())), preferred_element_type=F32
    )


def flip(axis, bits, block):
    count = lax.axis_size(axis)
    return lax.ppermute(block, axis, [(i ^ bits, i) for i in range(count)])


def flip_core(block):
    return flip("blk", 1, block)


def flip_x(block):
    return flip("blk", 2, block)


def flip_y(block):
    return flip("dp", 1, block)


def lines():
    count = lax.axis_size("dp")
    return [[z * 2 + y for z in range(count // 2)] for y in range(2)]


def gather_z(part, axis):
    return lax.all_gather(part, "dp", axis_index_groups=lines(), axis=axis, tiled=True)


def scatter_z(total, axis):
    return lax.psum_scatter(
        total, "dp", axis_index_groups=lines(), scatter_dimension=axis, tiled=True
    )


def column(groups, blk, runs, width, group, b, run, y):
    return (((group * blk + b) * runs + run) * 2 + y) * width


def split_columns(shard, groups, blk, runs, width):
    rows = shard.shape[0]
    count = groups * runs * width

    def kernel(y_ref, in_ref, out_ref):
        b = pl.program_id(1)
        y = jnp.where(pl.program_id(0) == 0, 1 - y_ref[0], y_ref[0])
        for group in range(groups):
            for run in range(runs):
                start = column(groups, blk, runs, width, group, b, run, y)
                to = (group * runs + run) * width
                out_ref[0, 0, :, to : to + width] = in_ref[:, pl.ds(pl.multiple_of(start, 128), width)]

    return pl.pallas_call(
        kernel,
        grid_spec=pltpu.PrefetchScalarGridSpec(
            num_scalar_prefetch=1,
            grid=(2, blk),
            in_specs=[pl.BlockSpec(shard.shape, lambda i, j, *_: (0, 0))],
            out_specs=pl.BlockSpec((1, 1, rows, count), lambda i, j, *_: (j, i, 0, 0)),
        ),
        out_shape=jax.ShapeDtypeStruct((blk, 2, rows, count), shard.dtype),
        compiler_params=pltpu.CompilerParams(vmem_limit_bytes=16 * 2**20),
        cost_estimate=pl.CostEstimate(flops=0, bytes_accessed=4 * shard.size, transcendentals=0),
    )((lax.axis_index("dp") % 2).reshape(1), shard)


def join_y(own, other):
    blk, rows, count = own.shape

    def kernel(y_ref, own_ref, other_ref, out_ref):
        out_ref[0, y_ref[0]] = own_ref[0]
        out_ref[0, 1 - y_ref[0]] = other_ref[0]

    piece = pl.BlockSpec((1, rows, count), lambda i, *_: (i, 0, 0))
    return pl.pallas_call(
        kernel,
        grid_spec=pltpu.PrefetchScalarGridSpec(
            num_scalar_prefetch=1,
            grid=(blk,),
            in_specs=[piece, piece],
            out_specs=pl.BlockSpec((1, 2, rows, count), lambda i, *_: (i, 0, 0, 0)),
        ),
        out_shape=jax.ShapeDtypeStruct((blk, 2, rows, count), own.dtype),
        compiler_params=pltpu.CompilerParams(vmem_limit_bytes=16 * 2**20),
        cost_estimate=pl.CostEstimate(flops=0, bytes_accessed=8 * own.size, transcendentals=0),
    )((lax.axis_index("dp") % 2).reshape(1), own, other)


def merge_columns(parts, groups, blk, runs, width):
    _, _, rows, count = parts.shape

    def kernel(in_ref, out_ref):
        b = pl.program_id(0)
        for y in range(2):
            for group in range(groups):
                for run in range(runs):
                    start = column(groups, blk, runs, width, group, b, run, y)
                    at = (group * runs + run) * width
                    out_ref[:, pl.ds(pl.multiple_of(start, 128), width)] = in_ref[
                        0, y, :, at : at + width
                    ].astype(F32)

    return pl.pallas_call(
        kernel,
        grid=(blk,),
        in_specs=[pl.BlockSpec((1, 2, rows, count), lambda i: (i, 0, 0, 0))],
        out_specs=pl.BlockSpec((rows, blk * 2 * count), lambda i: (0, 0)),
        out_shape=jax.ShapeDtypeStruct((rows, blk * 2 * count), F32),
        compiler_params=pltpu.CompilerParams(vmem_limit_bytes=16 * 2**20),
        cost_estimate=pl.CostEstimate(flops=0, bytes_accessed=6 * parts.size, transcendentals=0),
    )(parts)


def exchange(own, other):
    return lax.all_to_all(join_y(own, other), "blk", 0, 0)


TOPS = ((0, 5), (3, 4))
BOTTOMS = ((1, 2), (7, 6))


MOST = ((0, 0, 2, 0), (1, 0, 1, 5), (1, 1, 1, 2), (2, 0, 1, 3), (2, 1, 1, 7))
REST = ((0, 0, 1, 4), (1, 0, 1, 6))


def diagonal_of(from_x, from_y):
    half = from_x.shape[0] // 2
    return flip_y(from_x[:half]), flip_x(from_y[half:])


def assemble(pieces, runs, whole=None):
    half = BLOCK_HALF
    columns = pieces[0].shape[1]
    side_pieces = len(pieces) // 2
    copies, total = [], 0
    for side in range(2):
        for piece, start, count, to in runs:
            copies.append(
                (side * side_pieces + piece, start * half, count * half, (side * 8 + to) * half, total)
            )
            total += count * half

    def kernel(*refs):
        out_ref, held_ref, in_sems, out_sems = refs[-4:]
        reads, writes = [], []
        for i, (piece, start, count, to, at) in enumerate(copies):
            there = held_ref.at[pl.ds(at, count)]
            source = refs[piece].at[pl.ds(start, count)]
            reads.append(pltpu.make_async_copy(source, there, in_sems.at[i]))
            writes.append(pltpu.make_async_copy(there, out_ref.at[pl.ds(to, count)], out_sems.at[i]))
        for read in reads:
            read.start()
        for read, write in zip(reads, writes):
            read.wait()
            write.start()
        for write in writes:
            write.wait()

    inputs = [*pieces] if whole is None else [*pieces, whole]
    return pl.pallas_call(
        kernel,
        in_specs=[pl.BlockSpec(memory_space=pl.ANY)] * len(inputs),
        out_specs=pl.BlockSpec(memory_space=pltpu.HBM),
        out_shape=jax.ShapeDtypeStruct((16 * half, columns), pieces[0].dtype),
        input_output_aliases={} if whole is None else {len(inputs) - 1: 0},
        scratch_shapes=[pltpu.VMEM((total, columns), pieces[0].dtype)]
        + [pltpu.SemaphoreType.DMA((len(copies),))] * 2,
        compiler_params=pltpu.CompilerParams(vmem_limit_bytes=56 * 2**20),
        cost_estimate=pl.CostEstimate(flops=0, bytes_accessed=4 * total * columns, transcendentals=0),
    )(*inputs)


def last_sends(near, got, from_x, from_y):
    half = near.shape[0] // 4
    to_x = near[2 * half : 3 * half].astype(F32) + got[2 * half : 3 * half].astype(F32)
    to_y = near[3 * half :].astype(F32) + got[3 * half :].astype(F32)
    to_x = (to_x + from_y[:half].astype(F32)).astype(BF16)
    to_y = (to_y + from_x[:half].astype(F32)).astype(BF16)
    return to_x, to_y


def own_rows(near, got, from_x, from_y):
    half = near.shape[0] // 4
    own = near[: 2 * half].astype(F32) + got[: 2 * half].astype(F32)
    return own + jnp.concatenate([from_x[half:], from_y[half:]], axis=0).astype(F32)


def add_last(own, last_x, last_y):
    return own + jnp.concatenate([last_y, last_x], axis=0).astype(F32)


def sum_blk(norms):
    blk = lax.axis_size("blk")
    parts = norms.reshape(norms.shape[0], blk, -1).transpose(1, 0, 2)
    return jnp.sum(lax.all_to_all(parts, "blk", 0, 0), axis=0)


def sum_dp(parts, hidden):
    dp = lax.axis_size("dp")
    count = parts.shape[0]
    parts = parts.reshape(count, dp, -1).transpose(1, 0, 2)
    share = parts.shape[2]
    hidden = jnp.repeat(hidden.reshape(dp // 2, -1), 2, axis=0)
    both = jnp.concatenate([parts.reshape(dp, -1), hidden], axis=1)
    both = lax.all_to_all(both, "dp", 0, 0)
    mine = jnp.arange(dp) % 2 == lax.axis_index("dp") % 2
    return (
        jnp.sum(both[:, : count * share], axis=0).reshape(count, share),
        jnp.sum(jnp.where(mine[:, None], both[:, count * share :], 0.0), axis=0),
    )


def runs_of(places_ref, sequence, column, block, half):
    first, last = SPLITS[column]
    if first < half:
        top = min(last, half)
        yield places_ref[sequence, column, block], slice(first, top), slice(0, top - first)
    if last > half:
        start = max(first, half)
        yield (
            places_ref[sequence, column, 4 + block],
            slice(start - half, last - half),
            slice(start - first, last - first),
        )


def load_block(places_ref, sequence, column, block, ref, lanes, to_ref, row):
    for which, here, there in runs_of(places_ref, sequence, column, block, ref.shape[1]):
        to_ref[row + there.start : row + there.stop] = ref[which, here, lanes]


def store_block(places_ref, sequence, column, block, ref, lanes, value):
    for which, here, there in runs_of(places_ref, sequence, column, block, ref.shape[1]):
        ref[which, here, lanes] = value[there]


def scores_of(queries, keys, first, length):
    scores = contract_last(queries, keys) * SCALE
    key_places = lax.broadcasted_iota(jnp.int32, scores.shape, 1)
    query_places = first + lax.broadcasted_iota(jnp.int32, scores.shape, 0)
    allowed = (key_places <= query_places) & (key_places < length)
    return jnp.where(allowed, scores, NEGATIVE)


def attention_steps():
    for column, (first, last) in enumerate(SPLITS):
        size = last - first
        step = 1 if size * 4 > 512 else 4
        yield column, size, [(p, step, (p + step) * size) for p in range(0, 4, step)]


def attention_forward_kernel(places_ref, lengths_ref, in_ref, out_ref, log_ref, q_ref, k_ref, v_ref):
    sequence = pl.program_id(0)
    heads = in_ref.shape[-1] // (3 * HEAD)
    for column, size, runs in attention_steps():
        length = lengths_ref[sequence, column]
        for head in range(heads):
            for third, ref in enumerate((q_ref, k_ref, v_ref)):
                lanes = slice((third * heads + head) * HEAD, (third * heads + head + 1) * HEAD)
                for block in range(4):
                    load_block(places_ref, sequence, column, block, in_ref, lanes, ref, block * size)
            lanes = slice(head * HEAD, (head + 1) * HEAD)
            for start, step, keys in runs:
                rows = slice(start * size, (start + step) * size)
                scores = scores_of(q_ref[rows], k_ref[:keys], start * size, length)
                peak = jnp.max(scores, axis=-1, keepdims=True)
                weights = jnp.exp(scores - peak)
                total = jnp.sum(weights, axis=-1, keepdims=True)
                attended = jnp.dot(weights.astype(BF16), v_ref[:keys], preferred_element_type=F32)
                attended = (attended / total).astype(BF16)
                log_total = jnp.broadcast_to(peak + jnp.log(total), (step * size, HEAD))
                for i in range(step):
                    here = slice(i * size, (i + 1) * size)
                    at = (places_ref, sequence, column, start + i)
                    store_block(*at, out_ref, lanes, attended[here])
                    store_block(*at, log_ref, lanes, log_total[here])


def attention_backward_kernel(
    places_ref,
    lengths_ref,
    in_ref,
    grad_ref,
    log_ref,
    out_ref,
    q_ref,
    k_ref,
    v_ref,
    g_ref,
    log_rows_ref,
    dk_ref,
    dv_ref,
):
    sequence = pl.program_id(0)
    heads = in_ref.shape[-1] // (3 * HEAD)
    for column, size, runs in attention_steps():
        length = lengths_ref[sequence, column]
        for head in range(heads):
            columns = [
                slice((third * heads + head) * HEAD, (third * heads + head + 1) * HEAD)
                for third in range(3)
            ]
            lanes = slice(head * HEAD, (head + 1) * HEAD)
            for block in range(4):
                at = (places_ref, sequence, column, block)
                load_block(*at, in_ref, columns[0], q_ref, block * size)
                load_block(*at, in_ref, columns[1], k_ref, block * size)
                load_block(*at, in_ref, columns[2], v_ref, block * size)
                load_block(*at, grad_ref, lanes, g_ref, block * size)
                load_block(*at, log_ref, lanes, log_rows_ref, block * size)
            dk_ref[...] = jnp.zeros_like(dk_ref)
            dv_ref[...] = jnp.zeros_like(dv_ref)
            for start, step, keys in runs:
                rows = slice(start * size, (start + step) * size)
                queries, grads = q_ref[rows], g_ref[rows]
                scores = scores_of(queries, k_ref[:keys], start * size, length)
                probs = jnp.exp(scores - log_rows_ref[rows, :1])
                grad_probs = contract_last(grads, v_ref[:keys])
                delta = jnp.sum(probs * grad_probs, axis=-1, keepdims=True)
                grad_scores = (probs * (grad_probs - delta)).astype(BF16)
                dv_ref[:keys] += contract_first(probs.astype(BF16), grads)
                dk_ref[:keys] += contract_first(grad_scores, queries)
                dq = jnp.dot(grad_scores, k_ref[:keys], preferred_element_type=F32) * SCALE
                dq = dq.astype(BF16)
                for i in range(step):
                    at = (places_ref, sequence, column, start + i)
                    store_block(*at, out_ref, columns[0], dq[i * size : (i + 1) * size])
            for block in range(4):
                here = slice(block * size, (block + 1) * size)
                at = (places_ref, sequence, column, block)
                store_block(*at, out_ref, columns[1], (dk_ref[here] * SCALE).astype(BF16))
                store_block(*at, out_ref, columns[2], dv_ref[here].astype(BF16))


def attention_call(kernel, arrays, outs, scratch, places, lengths, matmuls):
    count = 4 * BLK_A
    half = arrays[0].shape[0] // 16

    def spec(columns):
        return pl.BlockSpec((16, half, columns), lambda s, *_: (0, 0, 0))

    heads = arrays[0].shape[1] // (3 * HEAD)
    results = pl.pallas_call(
        kernel,
        grid_spec=pltpu.PrefetchScalarGridSpec(
            num_scalar_prefetch=2,
            grid=(2,),
            in_specs=[spec(a.shape[1]) for a in arrays],
            out_specs=[spec(columns) for columns, _ in outs],
            scratch_shapes=[pltpu.VMEM((count, HEAD), dtype) for dtype in scratch],
        ),
        out_shape=[jax.ShapeDtypeStruct((16, half, c), dtype) for c, dtype in outs],
        compiler_params=pltpu.CompilerParams(vmem_limit_bytes=48 * 2**20),
        cost_estimate=pl.CostEstimate(
            flops=matmuls * 2 * heads * count * count * HEAD * 2,
            bytes_accessed=16 * half * HEAD * heads * 2 * 4,
            transcendentals=2 * heads * count * count,
        ),
    )(places, lengths, *[a.reshape(16, half, -1) for a in arrays])
    return [r.reshape(16 * half, -1) for r in results]


def body(
    hidden_in,
    cotangent,
    seq_lengths,
    block_order,
    w_qkv,
    w_out,
    w_up,
    w_down,
    norm_gains,
    norm_biases,
    hidden_bias,
):
    blk, dp = lax.axis_size("blk"), lax.axis_size("dp")
    lanes = dp // 2
    b, d = lax.axis_index("blk"), lax.axis_index("dp")
    z, y = d // 2, d % 2
    rows, width = hidden_in.shape[2:]
    pairs = width // HEAD // blk // 2
    part = pairs * HEAD
    half = rows // 2
    shard = w_qkv.shape[0]
    units = w_down.shape[0]
    x = hidden_in.reshape(rows, width).astype(F32)
    cot_low = cotangent.reshape(rows, width)

    qkv_cut = (3, blk, pairs, HEAD)
    up_cut = (1, blk, lanes, units)

    pieces = [[p for p in range(dp) if (p * shard // HEAD) % 2 == to_y] for to_y in range(2)]
    route = [(pieces[to_y][lane], lane * 2 + to_y) for to_y in range(2) for lane in range(lanes)]

    near = [(core, far) for core in range(2) for far in range(2)]
    holders = jnp.stack(
        [jnp.take(block_order, b ^ (far * 2 + core), axis=1) for core, far in near], axis=1
    )
    found = holders[:, None, :] == jnp.arange(4, dtype=jnp.int32)[None, :, None]
    tables = jnp.array(
        [[[core * 8 + t[s][far] for core, far in near] for t in (TOPS, BOTTOMS)] for s in range(2)],
        jnp.int32,
    )
    places = jnp.sum(jnp.where(found[None, :, None], tables[:, None, :, None], 0), axis=-1)
    places = places.reshape(2, 2, 8)

    gate = [seq_lengths]

    def seal(*values):
        gate[0], values = lax.optimization_barrier((gate[0], values))
        return values if len(values) > 1 else values[0]

    def enter(*values):
        values = lax.optimization_barrier((values, gate[0]))[0]
        return values if len(values) > 1 else values[0]

    def rows_of(array, first, last):
        return array[first * half : last * half]

    def times(left, right):
        return jnp.dot(left, right, preferred_element_type=F32)

    out_full = gather_z(lax.ppermute(w_out, "dp", route), 0)
    normed, first_pull = jax.vjp(layer_norm, x, norm_gains[0], norm_biases[0])
    normed_low = normed.astype(BF16)
    qkv_pair = lax.all_to_all(split_columns(w_qkv, *qkv_cut), "blk", 0, 0)
    qkv_pair, a_x, a_y, a_core, lengths = seal(
        qkv_pair,
        flip_x(normed_low),
        flip_y(normed_low),
        flip_core(normed_low),
        flip_y(after(seq_lengths, normed_low)),
    )
    lengths = jnp.concatenate([seq_lengths, lengths], axis=0)

    normed_low, qkv_pair, a_x, a_y, a_core = enter(normed_low, qkv_pair, a_x, a_y, a_core)
    qkv_part = join_y(qkv_pair[:, 1], flip_y(qkv_pair[:, 0])).reshape(blk, 2 * shard, 3 * part)
    qkv_full = gather_z(after(qkv_part, out_full), 1).reshape(width, 3 * part)
    down_full = gather_z(after(w_down, qkv_part), 0)
    a_across = diagonal_of(a_x, a_y)
    a_others = a_core, flip_core(a_x), flip_core(a_y)
    normed_all = assemble([normed_low, a_x, a_y, *a_others], MOST)
    a_across, normed_all, up_pair, _ = seal(
        a_across, normed_all, split_columns(enter(w_up), *up_cut), qkv_part
    )

    cot_low, normed_all, a_across = enter(cot_low, normed_all, a_across)
    cot_x, cot_y, cot_core = flip_x(cot_low), flip_y(cot_low), flip_core(cot_low)
    normed_all = assemble([*a_across, *[flip_core(piece) for piece in a_across]], REST, normed_all)
    cot_x, cot_y, cot_core, normed_all = seal(cot_x, cot_y, cot_core, normed_all)

    cot_x, cot_y, cot_core = enter(cot_x, cot_y, cot_core)
    cot_across = diagonal_of(cot_x, cot_y)
    cot_others = cot_core, flip_core(cot_x), flip_core(cot_y)
    cot_across, cot_others, qkv_full = seal(cot_across, cot_others, qkv_full)

    normed_all, up_pair, cot_across = enter(normed_all, up_pair, cot_across)
    projected, up_pair = seal(
        times(normed_all, qkv_full).astype(BF16), lax.all_to_all(up_pair, "blk", 0, 0)
    )
    projected, up_pair = enter(projected, up_pair)
    up_own, up_other = up_pair[:, 1], flip_y(up_pair[:, 0])
    attended_low, log_total = attention_call(
        attention_forward_kernel,
        [projected],
        [(part, BF16), (part, F32)],
        [BF16] * 3,
        places,
        lengths,
        2,
    )
    cot_others = [*cot_others, *[flip_core(piece) for piece in cot_across]]
    attended_low, up_other, cot_others = seal(attended_low, up_other, cot_others)
    up_part = join_y(*enter(up_own, up_other)).reshape(blk, 2 * shard, lanes * units)
    up_full = gather_z(after(up_part, qkv_full), 1).reshape(width, lanes * units)

    def start_sum(left, multiply, *beside):
        left = enter(left)
        far, near = [
            flip_core(multiply(rows_of(left, *run)).astype(BF16)) for run in ((12, 16), (8, 12))
        ]
        middle = far.shape[0] // 2
        to_x = (multiply(rows_of(left, 4, 6)) + far[:middle].astype(F32)).astype(BF16)
        to_y = (multiply(rows_of(left, 6, 8)) + far[middle:].astype(F32)).astype(BF16)
        to_x, to_y, near, beside = seal(to_x, to_y, near, beside)
        return enter(to_x), enter(to_y), near, beside

    to_x, to_y, near, _ = start_sum(attended_low, lambda v: times(v, out_full))
    own = times(rows_of(enter(attended_low), 0, 4), out_full)
    cot_all = assemble(enter(*[cot_low, cot_x, cot_y, *cot_others[:3]]), MOST)
    cot_all = assemble(enter(*[*cot_across, *cot_others[3:]]), REST, cot_all)
    from_x, from_y, own, cot_all = seal(flip_x(to_x), flip_y(to_y), own, cot_all)
    sums = enter(own, near, from_x, from_y)
    to_x, to_y = last_sends(*sums)
    last_x, last_y, own, down_full = seal(
        flip_x(to_x), flip_y(to_y), own_rows(*after(sums, to_x, to_y)), down_full
    )
    mixed = x + add_last(*enter(own, last_x, last_y))
    second, second_pull = jax.vjp(layer_norm, mixed, norm_gains[1], norm_biases[1])
    second_low = seal(second.astype(BF16))

    def gather_rows(part_low, beside, also):
        part_low = enter(part_low)
        from_x, from_y, from_core = flip_x(part_low), flip_y(part_low), flip_core(part_low)
        from_x, from_y, from_core, beside = seal(from_x, from_y, from_core, beside())
        part_low, from_x, from_y, from_core = enter(part_low, from_x, from_y, from_core)
        across = diagonal_of(from_x, from_y)
        others = from_core, flip_core(from_x), flip_core(from_y)
        across, whole, also = seal(
            across, assemble([part_low, from_x, from_y, *others], MOST), also(beside)
        )
        across, whole = enter(across, whole)
        whole = assemble([*across, *[flip_core(piece) for piece in across]], REST, whole)
        return seal(whole), beside, also

    second_all, grad_activated, up_full = gather_rows(
        second_low, lambda: contract_last(enter(cot_all), down_full), lambda beside: up_full
    )
    bias_part = lax.dynamic_slice_in_dim(hidden_bias.reshape(blk, lanes, 2, units), b, 1, 0)
    bias_part = lax.dynamic_index_in_dim(bias_part, y, 2, keepdims=False).reshape(-1)
    hidden_pre = times(enter(second_all), up_full) + bias_part
    activated, slope = gelu(hidden_pre)
    activated_low, grad_hidden_low = seal(
        activated.astype(BF16), (grad_activated * slope).astype(BF16)
    )

    to_x, to_y, near, _ = start_sum(grad_hidden_low, lambda v: contract_last(v, up_full))
    down_term = contract_first(enter(activated_low), cot_all).astype(BF16)
    down_sum = scatter_z(down_term, 0)
    own = contract_last(rows_of(enter(grad_hidden_low), 0, 4), up_full)
    from_x, from_y, own, down_term = seal(flip_x(to_x), flip_y(to_y), own, down_term)
    sums = enter(own, near, from_x, from_y)
    to_x, to_y = last_sends(*sums)
    result_low = times(rows_of(enter(activated_low), 0, 8), down_full).astype(BF16)
    last_x, last_y, own, result_low = seal(
        flip_x(to_x), flip_y(to_y), own_rows(*after(sums, to_x, to_y)), result_low
    )
    grad_mixed_norm, gain_two, bias_two = second_pull(add_last(*enter(own, last_x, last_y)))
    grad_mixed = cot_low.astype(F32) + grad_mixed_norm
    mixed_low, gain_two, bias_two = seal(grad_mixed.astype(BF16), gain_two, bias_two)

    def beside_gather():
        up_term = contract_first(second_all, enter(grad_hidden_low)).astype(BF16)
        result_near = times(rows_of(enter(activated_low), 8, 12), down_full).astype(BF16)
        return up_term, result_near

    def beside_second(beside):
        far = times(rows_of(enter(activated_low), 12, 16), down_full).astype(BF16)
        return far, flip_core(enter(beside[1])), down_sum

    mixed_all, (up_term, _), (result_far, got_near, down_sum) = gather_rows(
        mixed_low, beside_gather, beside_second
    )
    up_sum = scatter_z(up_term.reshape(blk, -1, lanes * units), 1)
    mixed_all, result_far = enter(mixed_all, result_far)
    got_far, grad_attended = seal(
        flip_core(result_far), contract_last(mixed_all, out_full).astype(BF16)
    )
    got_far, grad_attended = enter(got_far, grad_attended)
    to_x = rows_of(result_low, 4, 6).astype(F32) + got_far[: 2 * half].astype(F32)
    to_y = rows_of(result_low, 6, 8).astype(F32) + got_far[2 * half :].astype(F32)
    to_x, to_y = to_x.astype(BF16), to_y.astype(BF16)
    from_x, from_y = flip_x(to_x), flip_y(to_y)
    grad_attended = after(grad_attended, to_x, to_y)
    (grad_projected,) = attention_call(
        attention_backward_kernel,
        [projected, grad_attended, log_total],
        [(3 * part, BF16)],
        [BF16] * 4 + [F32] * 3,
        places,
        lengths,
        5,
    )
    qkv_term = contract_first(normed_all, grad_projected).astype(BF16)
    from_x, from_y, grad_projected, qkv_term = seal(from_x, from_y, grad_projected, qkv_term)

    def split_sum(total):
        parts = total.reshape(blk, 2, shard, -1)
        other = flip_y(lax.dynamic_index_in_dim(parts, 1 - y, 1, keepdims=False))
        return lax.dynamic_index_in_dim(parts, y, 1, keepdims=False), other

    qkv_sum = scatter_z(qkv_term.reshape(blk, -1, 3 * part), 1)
    result_sums = enter(rows_of(result_low, 0, 4), got_near, from_x, from_y)
    to_x, to_y = last_sends(*result_sums)
    left = after(grad_projected, to_x, to_y)
    far, near = [
        contract_last(rows_of(left, *run), qkv_full).astype(BF16) for run in ((12, 16), (8, 12))
    ]
    far, near, last_x, last_y = seal(far, near, flip_x(to_x), flip_y(to_y))
    left, far, near = enter(grad_projected, far, near)
    far, near = flip_core(far), flip_core(near)
    up_pair = split_sum(enter(up_sum))
    to_x = contract_last(rows_of(left, 4, 6), qkv_full) + far[: 2 * half].astype(F32)
    to_y = contract_last(rows_of(left, 6, 8), qkv_full) + far[2 * half :].astype(F32)
    to_x, to_y, up_pair = seal(to_x.astype(BF16), to_y.astype(BF16), up_pair)
    to_x, to_y = enter(to_x, to_y)
    hidden_sum = jnp.sum(enter(grad_hidden_low).astype(F32), axis=0)
    own = contract_last(rows_of(enter(grad_projected), 0, 4), qkv_full)
    result = mixed + add_last(own_rows(*enter(*result_sums)), last_x, last_y)
    out_term = contract_first(enter(attended_low), mixed_all).astype(BF16)
    from_x, from_y, own, result, out_term, hidden_sum = seal(
        flip_x(to_x), flip_y(to_y), own, result, out_term, hidden_sum
    )
    sums = enter(own, near, from_x, from_y)
    to_x, to_y = last_sends(*sums)
    last_x, last_y, own = seal(flip_x(to_x), flip_y(to_y), own_rows(*after(sums, to_x, to_y)))

    grad_input_norm, gain_one, bias_one = first_pull(add_last(*enter(own, last_x, last_y)))
    grad_input = (grad_mixed + grad_input_norm).astype(BF16)
    up_got = exchange(*enter(*up_pair))
    qkv_pair = split_sum(enter(qkv_sum))
    up_got, qkv_pair, gain_one, bias_one, grad_input, result = seal(
        up_got, qkv_pair, gain_one, bias_one, grad_input, result.astype(BF16)
    )

    norms = sum_blk(enter(jnp.stack([gain_one, gain_two, bias_one, bias_two])))
    qkv_got = exchange(*enter(*qkv_pair))
    out_sum = scatter_z(after(out_term, qkv_sum), 0)
    grad_up = merge_columns(enter(up_got), *up_cut)
    norms, qkv_got, grad_up = seal(norms, qkv_got, grad_up)
    norms, hidden_sum = sum_dp(enter(norms), hidden_sum)
    grad_qkv = merge_columns(enter(qkv_got), *qkv_cut)
    out_sum = after(out_sum, norms)
    grad_out = lax.ppermute(out_sum, "dp", [(j, i) for i, j in route]).astype(F32)
    return (
        result.reshape(1, 1, rows, width),
        grad_input.reshape(1, 1, rows, width),
        grad_qkv,
        grad_out,
        grad_up,
        down_sum.astype(F32),
        norms[:2],
        norms[2:],
        hidden_sum,
    )


def solution(mesh):
    return jax.shard_map(
        body,
        mesh=mesh,
        in_specs=(
            P("dp", "blk", None, None),
            P("dp", "blk", None, None),
            P("dp", None),
            P(),
            P(("blk", "dp"), None),
            P(("blk", "dp"), None),
            P(("blk", "dp"), None),
            P(("blk", "dp"), None),
            P(),
            P(),
            P(),
        ),
        out_specs=(
            P("dp", "blk", None, None),
            P("dp", "blk", None, None),
            P(("blk", "dp"), None),
            P(("blk", "dp"), None),
            P(("blk", "dp"), None),
            P(("blk", "dp"), None),
            P(None, ("blk", "dp")),
            P(None, ("blk", "dp")),
            P(("blk", "dp")),
        ),
        check_vma=False,
    )
```

```python
import jax
import jax.numpy as jnp
from jax import lax
from jax.experimental import pallas as pl
from jax.experimental.pallas import tpu as pltpu
from jax.sharding import PartitionSpec as P

HEAD = 128
BLK_A = 256
BLK_B = 64
SPLITS = ((0, BLK_A), (BLK_A, BLK_A + BLK_B))
BLOCK_HALF = (BLK_A + BLK_B) // 2

EPSILON = 1e-05
NEGATIVE = -1e30
SCALE = HEAD ** (-0.5)
BF16 = jnp.bfloat16
F32 = jnp.float32


def after(value, *others):
    return lax.optimization_barrier((value, others))[0]


def layer_norm(value, gain, bias):
    center = value - jnp.mean(value, axis=-1, keepdims=True)
    spread = jnp.mean(center * center, axis=-1, keepdims=True)
    return center * lax.rsqrt(spread + EPSILON) * gain + bias


def gelu(v):
    rate = (2.0 / 3.141592653589793) ** 0.5
    squared = v * v
    bend = jnp.tanh(rate * v * (1.0 + 0.044715 * squared))
    rise = 0.5 * (1.0 + bend)
    slope = rise + 0.5 * v * (1.0 - bend * bend) * rate * (1.0 + 3 * 0.044715 * squared)
    return v * rise, slope


def contract_last(left, right):
    return lax.dot_general(
        left, right, (((1,), (1,)), ((), ())), preferred_element_type=F32
    )


def contract_first(left, right):
    return lax.dot_general(
        left, right, (((0,), (0,)), ((), ())), preferred_element_type=F32
    )


def flip(axis, bits, block):
    count = lax.axis_size(axis)
    return lax.ppermute(block, axis, [(i ^ bits, i) for i in range(count)])


def flip_core(block):
    return flip("blk", 1, block)


def flip_x(block):
    return flip("blk", 2, block)


def flip_y(block):
    return flip("dp", 1, block)


def lines():
    count = lax.axis_size("dp")
    return [[z * 2 + y for z in range(count // 2)] for y in range(2)]


def gather_z(part, axis):
    return lax.all_gather(part, "dp", axis_index_groups=lines(), axis=axis, tiled=True)


def scatter_z(total, axis):
    return lax.psum_scatter(
        total, "dp", axis_index_groups=lines(), scatter_dimension=axis, tiled=True
    )


def column(groups, blk, runs, width, group, b, run, y):
    return (((group * blk + b) * runs + run) * 2 + y) * width


def split_columns(shard, groups, blk, runs, width):
    rows = shard.shape[0]
    count = groups * runs * width

    def kernel(y_ref, in_ref, out_ref):
        b = pl.program_id(1)
        y = jnp.where(pl.program_id(0) == 0, 1 - y_ref[0], y_ref[0])
        for group in range(groups):
            for run in range(runs):
                start = column(groups, blk, runs, width, group, b, run, y)
                to = (group * runs + run) * width
                out_ref[0, 0, :, to : to + width] = in_ref[:, pl.ds(pl.multiple_of(start, 128), width)]

    return pl.pallas_call(
        kernel,
        grid_spec=pltpu.PrefetchScalarGridSpec(
            num_scalar_prefetch=1,
            grid=(2, blk),
            in_specs=[pl.BlockSpec(shard.shape, lambda i, j, *_: (0, 0))],
            out_specs=pl.BlockSpec((1, 1, rows, count), lambda i, j, *_: (j, i, 0, 0)),
        ),
        out_shape=jax.ShapeDtypeStruct((blk, 2, rows, count), shard.dtype),
        compiler_params=pltpu.CompilerParams(vmem_limit_bytes=16 * 2**20),
        cost_estimate=pl.CostEstimate(flops=0, bytes_accessed=4 * shard.size, transcendentals=0),
    )((lax.axis_index("dp") % 2).reshape(1), shard)


def join_y(own, other):
    blk, rows, count = own.shape

    def kernel(y_ref, own_ref, other_ref, out_ref):
        out_ref[0, y_ref[0]] = own_ref[0]
        out_ref[0, 1 - y_ref[0]] = other_ref[0]

    piece = pl.BlockSpec((1, rows, count), lambda i, *_: (i, 0, 0))
    return pl.pallas_call(
        kernel,
        grid_spec=pltpu.PrefetchScalarGridSpec(
            num_scalar_prefetch=1,
            grid=(blk,),
            in_specs=[piece, piece],
            out_specs=pl.BlockSpec((1, 2, rows, count), lambda i, *_: (i, 0, 0, 0)),
        ),
        out_shape=jax.ShapeDtypeStruct((blk, 2, rows, count), own.dtype),
        compiler_params=pltpu.CompilerParams(vmem_limit_bytes=16 * 2**20),
        cost_estimate=pl.CostEstimate(flops=0, bytes_accessed=8 * own.size, transcendentals=0),
    )((lax.axis_index("dp") % 2).reshape(1), own, other)


def merge_columns(parts, groups, blk, runs, width):
    _, _, rows, count = parts.shape

    def kernel(in_ref, out_ref):
        b = pl.program_id(0)
        for y in range(2):
            for group in range(groups):
                for run in range(runs):
                    start = column(groups, blk, runs, width, group, b, run, y)
                    at = (group * runs + run) * width
                    out_ref[:, pl.ds(pl.multiple_of(start, 128), width)] = in_ref[
                        0, y, :, at : at + width
                    ].astype(F32)

    return pl.pallas_call(
        kernel,
        grid=(blk,),
        in_specs=[pl.BlockSpec((1, 2, rows, count), lambda i: (i, 0, 0, 0))],
        out_specs=pl.BlockSpec((rows, blk * 2 * count), lambda i: (0, 0)),
        out_shape=jax.ShapeDtypeStruct((rows, blk * 2 * count), F32),
        compiler_params=pltpu.CompilerParams(vmem_limit_bytes=16 * 2**20),
        cost_estimate=pl.CostEstimate(flops=0, bytes_accessed=6 * parts.size, transcendentals=0),
    )(parts)


def exchange(own, other):
    return lax.all_to_all(join_y(own, other), "blk", 0, 0)


TOPS = ((0, 5), (3, 4))
BOTTOMS = ((1, 2), (7, 6))


MOST = ((0, 0, 2, 0), (1, 0, 1, 5), (1, 1, 1, 2), (2, 0, 1, 3), (2, 1, 1, 7))
REST = ((0, 0, 1, 4), (1, 0, 1, 6))


def diagonal_of(from_x, from_y):
    half = from_x.shape[0] // 2
    return flip_y(from_x[:half]), flip_x(from_y[half:])


def assemble(pieces, runs, whole=None):
    half = BLOCK_HALF
    columns = pieces[0].shape[1]
    side_pieces = len(pieces) // 2
    copies, total = [], 0
    for side in range(2):
        for piece, start, count, to in runs:
            copies.append(
                (side * side_pieces + piece, start * half, count * half, (side * 8 + to) * half, total)
            )
            total += count * half

    def kernel(*refs):
        out_ref, held_ref, in_sems, out_sems = refs[-4:]
        reads, writes = [], []
        for i, (piece, start, count, to, at) in enumerate(copies):
            there = held_ref.at[pl.ds(at, count)]
            source = refs[piece].at[pl.ds(start, count)]
            reads.append(pltpu.make_async_copy(source, there, in_sems.at[i]))
            writes.append(pltpu.make_async_copy(there, out_ref.at[pl.ds(to, count)], out_sems.at[i]))
        for read in reads:
            read.start()
        for read, write in zip(reads, writes):
            read.wait()
            write.start()
        for write in writes:
            write.wait()

    inputs = [*pieces] if whole is None else [*pieces, whole]
    return pl.pallas_call(
        kernel,
        in_specs=[pl.BlockSpec(memory_space=pl.ANY)] * len(inputs),
        out_specs=pl.BlockSpec(memory_space=pltpu.HBM),
        out_shape=jax.ShapeDtypeStruct((16 * half, columns), pieces[0].dtype),
        input_output_aliases={} if whole is None else {len(inputs) - 1: 0},
        scratch_shapes=[pltpu.VMEM((total, columns), pieces[0].dtype)]
        + [pltpu.SemaphoreType.DMA((len(copies),))] * 2,
        compiler_params=pltpu.CompilerParams(vmem_limit_bytes=56 * 2**20),
        cost_estimate=pl.CostEstimate(flops=0, bytes_accessed=4 * total * columns, transcendentals=0),
    )(*inputs)


def last_sends(near, got, from_x, from_y):
    half = near.shape[0] // 4
    to_x = near[2 * half : 3 * half].astype(F32) + got[2 * half : 3 * half].astype(F32)
    to_y = near[3 * half :].astype(F32) + got[3 * half :].astype(F32)
    to_x = (to_x + from_y[:half].astype(F32)).astype(BF16)
    to_y = (to_y + from_x[:half].astype(F32)).astype(BF16)
    return to_x, to_y


def own_rows(near, got, from_x, from_y):
    half = near.shape[0] // 4
    own = near[: 2 * half].astype(F32) + got[: 2 * half].astype(F32)
    return own + jnp.concatenate([from_x[half:], from_y[half:]], axis=0).astype(F32)


def add_last(own, last_x, last_y):
    return own + jnp.concatenate([last_y, last_x], axis=0).astype(F32)


def sum_blk(norms):
    blk, b = lax.axis_size("blk"), lax.axis_index("blk")
    norms = norms + flip_core(norms)
    for bits in range(2, blk, 2):
        norms = norms + flip("blk", bits, norms)
    return lax.dynamic_slice_in_dim(norms, b * (norms.shape[1] // blk), norms.shape[1] // blk, 1)


def sum_dp(parts, hidden):
    dp = lax.axis_size("dp")
    count = parts.shape[0]
    parts = parts.reshape(count, dp, -1).transpose(1, 0, 2)
    share = parts.shape[2]
    hidden = jnp.repeat(hidden.reshape(dp // 2, -1), 2, axis=0)
    both = jnp.concatenate([parts.reshape(dp, -1), hidden], axis=1)
    both = lax.all_to_all(both, "dp", 0, 0)
    mine = jnp.arange(dp) % 2 == lax.axis_index("dp") % 2
    return (
        jnp.sum(both[:, : count * share], axis=0).reshape(count, share),
        jnp.sum(jnp.where(mine[:, None], both[:, count * share :], 0.0), axis=0),
    )


def runs_of(places_ref, sequence, column, block, half):
    first, last = SPLITS[column]
    if first < half:
        top = min(last, half)
        yield places_ref[sequence, column, block], slice(first, top), slice(0, top - first)
    if last > half:
        start = max(first, half)
        yield (
            places_ref[sequence, column, 4 + block],
            slice(start - half, last - half),
            slice(start - first, last - first),
        )


def load_block(places_ref, sequence, column, block, ref, lanes, to_ref, row):
    for which, here, there in runs_of(places_ref, sequence, column, block, ref.shape[1]):
        to_ref[row + there.start : row + there.stop] = ref[which, here, lanes]


def store_block(places_ref, sequence, column, block, ref, lanes, value):
    for which, here, there in runs_of(places_ref, sequence, column, block, ref.shape[1]):
        ref[which, here, lanes] = value[there]


def scores_of(queries, keys, first, length):
    scores = contract_last(queries, keys) * SCALE
    key_places = lax.broadcasted_iota(jnp.int32, scores.shape, 1)
    query_places = first + lax.broadcasted_iota(jnp.int32, scores.shape, 0)
    allowed = (key_places <= query_places) & (key_places < length)
    return jnp.where(allowed, scores, NEGATIVE)


def attention_steps():
    for column, (first, last) in enumerate(SPLITS):
        size = last - first
        step = 1 if size * 4 > 512 else 4
        yield column, size, [(p, step, (p + step) * size) for p in range(0, 4, step)]


def attention_forward_kernel(places_ref, lengths_ref, in_ref, out_ref, log_ref, q_ref, k_ref, v_ref):
    sequence = pl.program_id(0)
    heads = in_ref.shape[-1] // (3 * HEAD)
    for column, size, runs in attention_steps():
        length = lengths_ref[sequence, column]
        for head in range(heads):
            for third, ref in enumerate((q_ref, k_ref, v_ref)):
                lanes = slice((third * heads + head) * HEAD, (third * heads + head + 1) * HEAD)
                for block in range(4):
                    load_block(places_ref, sequence, column, block, in_ref, lanes, ref, block * size)
            lanes = slice(head * HEAD, (head + 1) * HEAD)
            for start, step, keys in runs:
                rows = slice(start * size, (start + step) * size)
                scores = scores_of(q_ref[rows], k_ref[:keys], start * size, length)
                peak = jnp.max(scores, axis=-1, keepdims=True)
                weights = jnp.exp(scores - peak)
                total = jnp.sum(weights, axis=-1, keepdims=True)
                attended = jnp.dot(weights.astype(BF16), v_ref[:keys], preferred_element_type=F32)
                attended = (attended / total).astype(BF16)
                log_total = jnp.broadcast_to(peak + jnp.log(total), (step * size, HEAD))
                for i in range(step):
                    here = slice(i * size, (i + 1) * size)
                    at = (places_ref, sequence, column, start + i)
                    store_block(*at, out_ref, lanes, attended[here])
                    store_block(*at, log_ref, lanes, log_total[here])


def attention_backward_kernel(
    places_ref,
    lengths_ref,
    in_ref,
    grad_ref,
    log_ref,
    out_ref,
    q_ref,
    k_ref,
    v_ref,
    g_ref,
    log_rows_ref,
    dk_ref,
    dv_ref,
):
    sequence = pl.program_id(0)
    heads = in_ref.shape[-1] // (3 * HEAD)
    for column, size, runs in attention_steps():
        length = lengths_ref[sequence, column]
        for head in range(heads):
            columns = [
                slice((third * heads + head) * HEAD, (third * heads + head + 1) * HEAD)
                for third in range(3)
            ]
            lanes = slice(head * HEAD, (head + 1) * HEAD)
            for block in range(4):
                at = (places_ref, sequence, column, block)
                load_block(*at, in_ref, columns[0], q_ref, block * size)
                load_block(*at, in_ref, columns[1], k_ref, block * size)
                load_block(*at, in_ref, columns[2], v_ref, block * size)
                load_block(*at, grad_ref, lanes, g_ref, block * size)
                load_block(*at, log_ref, lanes, log_rows_ref, block * size)
            dk_ref[...] = jnp.zeros_like(dk_ref)
            dv_ref[...] = jnp.zeros_like(dv_ref)
            for start, step, keys in runs:
                rows = slice(start * size, (start + step) * size)
                queries, grads = q_ref[rows], g_ref[rows]
                scores = scores_of(queries, k_ref[:keys], start * size, length)
                probs = jnp.exp(scores - log_rows_ref[rows, :1])
                grad_probs = contract_last(grads, v_ref[:keys])
                delta = jnp.sum(probs * grad_probs, axis=-1, keepdims=True)
                grad_scores = (probs * (grad_probs - delta)).astype(BF16)
                dv_ref[:keys] += contract_first(probs.astype(BF16), grads)
                dk_ref[:keys] += contract_first(grad_scores, queries)
                dq = jnp.dot(grad_scores, k_ref[:keys], preferred_element_type=F32) * SCALE
                dq = dq.astype(BF16)
                for i in range(step):
                    at = (places_ref, sequence, column, start + i)
                    store_block(*at, out_ref, columns[0], dq[i * size : (i + 1) * size])
            for block in range(4):
                here = slice(block * size, (block + 1) * size)
                at = (places_ref, sequence, column, block)
                store_block(*at, out_ref, columns[1], (dk_ref[here] * SCALE).astype(BF16))
                store_block(*at, out_ref, columns[2], dv_ref[here].astype(BF16))


def attention_call(kernel, arrays, outs, scratch, places, lengths, matmuls):
    count = 4 * BLK_A
    half = arrays[0].shape[0] // 16

    def spec(columns):
        return pl.BlockSpec((16, half, columns), lambda s, *_: (0, 0, 0))

    heads = arrays[0].shape[1] // (3 * HEAD)
    results = pl.pallas_call(
        kernel,
        grid_spec=pltpu.PrefetchScalarGridSpec(
            num_scalar_prefetch=2,
            grid=(2,),
            in_specs=[spec(a.shape[1]) for a in arrays],
            out_specs=[spec(columns) for columns, _ in outs],
            scratch_shapes=[pltpu.VMEM((count, HEAD), dtype) for dtype in scratch],
        ),
        out_shape=[jax.ShapeDtypeStruct((16, half, c), dtype) for c, dtype in outs],
        compiler_params=pltpu.CompilerParams(vmem_limit_bytes=48 * 2**20),
        cost_estimate=pl.CostEstimate(
            flops=matmuls * 2 * heads * count * count * HEAD * 2,
            bytes_accessed=16 * half * HEAD * heads * 2 * 4,
            transcendentals=2 * heads * count * count,
        ),
    )(places, lengths, *[a.reshape(16, half, -1) for a in arrays])
    return [r.reshape(16 * half, -1) for r in results]


def hidden_call(second_all, up_full, bias, grad_activated):
    count, width = second_all.shape
    units = up_full.shape[1]
    step, lanes = 256, 256

    def kernel(second_ref, up_ref, bias_ref, grad_ref, activated_ref, hidden_ref):
        second = second_ref[...]
        for first in range(0, units, lanes):
            at = slice(first, first + lanes)
            value = jnp.dot(second, up_ref[:, at], preferred_element_type=F32) + bias_ref[:, at]
            activated, slope = gelu(value)
            activated_ref[:, at] = activated.astype(BF16)
            hidden_ref[:, at] = (grad_ref[:, at] * slope).astype(BF16)

    def rows(columns):
        return pl.BlockSpec((step, columns), lambda i: (i, 0))

    def whole(*shape):
        return pl.BlockSpec(shape, lambda i: (0, 0))

    return pl.pallas_call(
        kernel,
        grid=(count // step,),
        in_specs=[rows(width), whole(width, units), whole(1, units), rows(units)],
        out_specs=[rows(units)] * 2,
        out_shape=[jax.ShapeDtypeStruct((count, units), BF16)] * 2,
        compiler_params=pltpu.CompilerParams(vmem_limit_bytes=40 * 2**20),
        cost_estimate=pl.CostEstimate(
            flops=2 * count * width * units,
            bytes_accessed=2 * count * width + 2 * width * units + 8 * count * units,
            transcendentals=count * units,
        ),
    )(second_all, up_full, bias.reshape(1, units), grad_activated)


def body(
    hidden_in,
    cotangent,
    seq_lengths,
    block_order,
    w_qkv,
    w_out,
    w_up,
    w_down,
    norm_gains,
    norm_biases,
    hidden_bias,
):
    blk, dp = lax.axis_size("blk"), lax.axis_size("dp")
    lanes = dp // 2
    b, d = lax.axis_index("blk"), lax.axis_index("dp")
    z, y = d // 2, d % 2
    rows, width = hidden_in.shape[2:]
    pairs = width // HEAD // blk // 2
    part = pairs * HEAD
    half = rows // 2
    shard = w_qkv.shape[0]
    units = w_down.shape[0]
    x = hidden_in.reshape(rows, width).astype(F32)
    cot_low = cotangent.reshape(rows, width)

    qkv_cut = (3, blk, pairs, HEAD)
    up_cut = (1, blk, lanes, units)

    pieces = [[p for p in range(dp) if (p * shard // HEAD) % 2 == to_y] for to_y in range(2)]
    route = [(pieces[to_y][lane], lane * 2 + to_y) for to_y in range(2) for lane in range(lanes)]

    near = [(core, far) for core in range(2) for far in range(2)]
    holders = jnp.stack(
        [jnp.take(block_order, b ^ (far * 2 + core), axis=1) for core, far in near], axis=1
    )
    found = holders[:, None, :] == jnp.arange(4, dtype=jnp.int32)[None, :, None]
    tables = jnp.array(
        [[[core * 8 + t[s][far] for core, far in near] for t in (TOPS, BOTTOMS)] for s in range(2)],
        jnp.int32,
    )
    places = jnp.sum(jnp.where(found[None, :, None], tables[:, None, :, None], 0), axis=-1)
    places = places.reshape(2, 2, 8)

    gate = [seq_lengths]

    def seal(*values):
        gate[0], values = lax.optimization_barrier((gate[0], values))
        return values if len(values) > 1 else values[0]

    def enter(*values):
        values = lax.optimization_barrier((values, gate[0]))[0]
        return values if len(values) > 1 else values[0]

    def rows_of(array, first, last):
        return array[first * half : last * half]

    def times(left, right):
        return jnp.dot(left, right, preferred_element_type=F32)

    normed, first_pull = jax.vjp(layer_norm, x, norm_gains[0], norm_biases[0])
    normed_low = normed.astype(BF16)
    qkv_pair = lax.all_to_all(split_columns(w_qkv, *qkv_cut), "blk", 0, 0)
    qkv_pair, normed_low, up_pair, out_piece = seal(
        qkv_pair, normed_low, split_columns(w_up, *up_cut), lax.ppermute(w_out, "dp", route)
    )

    normed_low, qkv_pair, up_pair = enter(normed_low, qkv_pair, up_pair)
    qkv_part = join_y(qkv_pair[:, 1], flip_y(qkv_pair[:, 0])).reshape(blk, 2 * shard, 3 * part)
    qkv_full = gather_z(qkv_part, 1).reshape(width, 3 * part)
    down_full = gather_z(after(w_down, qkv_part), 0)
    a_x, a_y, a_core, _ = seal(
        flip_x(normed_low), flip_y(normed_low), flip_core(normed_low), qkv_part
    )

    normed_low, a_x, a_y, a_core = enter(normed_low, a_x, a_y, a_core)
    a_across = diagonal_of(a_x, a_y)
    a_others = a_core, flip_core(a_x), flip_core(a_y)
    normed_all = assemble([normed_low, a_x, a_y, *a_others], MOST)
    a_across, normed_all = seal(a_across, normed_all)

    cot_low, normed_all, a_across = enter(cot_low, normed_all, a_across)
    cot_x, cot_y, cot_core = flip_x(cot_low), flip_y(cot_low), flip_core(cot_low)
    normed_all = assemble([*a_across, *[flip_core(piece) for piece in a_across]], REST, normed_all)
    out_full = jnp.broadcast_to(enter(out_piece)[None], (lanes, *out_piece.shape))
    out_full = lax.all_to_all(out_full, "dp", 0, 0, axis_index_groups=lines())
    cot_x, cot_y, cot_core, normed_all, qkv_full, out_full = seal(
        cot_x, cot_y, cot_core, normed_all, qkv_full, out_full
    )
    out_full = out_full.reshape(part, width)

    cot_x, cot_y, cot_core, normed_all = enter(cot_x, cot_y, cot_core, normed_all)
    cot_across = diagonal_of(cot_x, cot_y)
    cot_others = cot_core, flip_core(cot_x), flip_core(cot_y)
    projected = times(normed_all, qkv_full).astype(BF16)
    cot_across, cot_others, projected, lengths = seal(
        cot_across, cot_others, projected, flip_y(enter(seq_lengths))
    )
    lengths = jnp.concatenate([seq_lengths, lengths], axis=0)

    projected, up_pair, cot_across = enter(projected, up_pair, cot_across)
    up_pair = lax.all_to_all(up_pair, "blk", 0, 0)
    attended_low, log_total = attention_call(
        attention_forward_kernel,
        [projected],
        [(part, BF16), (part, F32)],
        [BF16] * 3,
        places,
        lengths,
        2,
    )
    cot_others = [*cot_others, *[flip_core(piece) for piece in cot_across]]
    attended_low, up_pair, cot_others = seal(attended_low, up_pair, cot_others)
    up_pair = enter(up_pair)

    def start_sum(left, multiply, *beside):
        left = enter(left)
        far, near = [
            flip_core(multiply(rows_of(left, *run)).astype(BF16)) for run in ((12, 16), (8, 12))
        ]
        middle = far.shape[0] // 2
        to_x = (multiply(rows_of(left, 4, 6)) + far[:middle].astype(F32)).astype(BF16)
        to_y = (multiply(rows_of(left, 6, 8)) + far[middle:].astype(F32)).astype(BF16)
        to_x, to_y, near, beside = seal(to_x, to_y, near, beside)
        return enter(to_x), enter(to_y), near, beside

    to_x, to_y, near, (up_other,) = start_sum(
        attended_low, lambda v: times(v, out_full), flip_y(up_pair[:, 0])
    )
    up_part = join_y(*enter(up_pair[:, 1], up_other)).reshape(blk, 2 * shard, lanes * units)
    up_full = gather_z(after(up_part, qkv_full), 1).reshape(width, lanes * units)
    own = times(rows_of(enter(attended_low), 0, 4), out_full)
    cot_all = assemble(enter(*[cot_low, cot_x, cot_y, *cot_others[:3]]), MOST)
    cot_all = assemble(enter(*[*cot_across, *cot_others[3:]]), REST, cot_all)
    from_x, from_y, own, cot_all, down_full = seal(
        flip_x(to_x), flip_y(to_y), own, cot_all, down_full
    )
    sums = enter(own, near, from_x, from_y)
    to_x, to_y = last_sends(*sums)
    last_x, last_y, own = seal(flip_x(to_x), flip_y(to_y), own_rows(*after(sums, to_x, to_y)))
    mixed = x + add_last(*enter(own, last_x, last_y))
    second, second_pull = jax.vjp(layer_norm, mixed, norm_gains[1], norm_biases[1])
    second_low = seal(second.astype(BF16))

    def gather_rows(part_low, beside, also):
        part_low = enter(part_low)
        from_x, from_y, from_core = flip_x(part_low), flip_y(part_low), flip_core(part_low)
        from_x, from_y, from_core, beside = seal(from_x, from_y, from_core, beside())
        part_low, from_x, from_y, from_core = enter(part_low, from_x, from_y, from_core)
        across = diagonal_of(from_x, from_y)
        others = from_core, flip_core(from_x), flip_core(from_y)
        across, whole, also = seal(
            across, assemble([part_low, from_x, from_y, *others], MOST), also(beside)
        )
        across, whole = enter(across, whole)
        whole = assemble([*across, *[flip_core(piece) for piece in across]], REST, whole)
        return seal(whole), beside, also

    second_all, grad_activated, up_full = gather_rows(
        second_low, lambda: contract_last(enter(cot_all), down_full), lambda beside: up_full
    )
    bias_part = lax.dynamic_slice_in_dim(hidden_bias.reshape(blk, lanes, 2, units), b, 1, 0)
    bias_part = lax.dynamic_index_in_dim(bias_part, y, 2, keepdims=False).reshape(-1)
    activated_low, grad_hidden_low = seal(
        *hidden_call(enter(second_all), up_full, bias_part, grad_activated)
    )

    to_x, to_y, near, _ = start_sum(grad_hidden_low, lambda v: contract_last(v, up_full))
    down_term = contract_first(enter(activated_low), cot_all).astype(BF16)
    down_sum = scatter_z(down_term, 0)
    own = contract_last(rows_of(enter(grad_hidden_low), 0, 4), up_full)
    from_x, from_y, own, down_term = seal(flip_x(to_x), flip_y(to_y), own, down_term)
    sums = enter(own, near, from_x, from_y)
    to_x, to_y = last_sends(*sums)
    result_low = times(rows_of(enter(activated_low), 0, 8), down_full).astype(BF16)
    last_x, last_y, own, result_low = seal(
        flip_x(to_x), flip_y(to_y), own_rows(*after(sums, to_x, to_y)), result_low
    )
    grad_mixed_norm, gain_two, bias_two = second_pull(add_last(*enter(own, last_x, last_y)))
    grad_mixed = cot_low.astype(F32) + grad_mixed_norm
    mixed_low, gain_two, bias_two = seal(grad_mixed.astype(BF16), gain_two, bias_two)

    def beside_gather():
        up_term = contract_first(second_all, enter(grad_hidden_low)).astype(BF16)
        result_near = times(rows_of(enter(activated_low), 8, 12), down_full).astype(BF16)
        return up_term, result_near

    def beside_second(beside):
        far = times(rows_of(enter(activated_low), 12, 16), down_full).astype(BF16)
        return far, flip_core(enter(beside[1])), down_sum

    mixed_all, (up_term, _), (result_far, got_near, down_sum) = gather_rows(
        mixed_low, beside_gather, beside_second
    )
    up_sum = scatter_z(up_term.reshape(blk, -1, lanes * units), 1)
    mixed_all, result_far = enter(mixed_all, result_far)
    got_far, grad_attended = seal(
        flip_core(result_far), contract_last(mixed_all, out_full).astype(BF16)
    )
    got_far, grad_attended = enter(got_far, grad_attended)
    to_x = rows_of(result_low, 4, 6).astype(F32) + got_far[: 2 * half].astype(F32)
    to_y = rows_of(result_low, 6, 8).astype(F32) + got_far[2 * half :].astype(F32)
    to_x, to_y = to_x.astype(BF16), to_y.astype(BF16)
    from_x, from_y = flip_x(to_x), flip_y(to_y)
    grad_attended = after(grad_attended, to_x, to_y)
    (grad_projected,) = attention_call(
        attention_backward_kernel,
        [projected, grad_attended, log_total],
        [(3 * part, BF16)],
        [BF16] * 4 + [F32] * 3,
        places,
        lengths,
        5,
    )
    qkv_term = contract_first(normed_all, grad_projected).astype(BF16)
    from_x, from_y, grad_projected, qkv_term = seal(from_x, from_y, grad_projected, qkv_term)

    def split_sum(total):
        parts = total.reshape(blk, 2, shard, -1)
        other = flip_y(lax.dynamic_index_in_dim(parts, 1 - y, 1, keepdims=False))
        return lax.dynamic_index_in_dim(parts, y, 1, keepdims=False), other

    qkv_sum = scatter_z(qkv_term.reshape(blk, -1, 3 * part), 1)
    result_sums = enter(rows_of(result_low, 0, 4), got_near, from_x, from_y)
    to_x, to_y = last_sends(*result_sums)
    left = after(grad_projected, to_x, to_y)
    far, near = [
        contract_last(rows_of(left, *run), qkv_full).astype(BF16) for run in ((12, 16), (8, 12))
    ]
    far, near, last_x, last_y = seal(far, near, flip_x(to_x), flip_y(to_y))
    left, far, near = enter(grad_projected, far, near)
    far, near = flip_core(far), flip_core(near)
    up_pair = split_sum(enter(up_sum))
    to_x = contract_last(rows_of(left, 4, 6), qkv_full) + far[: 2 * half].astype(F32)
    to_y = contract_last(rows_of(left, 6, 8), qkv_full) + far[2 * half :].astype(F32)
    to_x, to_y, up_pair = seal(to_x.astype(BF16), to_y.astype(BF16), up_pair)
    to_x, to_y = enter(to_x, to_y)
    hidden_sum = jnp.sum(enter(grad_hidden_low).astype(F32), axis=0)
    own = contract_last(rows_of(enter(grad_projected), 0, 4), qkv_full)
    result = mixed + add_last(own_rows(*enter(*result_sums)), last_x, last_y)
    out_term = contract_first(enter(attended_low), mixed_all).astype(BF16)
    from_x, from_y, own, result, out_term, hidden_sum = seal(
        flip_x(to_x), flip_y(to_y), own, result, out_term, hidden_sum
    )
    sums = enter(own, near, from_x, from_y)
    to_x, to_y = last_sends(*sums)
    last_x, last_y, own, qkv_sum = seal(
        flip_x(to_x), flip_y(to_y), own_rows(*after(sums, to_x, to_y)), qkv_sum
    )

    grad_input_norm, gain_one, bias_one = first_pull(add_last(*enter(own, last_x, last_y)))
    grad_input = (grad_mixed + grad_input_norm).astype(BF16)
    up_got = exchange(*enter(*up_pair))
    qkv_pair = split_sum(enter(qkv_sum))
    up_got, qkv_pair, gain_one, bias_one, grad_input, result = seal(
        up_got, qkv_pair, gain_one, bias_one, grad_input, result.astype(BF16)
    )

    norms = sum_blk(enter(jnp.stack([gain_one, gain_two, bias_one, bias_two])))
    qkv_got = exchange(*enter(*qkv_pair))
    out_sum = scatter_z(after(out_term, qkv_sum), 0)
    grad_up = merge_columns(enter(up_got), *up_cut)
    norms, qkv_got, grad_up = seal(norms, qkv_got, grad_up)
    norms, hidden_sum = sum_dp(enter(norms), hidden_sum)
    grad_qkv = merge_columns(enter(qkv_got), *qkv_cut)
    out_sum = after(out_sum, norms)
    grad_out = lax.ppermute(out_sum, "dp", [(j, i) for i, j in route]).astype(F32)
    return (
        result.reshape(1, 1, rows, width),
        grad_input.reshape(1, 1, rows, width),
        grad_qkv,
        grad_out,
        grad_up,
        down_sum.astype(F32),
        norms[:2],
        norms[2:],
        hidden_sum,
    )


def solution(mesh):
    return jax.shard_map(
        body,
        mesh=mesh,
        in_specs=(
            P("dp", "blk", None, None),
            P("dp", "blk", None, None),
            P("dp", None),
            P(),
            P(("blk", "dp"), None),
            P(("blk", "dp"), None),
            P(("blk", "dp"), None),
            P(("blk", "dp"), None),
            P(),
            P(),
            P(),
        ),
        out_specs=(
            P("dp", "blk", None, None),
            P("dp", "blk", None, None),
            P(("blk", "dp"), None),
            P(("blk", "dp"), None),
            P(("blk", "dp"), None),
            P(("blk", "dp"), None),
            P(None, ("blk", "dp")),
            P(None, ("blk", "dp")),
            P(("blk", "dp")),
        ),
        check_vma=False,
    )
```

```python
import jax
import jax.numpy as jnp
from jax import lax
from jax.experimental import pallas as pl
from jax.experimental.pallas import tpu as pltpu
from jax.sharding import PartitionSpec as P

HEAD = 128
BLK_A = 256
BLK_B = 64
SPLITS = ((0, BLK_A), (BLK_A, BLK_A + BLK_B))
BLOCK_HALF = (BLK_A + BLK_B) // 2

EPSILON = 1e-05
NEGATIVE = -1e30
SCALE = HEAD ** (-0.5)
BF16 = jnp.bfloat16
F32 = jnp.float32


def after(value, *others):
    return lax.optimization_barrier((value, others))[0]


def layer_norm(value, gain, bias):
    center = value - jnp.mean(value, axis=-1, keepdims=True)
    spread = jnp.mean(center * center, axis=-1, keepdims=True)
    return center * lax.rsqrt(spread + EPSILON) * gain + bias


def gelu(v):
    rate = (2.0 / 3.141592653589793) ** 0.5
    squared = v * v
    bend = jnp.tanh(rate * v * (1.0 + 0.044715 * squared))
    rise = 0.5 * (1.0 + bend)
    slope = rise + 0.5 * v * (1.0 - bend * bend) * rate * (1.0 + 3 * 0.044715 * squared)
    return v * rise, slope


def contract_last(left, right):
    return lax.dot_general(
        left, right, (((1,), (1,)), ((), ())), preferred_element_type=F32
    )


def contract_first(left, right):
    return lax.dot_general(
        left, right, (((0,), (0,)), ((), ())), preferred_element_type=F32
    )


def flip(axis, bits, block):
    count = lax.axis_size(axis)
    return lax.ppermute(block, axis, [(i ^ bits, i) for i in range(count)])


def flip_core(block):
    return flip("blk", 1, block)


def flip_x(block):
    return flip("blk", 2, block)


def flip_y(block):
    return flip("dp", 1, block)


def lines():
    count = lax.axis_size("dp")
    return [[z * 2 + y for z in range(count // 2)] for y in range(2)]


def gather_z(part, axis):
    return lax.all_gather(part, "dp", axis_index_groups=lines(), axis=axis, tiled=True)


def scatter_z(total, axis):
    return lax.psum_scatter(
        total, "dp", axis_index_groups=lines(), scatter_dimension=axis, tiled=True
    )


def column(groups, blk, runs, width, group, b, run, y):
    return (((group * blk + b) * runs + run) * 2 + y) * width


def split_columns(shard, groups, blk, runs, width):
    rows = shard.shape[0]
    count = groups * runs * width

    def kernel(y_ref, in_ref, out_ref):
        b = pl.program_id(1)
        y = jnp.where(pl.program_id(0) == 0, 1 - y_ref[0], y_ref[0])
        for group in range(groups):
            for run in range(runs):
                start = column(groups, blk, runs, width, group, b, run, y)
                to = (group * runs + run) * width
                out_ref[0, 0, :, to : to + width] = in_ref[:, pl.ds(pl.multiple_of(start, 128), width)]

    return pl.pallas_call(
        kernel,
        grid_spec=pltpu.PrefetchScalarGridSpec(
            num_scalar_prefetch=1,
            grid=(2, blk),
            in_specs=[pl.BlockSpec(shard.shape, lambda i, j, *_: (0, 0))],
            out_specs=pl.BlockSpec((1, 1, rows, count), lambda i, j, *_: (j, i, 0, 0)),
        ),
        out_shape=jax.ShapeDtypeStruct((blk, 2, rows, count), shard.dtype),
        compiler_params=pltpu.CompilerParams(vmem_limit_bytes=16 * 2**20),
        cost_estimate=pl.CostEstimate(flops=0, bytes_accessed=4 * shard.size, transcendentals=0),
    )((lax.axis_index("dp") % 2).reshape(1), shard)


def join_y(own, other):
    blk, rows, count = own.shape

    def kernel(y_ref, own_ref, other_ref, out_ref):
        out_ref[0, y_ref[0]] = own_ref[0]
        out_ref[0, 1 - y_ref[0]] = other_ref[0]

    piece = pl.BlockSpec((1, rows, count), lambda i, *_: (i, 0, 0))
    return pl.pallas_call(
        kernel,
        grid_spec=pltpu.PrefetchScalarGridSpec(
            num_scalar_prefetch=1,
            grid=(blk,),
            in_specs=[piece, piece],
            out_specs=pl.BlockSpec((1, 2, rows, count), lambda i, *_: (i, 0, 0, 0)),
        ),
        out_shape=jax.ShapeDtypeStruct((blk, 2, rows, count), own.dtype),
        compiler_params=pltpu.CompilerParams(vmem_limit_bytes=16 * 2**20),
        cost_estimate=pl.CostEstimate(flops=0, bytes_accessed=8 * own.size, transcendentals=0),
    )((lax.axis_index("dp") % 2).reshape(1), own, other)


def merge_columns(parts, groups, blk, runs, width):
    _, _, rows, count = parts.shape

    def kernel(in_ref, out_ref):
        b = pl.program_id(0)
        for y in range(2):
            for group in range(groups):
                for run in range(runs):
                    start = column(groups, blk, runs, width, group, b, run, y)
                    at = (group * runs + run) * width
                    out_ref[:, pl.ds(pl.multiple_of(start, 128), width)] = in_ref[
                        0, y, :, at : at + width
                    ].astype(F32)

    return pl.pallas_call(
        kernel,
        grid=(blk,),
        in_specs=[pl.BlockSpec((1, 2, rows, count), lambda i: (i, 0, 0, 0))],
        out_specs=pl.BlockSpec((rows, blk * 2 * count), lambda i: (0, 0)),
        out_shape=jax.ShapeDtypeStruct((rows, blk * 2 * count), F32),
        compiler_params=pltpu.CompilerParams(vmem_limit_bytes=16 * 2**20),
        cost_estimate=pl.CostEstimate(flops=0, bytes_accessed=6 * parts.size, transcendentals=0),
    )(parts)


def exchange(own, other):
    return lax.all_to_all(join_y(own, other), "blk", 0, 0)


TOPS = ((0, 5), (3, 4))
BOTTOMS = ((1, 2), (7, 6))


MOST = ((0, 0, 2, 0), (1, 0, 1, 5), (1, 1, 1, 2), (2, 0, 1, 3), (2, 1, 1, 7))
REST = ((0, 0, 1, 4), (1, 0, 1, 6))


def diagonal_of(from_x, from_y):
    half = from_x.shape[0] // 2
    return flip_y(from_x[:half]), flip_x(from_y[half:])


def assemble(pieces, runs, whole=None):
    half = BLOCK_HALF
    columns = pieces[0].shape[1]
    side_pieces = len(pieces) // 2
    copies, total = [], 0
    for side in range(2):
        for piece, start, count, to in runs:
            copies.append(
                (side * side_pieces + piece, start * half, count * half, (side * 8 + to) * half, total)
            )
            total += count * half

    def kernel(*refs):
        out_ref, held_ref, in_sems, out_sems = refs[-4:]
        reads, writes = [], []
        for i, (piece, start, count, to, at) in enumerate(copies):
            there = held_ref.at[pl.ds(at, count)]
            source = refs[piece].at[pl.ds(start, count)]
            reads.append(pltpu.make_async_copy(source, there, in_sems.at[i]))
            writes.append(pltpu.make_async_copy(there, out_ref.at[pl.ds(to, count)], out_sems.at[i]))
        for read in reads:
            read.start()
        for read, write in zip(reads, writes):
            read.wait()
            write.start()
        for write in writes:
            write.wait()

    inputs = [*pieces] if whole is None else [*pieces, whole]
    return pl.pallas_call(
        kernel,
        in_specs=[pl.BlockSpec(memory_space=pl.ANY)] * len(inputs),
        out_specs=pl.BlockSpec(memory_space=pltpu.HBM),
        out_shape=jax.ShapeDtypeStruct((16 * half, columns), pieces[0].dtype),
        input_output_aliases={} if whole is None else {len(inputs) - 1: 0},
        scratch_shapes=[pltpu.VMEM((total, columns), pieces[0].dtype)]
        + [pltpu.SemaphoreType.DMA((len(copies),))] * 2,
        compiler_params=pltpu.CompilerParams(vmem_limit_bytes=56 * 2**20),
        cost_estimate=pl.CostEstimate(flops=0, bytes_accessed=4 * total * columns, transcendentals=0),
    )(*inputs)


def last_sends(near, got, from_x, from_y):
    half = near.shape[0] // 4
    to_x = near[2 * half : 3 * half].astype(F32) + got[2 * half : 3 * half].astype(F32)
    to_y = near[3 * half :].astype(F32) + got[3 * half :].astype(F32)
    to_x = (to_x + from_y[:half].astype(F32)).astype(BF16)
    to_y = (to_y + from_x[:half].astype(F32)).astype(BF16)
    return to_x, to_y


def own_rows(near, got, from_x, from_y):
    half = near.shape[0] // 4
    own = near[: 2 * half].astype(F32) + got[: 2 * half].astype(F32)
    return own + jnp.concatenate([from_x[half:], from_y[half:]], axis=0).astype(F32)


def add_last(own, last_x, last_y):
    return own + jnp.concatenate([last_y, last_x], axis=0).astype(F32)


def sum_blk(norms):
    blk, b = lax.axis_size("blk"), lax.axis_index("blk")
    norms = norms + flip_core(norms)
    for bits in range(2, blk, 2):
        norms = norms + flip("blk", bits, norms)
    return lax.dynamic_slice_in_dim(norms, b * (norms.shape[1] // blk), norms.shape[1] // blk, 1)


def sum_dp(parts, hidden):
    dp, d = lax.axis_size("dp"), lax.axis_index("dp")
    count, columns = parts.shape
    parts = parts + flip_y(parts)
    both = jnp.concatenate([parts.reshape(-1), hidden])
    bits = 2
    while bits < dp:
        both = both + flip("dp", bits, both)
        bits *= 2
    units = hidden.shape[0] // (dp // 2)
    parts, hidden = both[: count * columns].reshape(count, columns), both[count * columns :]
    return (
        lax.dynamic_slice_in_dim(parts, d * (columns // dp), columns // dp, 1),
        lax.dynamic_slice_in_dim(hidden, (d // 2) * units, units),
    )


def runs_of(places_ref, sequence, column, block, half):
    first, last = SPLITS[column]
    if first < half:
        top = min(last, half)
        yield places_ref[sequence, column, block], slice(first, top), slice(0, top - first)
    if last > half:
        start = max(first, half)
        yield (
            places_ref[sequence, column, 4 + block],
            slice(start - half, last - half),
            slice(start - first, last - first),
        )


def load_block(places_ref, sequence, column, block, ref, lanes, to_ref, row):
    for which, here, there in runs_of(places_ref, sequence, column, block, ref.shape[1]):
        to_ref[row + there.start : row + there.stop] = ref[which, here, lanes]


def store_block(places_ref, sequence, column, block, ref, lanes, value):
    for which, here, there in runs_of(places_ref, sequence, column, block, ref.shape[1]):
        ref[which, here, lanes] = value[there]


def scores_of(queries, keys, first, length):
    scores = contract_last(queries, keys) * SCALE
    key_places = lax.broadcasted_iota(jnp.int32, scores.shape, 1)
    query_places = first + lax.broadcasted_iota(jnp.int32, scores.shape, 0)
    allowed = (key_places <= query_places) & (key_places < length)
    return jnp.where(allowed, scores, NEGATIVE)


def attention_steps():
    for column, (first, last) in enumerate(SPLITS):
        size = last - first
        step = 1 if size * 4 > 512 else 4
        yield column, size, [(p, step, (p + step) * size) for p in range(0, 4, step)]


def attention_forward_kernel(places_ref, lengths_ref, in_ref, out_ref, log_ref, q_ref, k_ref, v_ref):
    sequence = pl.program_id(0)
    heads = in_ref.shape[-1] // (3 * HEAD)
    for column, size, runs in attention_steps():
        length = lengths_ref[sequence, column]
        for head in range(heads):
            for third, ref in enumerate((q_ref, k_ref, v_ref)):
                lanes = slice((third * heads + head) * HEAD, (third * heads + head + 1) * HEAD)
                for block in range(4):
                    load_block(places_ref, sequence, column, block, in_ref, lanes, ref, block * size)
            lanes = slice(head * HEAD, (head + 1) * HEAD)
            for start, step, keys in runs:
                rows = slice(start * size, (start + step) * size)
                scores = scores_of(q_ref[rows], k_ref[:keys], start * size, length)
                peak = jnp.max(scores, axis=-1, keepdims=True)
                weights = jnp.exp(scores - peak)
                total = jnp.sum(weights, axis=-1, keepdims=True)
                attended = jnp.dot(weights.astype(BF16), v_ref[:keys], preferred_element_type=F32)
                attended = (attended / total).astype(BF16)
                log_total = jnp.broadcast_to(peak + jnp.log(total), (step * size, HEAD))
                for i in range(step):
                    here = slice(i * size, (i + 1) * size)
                    at = (places_ref, sequence, column, start + i)
                    store_block(*at, out_ref, lanes, attended[here])
                    store_block(*at, log_ref, lanes, log_total[here])


def attention_backward_kernel(
    places_ref,
    lengths_ref,
    in_ref,
    grad_ref,
    log_ref,
    out_ref,
    q_ref,
    k_ref,
    v_ref,
    g_ref,
    log_rows_ref,
    dk_ref,
    dv_ref,
):
    sequence = pl.program_id(0)
    heads = in_ref.shape[-1] // (3 * HEAD)
    for column, size, runs in attention_steps():
        length = lengths_ref[sequence, column]
        for head in range(heads):
            columns = [
                slice((third * heads + head) * HEAD, (third * heads + head + 1) * HEAD)
                for third in range(3)
            ]
            lanes = slice(head * HEAD, (head + 1) * HEAD)
            for block in range(4):
                at = (places_ref, sequence, column, block)
                load_block(*at, in_ref, columns[0], q_ref, block * size)
                load_block(*at, in_ref, columns[1], k_ref, block * size)
                load_block(*at, in_ref, columns[2], v_ref, block * size)
                load_block(*at, grad_ref, lanes, g_ref, block * size)
                load_block(*at, log_ref, lanes, log_rows_ref, block * size)
            dk_ref[...] = jnp.zeros_like(dk_ref)
            dv_ref[...] = jnp.zeros_like(dv_ref)
            for start, step, keys in runs:
                rows = slice(start * size, (start + step) * size)
                queries, grads = q_ref[rows], g_ref[rows]
                scores = scores_of(queries, k_ref[:keys], start * size, length)
                probs = jnp.exp(scores - log_rows_ref[rows, :1])
                grad_probs = contract_last(grads, v_ref[:keys])
                delta = jnp.sum(probs * grad_probs, axis=-1, keepdims=True)
                grad_scores = (probs * (grad_probs - delta)).astype(BF16)
                dv_ref[:keys] += contract_first(probs.astype(BF16), grads)
                dk_ref[:keys] += contract_first(grad_scores, queries)
                dq = jnp.dot(grad_scores, k_ref[:keys], preferred_element_type=F32) * SCALE
                dq = dq.astype(BF16)
                for i in range(step):
                    at = (places_ref, sequence, column, start + i)
                    store_block(*at, out_ref, columns[0], dq[i * size : (i + 1) * size])
            for block in range(4):
                here = slice(block * size, (block + 1) * size)
                at = (places_ref, sequence, column, block)
                store_block(*at, out_ref, columns[1], (dk_ref[here] * SCALE).astype(BF16))
                store_block(*at, out_ref, columns[2], dv_ref[here].astype(BF16))


def attention_call(kernel, arrays, outs, scratch, places, lengths, matmuls):
    count = 4 * BLK_A
    half = arrays[0].shape[0] // 16

    def spec(columns):
        return pl.BlockSpec((16, half, columns), lambda s, *_: (0, 0, 0))

    heads = arrays[0].shape[1] // (3 * HEAD)
    results = pl.pallas_call(
        kernel,
        grid_spec=pltpu.PrefetchScalarGridSpec(
            num_scalar_prefetch=2,
            grid=(2,),
            in_specs=[spec(a.shape[1]) for a in arrays],
            out_specs=[spec(columns) for columns, _ in outs],
            scratch_shapes=[pltpu.VMEM((count, HEAD), dtype) for dtype in scratch],
        ),
        out_shape=[jax.ShapeDtypeStruct((16, half, c), dtype) for c, dtype in outs],
        compiler_params=pltpu.CompilerParams(vmem_limit_bytes=48 * 2**20),
        cost_estimate=pl.CostEstimate(
            flops=matmuls * 2 * heads * count * count * HEAD * 2,
            bytes_accessed=16 * half * HEAD * heads * 2 * 4,
            transcendentals=2 * heads * count * count,
        ),
    )(places, lengths, *[a.reshape(16, half, -1) for a in arrays])
    return [r.reshape(16 * half, -1) for r in results]


def hidden_call(second_all, up_full, bias, grad_activated):
    count, width = second_all.shape
    units = up_full.shape[1]
    step, lanes = 256, 256

    def kernel(second_ref, up_ref, bias_ref, grad_ref, activated_ref, hidden_ref):
        second = second_ref[...]
        for first in range(0, units, lanes):
            at = slice(first, first + lanes)
            value = jnp.dot(second, up_ref[:, at], preferred_element_type=F32) + bias_ref[:, at]
            activated, slope = gelu(value)
            activated_ref[:, at] = activated.astype(BF16)
            hidden_ref[:, at] = (grad_ref[:, at] * slope).astype(BF16)

    def rows(columns):
        return pl.BlockSpec((step, columns), lambda i: (i, 0))

    def whole(*shape):
        return pl.BlockSpec(shape, lambda i: (0, 0))

    return pl.pallas_call(
        kernel,
        grid=(count // step,),
        in_specs=[rows(width), whole(width, units), whole(1, units), rows(units)],
        out_specs=[rows(units)] * 2,
        out_shape=[jax.ShapeDtypeStruct((count, units), BF16)] * 2,
        compiler_params=pltpu.CompilerParams(vmem_limit_bytes=40 * 2**20),
        cost_estimate=pl.CostEstimate(
            flops=2 * count * width * units,
            bytes_accessed=2 * count * width + 2 * width * units + 8 * count * units,
            transcendentals=count * units,
        ),
    )(second_all, up_full, bias.reshape(1, units), grad_activated)


def body(
    hidden_in,
    cotangent,
    seq_lengths,
    block_order,
    w_qkv,
    w_out,
    w_up,
    w_down,
    norm_gains,
    norm_biases,
    hidden_bias,
):
    blk, dp = lax.axis_size("blk"), lax.axis_size("dp")
    lanes = dp // 2
    b, d = lax.axis_index("blk"), lax.axis_index("dp")
    z, y = d // 2, d % 2
    rows, width = hidden_in.shape[2:]
    pairs = width // HEAD // blk // 2
    part = pairs * HEAD
    half = rows // 2
    shard = w_qkv.shape[0]
    units = w_down.shape[0]
    x = hidden_in.reshape(rows, width).astype(F32)
    cot_low = cotangent.reshape(rows, width)

    qkv_cut = (3, blk, pairs, HEAD)
    up_cut = (1, blk, lanes, units)

    pieces = [[p for p in range(dp) if (p * shard // HEAD) % 2 == to_y] for to_y in range(2)]
    route = [(pieces[to_y][lane], lane * 2 + to_y) for to_y in range(2) for lane in range(lanes)]

    near = [(core, far) for core in range(2) for far in range(2)]
    holders = jnp.stack(
        [jnp.take(block_order, b ^ (far * 2 + core), axis=1) for core, far in near], axis=1
    )
    found = holders[:, None, :] == jnp.arange(4, dtype=jnp.int32)[None, :, None]
    tables = jnp.array(
        [[[core * 8 + t[s][far] for core, far in near] for t in (TOPS, BOTTOMS)] for s in range(2)],
        jnp.int32,
    )
    places = jnp.sum(jnp.where(found[None, :, None], tables[:, None, :, None], 0), axis=-1)
    places = places.reshape(2, 2, 8)

    gate = [seq_lengths]

    def seal(*values):
        gate[0], values = lax.optimization_barrier((gate[0], values))
        return values if len(values) > 1 else values[0]

    def enter(*values):
        values = lax.optimization_barrier((values, gate[0]))[0]
        return values if len(values) > 1 else values[0]

    def rows_of(array, first, last):
        return array[first * half : last * half]

    def times(left, right):
        return jnp.dot(left, right, preferred_element_type=F32)

    normed, first_pull = jax.vjp(layer_norm, x, norm_gains[0], norm_biases[0])
    normed_low = normed.astype(BF16)
    qkv_pair = lax.all_to_all(split_columns(w_qkv, *qkv_cut), "blk", 0, 0)
    qkv_pair, normed_low, up_pair, out_piece = seal(
        qkv_pair, normed_low, split_columns(w_up, *up_cut), lax.ppermute(w_out, "dp", route)
    )

    normed_low, qkv_pair, up_pair = enter(normed_low, qkv_pair, up_pair)
    qkv_part = join_y(qkv_pair[:, 1], flip_y(qkv_pair[:, 0])).reshape(blk, 2 * shard, 3 * part)
    qkv_full = gather_z(qkv_part, 1).reshape(width, 3 * part)
    down_full = gather_z(after(w_down, qkv_part), 0)
    a_x, a_y, a_core, _ = seal(
        flip_x(normed_low), flip_y(normed_low), flip_core(normed_low), qkv_part
    )

    normed_low, a_x, a_y, a_core = enter(normed_low, a_x, a_y, a_core)
    a_across = diagonal_of(a_x, a_y)
    a_others = a_core, flip_core(a_x), flip_core(a_y)
    normed_all = assemble([normed_low, a_x, a_y, *a_others], MOST)
    a_across, normed_all = seal(a_across, normed_all)

    cot_low, normed_all, a_across = enter(cot_low, normed_all, a_across)
    cot_x, cot_y, cot_core = flip_x(cot_low), flip_y(cot_low), flip_core(cot_low)
    normed_all = assemble([*a_across, *[flip_core(piece) for piece in a_across]], REST, normed_all)
    out_full = jnp.broadcast_to(enter(out_piece)[None], (lanes, *out_piece.shape))
    out_full = lax.all_to_all(out_full, "dp", 0, 0, axis_index_groups=lines())
    cot_x, cot_y, cot_core, normed_all, qkv_full, out_full = seal(
        cot_x, cot_y, cot_core, normed_all, qkv_full, out_full
    )
    out_full = out_full.reshape(part, width)

    cot_x, cot_y, cot_core, normed_all = enter(cot_x, cot_y, cot_core, normed_all)
    cot_across = diagonal_of(cot_x, cot_y)
    cot_others = cot_core, flip_core(cot_x), flip_core(cot_y)
    projected = times(normed_all, qkv_full).astype(BF16)
    cot_across, cot_others, projected, lengths = seal(
        cot_across, cot_others, projected, flip_y(enter(seq_lengths))
    )
    lengths = jnp.concatenate([seq_lengths, lengths], axis=0)

    projected, up_pair, cot_across = enter(projected, up_pair, cot_across)
    up_pair = lax.all_to_all(up_pair, "blk", 0, 0)
    attended_low, log_total = attention_call(
        attention_forward_kernel,
        [projected],
        [(part, BF16), (part, F32)],
        [BF16] * 3,
        places,
        lengths,
        2,
    )
    cot_others = [*cot_others, *[flip_core(piece) for piece in cot_across]]
    attended_low, up_pair, cot_others = seal(attended_low, up_pair, cot_others)
    up_pair = enter(up_pair)

    def start_sum(left, multiply, *beside):
        left = enter(left)
        far, near = [
            flip_core(multiply(rows_of(left, *run)).astype(BF16)) for run in ((12, 16), (8, 12))
        ]
        middle = far.shape[0] // 2
        to_x = (multiply(rows_of(left, 4, 6)) + far[:middle].astype(F32)).astype(BF16)
        to_y = (multiply(rows_of(left, 6, 8)) + far[middle:].astype(F32)).astype(BF16)
        to_x, to_y, near, beside = seal(to_x, to_y, near, beside)
        return enter(to_x), enter(to_y), near, beside

    to_x, to_y, near, (up_other,) = start_sum(
        attended_low, lambda v: times(v, out_full), flip_y(up_pair[:, 0])
    )
    up_part = join_y(*enter(up_pair[:, 1], up_other)).reshape(blk, 2 * shard, lanes * units)
    up_full = gather_z(after(up_part, qkv_full), 1).reshape(width, lanes * units)
    own = times(rows_of(enter(attended_low), 0, 4), out_full)
    cot_all = assemble(enter(*[cot_low, cot_x, cot_y, *cot_others[:3]]), MOST)
    cot_all = assemble(enter(*[*cot_across, *cot_others[3:]]), REST, cot_all)
    from_x, from_y, own, cot_all, down_full = seal(
        flip_x(to_x), flip_y(to_y), own, cot_all, down_full
    )
    sums = enter(own, near, from_x, from_y)
    to_x, to_y = last_sends(*sums)
    last_x, last_y, own = seal(flip_x(to_x), flip_y(to_y), own_rows(*after(sums, to_x, to_y)))
    mixed = x + add_last(*enter(own, last_x, last_y))
    second, second_pull = jax.vjp(layer_norm, mixed, norm_gains[1], norm_biases[1])
    second_low = seal(second.astype(BF16))

    def gather_rows(part_low, beside, also):
        part_low = enter(part_low)
        from_x, from_y, from_core = flip_x(part_low), flip_y(part_low), flip_core(part_low)
        from_x, from_y, from_core, beside = seal(from_x, from_y, from_core, beside())
        part_low, from_x, from_y, from_core = enter(part_low, from_x, from_y, from_core)
        across = diagonal_of(from_x, from_y)
        others = from_core, flip_core(from_x), flip_core(from_y)
        across, whole, also = seal(
            across, assemble([part_low, from_x, from_y, *others], MOST), also(beside)
        )
        across, whole = enter(across, whole)
        whole = assemble([*across, *[flip_core(piece) for piece in across]], REST, whole)
        return seal(whole), beside, also

    second_all, grad_activated, up_full = gather_rows(
        second_low, lambda: contract_last(enter(cot_all), down_full), lambda beside: up_full
    )
    bias_part = lax.dynamic_slice_in_dim(hidden_bias.reshape(blk, lanes, 2, units), b, 1, 0)
    bias_part = lax.dynamic_index_in_dim(bias_part, y, 2, keepdims=False).reshape(-1)
    activated_low, grad_hidden_low = seal(
        *hidden_call(enter(second_all), up_full, bias_part, grad_activated)
    )

    to_x, to_y, near, _ = start_sum(grad_hidden_low, lambda v: contract_last(v, up_full))
    down_term = contract_first(enter(activated_low), cot_all).astype(BF16)
    down_sum = scatter_z(down_term, 0)
    own = contract_last(rows_of(enter(grad_hidden_low), 0, 4), up_full)
    from_x, from_y, own, down_term = seal(flip_x(to_x), flip_y(to_y), own, down_term)
    sums = enter(own, near, from_x, from_y)
    to_x, to_y = last_sends(*sums)
    result_low = times(rows_of(enter(activated_low), 0, 8), down_full).astype(BF16)
    last_x, last_y, own, result_low = seal(
        flip_x(to_x), flip_y(to_y), own_rows(*after(sums, to_x, to_y)), result_low
    )
    grad_mixed_norm, gain_two, bias_two = second_pull(add_last(*enter(own, last_x, last_y)))
    grad_mixed = cot_low.astype(F32) + grad_mixed_norm
    mixed_low, gain_two, bias_two = seal(grad_mixed.astype(BF16), gain_two, bias_two)

    def beside_gather():
        up_term = contract_first(second_all, enter(grad_hidden_low)).astype(BF16)
        result_near = times(rows_of(enter(activated_low), 8, 12), down_full).astype(BF16)
        return up_term, result_near

    def beside_second(beside):
        far = times(rows_of(enter(activated_low), 12, 16), down_full).astype(BF16)
        return far, flip_core(enter(beside[1])), down_sum

    mixed_all, (up_term, _), (result_far, got_near, down_sum) = gather_rows(
        mixed_low, beside_gather, beside_second
    )
    up_sum = scatter_z(up_term.reshape(blk, -1, lanes * units), 1)
    mixed_all, result_far = enter(mixed_all, result_far)
    got_far, grad_attended = seal(
        flip_core(result_far), contract_last(mixed_all, out_full).astype(BF16)
    )
    got_far, grad_attended = enter(got_far, grad_attended)
    to_x = rows_of(result_low, 4, 6).astype(F32) + got_far[: 2 * half].astype(F32)
    to_y = rows_of(result_low, 6, 8).astype(F32) + got_far[2 * half :].astype(F32)
    to_x, to_y = to_x.astype(BF16), to_y.astype(BF16)
    from_x, from_y = flip_x(to_x), flip_y(to_y)
    grad_attended = after(grad_attended, to_x, to_y)
    (grad_projected,) = attention_call(
        attention_backward_kernel,
        [projected, grad_attended, log_total],
        [(3 * part, BF16)],
        [BF16] * 4 + [F32] * 3,
        places,
        lengths,
        5,
    )
    qkv_term = contract_first(normed_all, grad_projected).astype(BF16)
    from_x, from_y, grad_projected, qkv_term = seal(from_x, from_y, grad_projected, qkv_term)

    def split_sum(total):
        parts = total.reshape(blk, 2, shard, -1)
        other = flip_y(lax.dynamic_index_in_dim(parts, 1 - y, 1, keepdims=False))
        return lax.dynamic_index_in_dim(parts, y, 1, keepdims=False), other

    qkv_sum = scatter_z(qkv_term.reshape(blk, -1, 3 * part), 1)
    result_sums = enter(rows_of(result_low, 0, 4), got_near, from_x, from_y)
    to_x, to_y = last_sends(*result_sums)
    left = after(grad_projected, to_x, to_y)
    far, near = [
        contract_last(rows_of(left, *run), qkv_full).astype(BF16) for run in ((12, 16), (8, 12))
    ]
    far, near, last_x, last_y = seal(far, near, flip_x(to_x), flip_y(to_y))
    left, far, near = enter(grad_projected, far, near)
    far, near = flip_core(far), flip_core(near)
    up_pair = split_sum(enter(up_sum))
    to_x = contract_last(rows_of(left, 4, 6), qkv_full) + far[: 2 * half].astype(F32)
    to_y = contract_last(rows_of(left, 6, 8), qkv_full) + far[2 * half :].astype(F32)
    to_x, to_y, up_pair = seal(to_x.astype(BF16), to_y.astype(BF16), up_pair)
    to_x, to_y = enter(to_x, to_y)
    hidden_sum = jnp.sum(enter(grad_hidden_low).astype(F32), axis=0)
    own = contract_last(rows_of(enter(grad_projected), 0, 4), qkv_full)
    result = mixed + add_last(own_rows(*enter(*result_sums)), last_x, last_y)
    out_term = contract_first(enter(attended_low), mixed_all).astype(BF16)
    from_x, from_y, own, result, out_term, hidden_sum = seal(
        flip_x(to_x), flip_y(to_y), own, result, out_term, hidden_sum
    )
    sums = enter(own, near, from_x, from_y)
    to_x, to_y = last_sends(*sums)
    last_x, last_y, own, qkv_sum = seal(
        flip_x(to_x), flip_y(to_y), own_rows(*after(sums, to_x, to_y)), qkv_sum
    )

    grad_input_norm, gain_one, bias_one = first_pull(add_last(*enter(own, last_x, last_y)))
    grad_input = (grad_mixed + grad_input_norm).astype(BF16)
    up_got = exchange(*enter(*up_pair))
    qkv_pair = split_sum(enter(qkv_sum))
    up_got, qkv_pair, gain_one, bias_one, grad_input, result = seal(
        up_got, qkv_pair, gain_one, bias_one, grad_input, result.astype(BF16)
    )

    norms = sum_blk(enter(jnp.stack([gain_one, gain_two, bias_one, bias_two])))
    qkv_got = exchange(*enter(*qkv_pair))
    out_sum = scatter_z(after(out_term, qkv_sum), 0)
    grad_up = merge_columns(enter(up_got), *up_cut)
    norms, hidden_sum = sum_dp(norms, hidden_sum)
    grad_qkv = merge_columns(qkv_got, *qkv_cut)
    out_sum = after(out_sum, norms)
    grad_out = lax.ppermute(out_sum, "dp", [(j, i) for i, j in route]).astype(F32)
    return (
        result.reshape(1, 1, rows, width),
        grad_input.reshape(1, 1, rows, width),
        grad_qkv,
        grad_out,
        grad_up,
        down_sum.astype(F32),
        norms[:2],
        norms[2:],
        hidden_sum,
    )


def solution(mesh):
    return jax.shard_map(
        body,
        mesh=mesh,
        in_specs=(
            P("dp", "blk", None, None),
            P("dp", "blk", None, None),
            P("dp", None),
            P(),
            P(("blk", "dp"), None),
            P(("blk", "dp"), None),
            P(("blk", "dp"), None),
            P(("blk", "dp"), None),
            P(),
            P(),
            P(),
        ),
        out_specs=(
            P("dp", "blk", None, None),
            P("dp", "blk", None, None),
            P(("blk", "dp"), None),
            P(("blk", "dp"), None),
            P(("blk", "dp"), None),
            P(("blk", "dp"), None),
            P(None, ("blk", "dp")),
            P(None, ("blk", "dp")),
            P(("blk", "dp")),
        ),
        check_vma=False,
    )
```

```python
import jax
import jax.numpy as jnp
from jax import lax
from jax.experimental import pallas as pl
from jax.experimental.pallas import tpu as pltpu
from jax.sharding import PartitionSpec as P

HEAD = 128
BLK_A = 256
BLK_B = 64
SPLITS = ((0, BLK_A), (BLK_A, BLK_A + BLK_B))
BLOCK_HALF = (BLK_A + BLK_B) // 2

EPSILON = 1e-05
NEGATIVE = -1e30
SCALE = HEAD ** (-0.5)
BF16 = jnp.bfloat16
F32 = jnp.float32


def after(value, *others):
    return lax.optimization_barrier((value, others))[0]


def layer_norm(value, gain, bias):
    center = value - jnp.mean(value, axis=-1, keepdims=True)
    spread = jnp.mean(center * center, axis=-1, keepdims=True)
    return center * lax.rsqrt(spread + EPSILON) * gain + bias


def gelu(v):
    rate = (2.0 / 3.141592653589793) ** 0.5
    squared = v * v
    bend = jnp.tanh(rate * v * (1.0 + 0.044715 * squared))
    rise = 0.5 * (1.0 + bend)
    slope = rise + 0.5 * v * (1.0 - bend * bend) * rate * (1.0 + 3 * 0.044715 * squared)
    return v * rise, slope


def contract_last(left, right):
    return lax.dot_general(
        left, right, (((1,), (1,)), ((), ())), preferred_element_type=F32
    )


def contract_first(left, right):
    return lax.dot_general(
        left, right, (((0,), (0,)), ((), ())), preferred_element_type=F32
    )


def flip(axis, bits, block):
    count = lax.axis_size(axis)
    return lax.ppermute(block, axis, [(i ^ bits, i) for i in range(count)])


def flip_core(block):
    return flip("blk", 1, block)


def flip_x(block):
    return flip("blk", 2, block)


def flip_y(block):
    return flip("dp", 1, block)


def lines():
    count = lax.axis_size("dp")
    return [[z * 2 + y for z in range(count // 2)] for y in range(2)]


def gather_z(part, axis):
    return lax.all_gather(part, "dp", axis_index_groups=lines(), axis=axis, tiled=True)


def scatter_z(total, axis):
    return lax.psum_scatter(
        total, "dp", axis_index_groups=lines(), scatter_dimension=axis, tiled=True
    )


def column(groups, blk, runs, width, group, b, run, y):
    return (((group * blk + b) * runs + run) * 2 + y) * width


def split_columns(shard, groups, blk, runs, width):
    rows = shard.shape[0]
    count = groups * runs * width

    def kernel(y_ref, in_ref, out_ref):
        b = pl.program_id(1)
        y = jnp.where(pl.program_id(0) == 0, 1 - y_ref[0], y_ref[0])
        for group in range(groups):
            for run in range(runs):
                start = column(groups, blk, runs, width, group, b, run, y)
                to = (group * runs + run) * width
                out_ref[0, 0, :, to : to + width] = in_ref[:, pl.ds(pl.multiple_of(start, 128), width)]

    return pl.pallas_call(
        kernel,
        grid_spec=pltpu.PrefetchScalarGridSpec(
            num_scalar_prefetch=1,
            grid=(2, blk),
            in_specs=[pl.BlockSpec(shard.shape, lambda i, j, *_: (0, 0))],
            out_specs=pl.BlockSpec((1, 1, rows, count), lambda i, j, *_: (j, i, 0, 0)),
        ),
        out_shape=jax.ShapeDtypeStruct((blk, 2, rows, count), shard.dtype),
        compiler_params=pltpu.CompilerParams(vmem_limit_bytes=16 * 2**20),
        cost_estimate=pl.CostEstimate(flops=0, bytes_accessed=4 * shard.size, transcendentals=0),
    )((lax.axis_index("dp") % 2).reshape(1), shard)


def join_y(own, other):
    blk, rows, count = own.shape

    def kernel(y_ref, own_ref, other_ref, out_ref):
        out_ref[0, y_ref[0]] = own_ref[0]
        out_ref[0, 1 - y_ref[0]] = other_ref[0]

    piece = pl.BlockSpec((1, rows, count), lambda i, *_: (i, 0, 0))
    return pl.pallas_call(
        kernel,
        grid_spec=pltpu.PrefetchScalarGridSpec(
            num_scalar_prefetch=1,
            grid=(blk,),
            in_specs=[piece, piece],
            out_specs=pl.BlockSpec((1, 2, rows, count), lambda i, *_: (i, 0, 0, 0)),
        ),
        out_shape=jax.ShapeDtypeStruct((blk, 2, rows, count), own.dtype),
        compiler_params=pltpu.CompilerParams(vmem_limit_bytes=16 * 2**20),
        cost_estimate=pl.CostEstimate(flops=0, bytes_accessed=8 * own.size, transcendentals=0),
    )((lax.axis_index("dp") % 2).reshape(1), own, other)


def merge_columns(parts, groups, blk, runs, width):
    _, _, rows, count = parts.shape

    def kernel(in_ref, out_ref):
        b = pl.program_id(0)
        for y in range(2):
            for group in range(groups):
                for run in range(runs):
                    start = column(groups, blk, runs, width, group, b, run, y)
                    at = (group * runs + run) * width
                    out_ref[:, pl.ds(pl.multiple_of(start, 128), width)] = in_ref[
                        0, y, :, at : at + width
                    ].astype(F32)

    return pl.pallas_call(
        kernel,
        grid=(blk,),
        in_specs=[pl.BlockSpec((1, 2, rows, count), lambda i: (i, 0, 0, 0))],
        out_specs=pl.BlockSpec((rows, blk * 2 * count), lambda i: (0, 0)),
        out_shape=jax.ShapeDtypeStruct((rows, blk * 2 * count), F32),
        compiler_params=pltpu.CompilerParams(vmem_limit_bytes=16 * 2**20),
        cost_estimate=pl.CostEstimate(flops=0, bytes_accessed=6 * parts.size, transcendentals=0),
    )(parts)


def exchange(own, other):
    return lax.all_to_all(join_y(own, other), "blk", 0, 0)


TOPS = ((0, 5), (3, 4))
BOTTOMS = ((1, 2), (7, 6))


MOST = ((0, 0, 2, 0), (1, 0, 1, 5), (1, 1, 1, 2), (2, 0, 1, 3), (2, 1, 1, 7))
REST = ((0, 0, 1, 4), (1, 0, 1, 6))


def diagonal_of(from_x, from_y):
    half = from_x.shape[0] // 2
    return flip_y(from_x[:half]), flip_x(from_y[half:])


def assemble(pieces, runs, whole=None):
    half = BLOCK_HALF
    columns = pieces[0].shape[1]
    side_pieces = len(pieces) // 2
    copies, total = [], 0
    for side in range(2):
        for piece, start, count, to in runs:
            copies.append(
                (side * side_pieces + piece, start * half, count * half, (side * 8 + to) * half, total)
            )
            total += count * half

    def kernel(*refs):
        out_ref, held_ref, in_sems, out_sems = refs[-4:]
        reads, writes = [], []
        for i, (piece, start, count, to, at) in enumerate(copies):
            there = held_ref.at[pl.ds(at, count)]
            source = refs[piece].at[pl.ds(start, count)]
            reads.append(pltpu.make_async_copy(source, there, in_sems.at[i]))
            writes.append(pltpu.make_async_copy(there, out_ref.at[pl.ds(to, count)], out_sems.at[i]))
        for read in reads:
            read.start()
        for read, write in zip(reads, writes):
            read.wait()
            write.start()
        for write in writes:
            write.wait()

    inputs = [*pieces] if whole is None else [*pieces, whole]
    return pl.pallas_call(
        kernel,
        in_specs=[pl.BlockSpec(memory_space=pl.ANY)] * len(inputs),
        out_specs=pl.BlockSpec(memory_space=pltpu.HBM),
        out_shape=jax.ShapeDtypeStruct((16 * half, columns), pieces[0].dtype),
        input_output_aliases={} if whole is None else {len(inputs) - 1: 0},
        scratch_shapes=[pltpu.VMEM((total, columns), pieces[0].dtype)]
        + [pltpu.SemaphoreType.DMA((len(copies),))] * 2,
        compiler_params=pltpu.CompilerParams(vmem_limit_bytes=56 * 2**20),
        cost_estimate=pl.CostEstimate(flops=0, bytes_accessed=4 * total * columns, transcendentals=0),
    )(*inputs)


def last_sends(near, got, from_x, from_y):
    half = near.shape[0] // 4
    to_x = near[2 * half : 3 * half].astype(F32) + got[2 * half : 3 * half].astype(F32)
    to_y = near[3 * half :].astype(F32) + got[3 * half :].astype(F32)
    to_x = (to_x + from_y[:half].astype(F32)).astype(BF16)
    to_y = (to_y + from_x[:half].astype(F32)).astype(BF16)
    return to_x, to_y


def own_rows(near, got, from_x, from_y):
    half = near.shape[0] // 4
    own = near[: 2 * half].astype(F32) + got[: 2 * half].astype(F32)
    return own + jnp.concatenate([from_x[half:], from_y[half:]], axis=0).astype(F32)


def add_last(own, last_x, last_y):
    return own + jnp.concatenate([last_y, last_x], axis=0).astype(F32)


def sum_blk(norms):
    blk, b = lax.axis_size("blk"), lax.axis_index("blk")
    norms = norms + flip_core(norms)
    for bits in range(2, blk, 2):
        norms = norms + flip("blk", bits, norms)
    return lax.dynamic_slice_in_dim(norms, b * (norms.shape[1] // blk), norms.shape[1] // blk, 1)


def sum_dp(parts, hidden):
    dp, d = lax.axis_size("dp"), lax.axis_index("dp")
    count, columns = parts.shape
    parts = parts + flip_y(parts)
    both = jnp.concatenate([parts.reshape(-1), hidden])
    bits = 2
    while bits < dp:
        both = both + flip("dp", bits, both)
        bits *= 2
    units = hidden.shape[0] // (dp // 2)
    parts, hidden = both[: count * columns].reshape(count, columns), both[count * columns :]
    return (
        lax.dynamic_slice_in_dim(parts, d * (columns // dp), columns // dp, 1),
        lax.dynamic_slice_in_dim(hidden, (d // 2) * units, units),
    )


def runs_of(places_ref, sequence, column, block, half):
    first, last = SPLITS[column]
    if first < half:
        top = min(last, half)
        yield places_ref[sequence, column, block], slice(first, top), slice(0, top - first)
    if last > half:
        start = max(first, half)
        yield (
            places_ref[sequence, column, 4 + block],
            slice(start - half, last - half),
            slice(start - first, last - first),
        )


def load_block(places_ref, sequence, column, block, ref, lanes, to_ref, row):
    for which, here, there in runs_of(places_ref, sequence, column, block, ref.shape[1]):
        to_ref[row + there.start : row + there.stop] = ref[which, here, lanes]


def store_block(places_ref, sequence, column, block, ref, lanes, value):
    for which, here, there in runs_of(places_ref, sequence, column, block, ref.shape[1]):
        ref[which, here, lanes] = value[there]


def scores_of(queries, keys, first, length):
    scores = contract_last(queries, keys) * SCALE
    key_places = lax.broadcasted_iota(jnp.int32, scores.shape, 1)
    query_places = first + lax.broadcasted_iota(jnp.int32, scores.shape, 0)
    allowed = (key_places <= query_places) & (key_places < length)
    return jnp.where(allowed, scores, NEGATIVE)


def attention_steps():
    for column, (first, last) in enumerate(SPLITS):
        size = last - first
        step = 1 if size * 4 > 512 else 4
        yield column, size, [(p, step, (p + step) * size) for p in range(0, 4, step)]


def attention_forward_kernel(places_ref, lengths_ref, in_ref, out_ref, log_ref, q_ref, k_ref, v_ref):
    sequence = pl.program_id(0)
    heads = in_ref.shape[-1] // (3 * HEAD)
    for column, size, runs in attention_steps():
        length = lengths_ref[sequence, column]
        for head in range(heads):
            for third, ref in enumerate((q_ref, k_ref, v_ref)):
                lanes = slice((third * heads + head) * HEAD, (third * heads + head + 1) * HEAD)
                for block in range(4):
                    load_block(places_ref, sequence, column, block, in_ref, lanes, ref, block * size)
            lanes = slice(head * HEAD, (head + 1) * HEAD)
            for start, step, keys in runs:
                rows = slice(start * size, (start + step) * size)
                scores = scores_of(q_ref[rows], k_ref[:keys], start * size, length)
                peak = jnp.max(scores, axis=-1, keepdims=True)
                weights = jnp.exp(scores - peak)
                total = jnp.sum(weights, axis=-1, keepdims=True)
                attended = jnp.dot(weights.astype(BF16), v_ref[:keys], preferred_element_type=F32)
                attended = (attended / total).astype(BF16)
                log_total = jnp.broadcast_to(peak + jnp.log(total), (step * size, HEAD))
                for i in range(step):
                    here = slice(i * size, (i + 1) * size)
                    at = (places_ref, sequence, column, start + i)
                    store_block(*at, out_ref, lanes, attended[here])
                    store_block(*at, log_ref, lanes, log_total[here])


def attention_backward_kernel(
    places_ref,
    lengths_ref,
    in_ref,
    grad_ref,
    log_ref,
    out_ref,
    q_ref,
    k_ref,
    v_ref,
    g_ref,
    log_rows_ref,
    dk_ref,
    dv_ref,
):
    sequence = pl.program_id(0)
    heads = in_ref.shape[-1] // (3 * HEAD)
    for column, size, runs in attention_steps():
        length = lengths_ref[sequence, column]
        for head in range(heads):
            columns = [
                slice((third * heads + head) * HEAD, (third * heads + head + 1) * HEAD)
                for third in range(3)
            ]
            lanes = slice(head * HEAD, (head + 1) * HEAD)
            for block in range(4):
                at = (places_ref, sequence, column, block)
                load_block(*at, in_ref, columns[0], q_ref, block * size)
                load_block(*at, in_ref, columns[1], k_ref, block * size)
                load_block(*at, in_ref, columns[2], v_ref, block * size)
                load_block(*at, grad_ref, lanes, g_ref, block * size)
                load_block(*at, log_ref, lanes, log_rows_ref, block * size)
            dk_ref[...] = jnp.zeros_like(dk_ref)
            dv_ref[...] = jnp.zeros_like(dv_ref)
            for start, step, keys in runs:
                rows = slice(start * size, (start + step) * size)
                queries, grads = q_ref[rows], g_ref[rows]
                scores = scores_of(queries, k_ref[:keys], start * size, length)
                probs = jnp.exp(scores - log_rows_ref[rows, :1])
                grad_probs = contract_last(grads, v_ref[:keys])
                delta = jnp.sum(probs * grad_probs, axis=-1, keepdims=True)
                grad_scores = (probs * (grad_probs - delta)).astype(BF16)
                dv_ref[:keys] += contract_first(probs.astype(BF16), grads)
                dk_ref[:keys] += contract_first(grad_scores, queries)
                dq = jnp.dot(grad_scores, k_ref[:keys], preferred_element_type=F32) * SCALE
                dq = dq.astype(BF16)
                for i in range(step):
                    at = (places_ref, sequence, column, start + i)
                    store_block(*at, out_ref, columns[0], dq[i * size : (i + 1) * size])
            for block in range(4):
                here = slice(block * size, (block + 1) * size)
                at = (places_ref, sequence, column, block)
                store_block(*at, out_ref, columns[1], (dk_ref[here] * SCALE).astype(BF16))
                store_block(*at, out_ref, columns[2], dv_ref[here].astype(BF16))


def attention_call(kernel, arrays, outs, scratch, places, lengths, matmuls):
    count = 4 * BLK_A
    half = arrays[0].shape[0] // 16

    def spec(columns):
        return pl.BlockSpec((16, half, columns), lambda s, *_: (0, 0, 0))

    heads = arrays[0].shape[1] // (3 * HEAD)
    results = pl.pallas_call(
        kernel,
        grid_spec=pltpu.PrefetchScalarGridSpec(
            num_scalar_prefetch=2,
            grid=(2,),
            in_specs=[spec(a.shape[1]) for a in arrays],
            out_specs=[spec(columns) for columns, _ in outs],
            scratch_shapes=[pltpu.VMEM((count, HEAD), dtype) for dtype in scratch],
        ),
        out_shape=[jax.ShapeDtypeStruct((16, half, c), dtype) for c, dtype in outs],
        compiler_params=pltpu.CompilerParams(vmem_limit_bytes=48 * 2**20),
        cost_estimate=pl.CostEstimate(
            flops=matmuls * 2 * heads * count * count * HEAD * 2,
            bytes_accessed=16 * half * HEAD * heads * 2 * 4,
            transcendentals=2 * heads * count * count,
        ),
    )(places, lengths, *[a.reshape(16, half, -1) for a in arrays])
    return [r.reshape(16 * half, -1) for r in results]


def hidden_call(second_all, up_full, bias, grad_activated):
    count, width = second_all.shape
    units = up_full.shape[1]
    step, lanes = 256, 256

    def kernel(second_ref, up_ref, bias_ref, grad_ref, activated_ref, hidden_ref):
        second = second_ref[...]
        for first in range(0, units, lanes):
            at = slice(first, first + lanes)
            value = jnp.dot(second, up_ref[:, at], preferred_element_type=F32) + bias_ref[:, at]
            activated, slope = gelu(value)
            activated_ref[:, at] = activated.astype(BF16)
            hidden_ref[:, at] = (grad_ref[:, at] * slope).astype(BF16)

    def rows(columns):
        return pl.BlockSpec((step, columns), lambda i: (i, 0))

    def whole(*shape):
        return pl.BlockSpec(shape, lambda i: (0, 0))

    return pl.pallas_call(
        kernel,
        grid=(count // step,),
        in_specs=[rows(width), whole(width, units), whole(1, units), rows(units)],
        out_specs=[rows(units)] * 2,
        out_shape=[jax.ShapeDtypeStruct((count, units), BF16)] * 2,
        compiler_params=pltpu.CompilerParams(vmem_limit_bytes=40 * 2**20),
        cost_estimate=pl.CostEstimate(
            flops=2 * count * width * units,
            bytes_accessed=2 * count * width + 2 * width * units + 8 * count * units,
            transcendentals=count * units,
        ),
    )(second_all, up_full, bias.reshape(1, units), grad_activated)


def body(
    hidden_in,
    cotangent,
    seq_lengths,
    block_order,
    w_qkv,
    w_out,
    w_up,
    w_down,
    norm_gains,
    norm_biases,
    hidden_bias,
):
    blk, dp = lax.axis_size("blk"), lax.axis_size("dp")
    lanes = dp // 2
    b, d = lax.axis_index("blk"), lax.axis_index("dp")
    z, y = d // 2, d % 2
    rows, width = hidden_in.shape[2:]
    pairs = width // HEAD // blk // 2
    part = pairs * HEAD
    half = rows // 2
    shard = w_qkv.shape[0]
    units = w_down.shape[0]
    x = hidden_in.reshape(rows, width).astype(F32)
    cot_low = cotangent.reshape(rows, width)

    qkv_cut = (3, blk, pairs, HEAD)
    up_cut = (1, blk, lanes, units)

    pieces = [[p for p in range(dp) if (p * shard // HEAD) % 2 == to_y] for to_y in range(2)]
    route = [(pieces[to_y][lane], lane * 2 + to_y) for to_y in range(2) for lane in range(lanes)]

    near = [(core, far) for core in range(2) for far in range(2)]
    holders = jnp.stack(
        [jnp.take(block_order, b ^ (far * 2 + core), axis=1) for core, far in near], axis=1
    )
    found = holders[:, None, :] == jnp.arange(4, dtype=jnp.int32)[None, :, None]
    tables = jnp.array(
        [[[core * 8 + t[s][far] for core, far in near] for t in (TOPS, BOTTOMS)] for s in range(2)],
        jnp.int32,
    )
    places = jnp.sum(jnp.where(found[None, :, None], tables[:, None, :, None], 0), axis=-1)
    places = places.reshape(2, 2, 8)

    gate = [seq_lengths]

    def seal(*values):
        gate[0], values = lax.optimization_barrier((gate[0], values))
        return values if len(values) > 1 else values[0]

    def enter(*values):
        values = lax.optimization_barrier((values, gate[0]))[0]
        return values if len(values) > 1 else values[0]

    def rows_of(array, first, last):
        return array[first * half : last * half]

    def times(left, right):
        return jnp.dot(left, right, preferred_element_type=F32)

    normed, first_pull = jax.vjp(layer_norm, x, norm_gains[0], norm_biases[0])
    normed_low = normed.astype(BF16)
    qkv_pair = lax.all_to_all(split_columns(w_qkv, *qkv_cut), "blk", 0, 0)
    qkv_pair, normed_low, up_pair, out_piece = seal(
        qkv_pair, normed_low, split_columns(w_up, *up_cut), lax.ppermute(w_out, "dp", route)
    )

    normed_low, qkv_pair, up_pair = enter(normed_low, qkv_pair, up_pair)
    qkv_part = join_y(qkv_pair[:, 1], flip_y(qkv_pair[:, 0])).reshape(blk, 2 * shard, 3 * part)
    qkv_full = gather_z(qkv_part, 1).reshape(width, 3 * part)
    down_full = gather_z(after(w_down, qkv_part), 0)
    a_x, a_y, a_core, _ = seal(
        flip_x(normed_low), flip_y(normed_low), flip_core(normed_low), qkv_part
    )

    normed_low, a_x, a_y, a_core = enter(normed_low, a_x, a_y, a_core)
    a_across = diagonal_of(a_x, a_y)
    a_others = a_core, flip_core(a_x), flip_core(a_y)
    normed_all = assemble([normed_low, a_x, a_y, *a_others], MOST)
    a_across, normed_all = seal(a_across, normed_all)

    cot_low, normed_all, a_across = enter(cot_low, normed_all, a_across)
    cot_x, cot_y, cot_core = flip_x(cot_low), flip_y(cot_low), flip_core(cot_low)
    normed_all = assemble([*a_across, *[flip_core(piece) for piece in a_across]], REST, normed_all)
    out_full = jnp.broadcast_to(enter(out_piece)[None], (lanes, *out_piece.shape))
    out_full = lax.all_to_all(out_full, "dp", 0, 0, axis_index_groups=lines())
    cot_x, cot_y, cot_core, normed_all, qkv_full, out_full = seal(
        cot_x, cot_y, cot_core, normed_all, qkv_full, out_full
    )
    out_full = out_full.reshape(part, width)

    cot_x, cot_y, cot_core, normed_all = enter(cot_x, cot_y, cot_core, normed_all)
    cot_across = diagonal_of(cot_x, cot_y)
    cot_others = cot_core, flip_core(cot_x), flip_core(cot_y)
    projected = times(normed_all, qkv_full).astype(BF16)
    up_pair = enter(up_pair)
    cot_across, cot_others, projected, up_other, lengths = seal(
        cot_across, cot_others, projected, flip_y(up_pair[:, 0]), flip_y(enter(seq_lengths))
    )
    lengths = jnp.concatenate([seq_lengths, lengths], axis=0)

    projected, up_own, up_other, cot_across = enter(projected, up_pair[:, 1], up_other, cot_across)
    up_part = exchange(up_own, up_other).reshape(blk, 2 * shard, lanes * units)
    up_full = gather_z(after(up_part, qkv_full), 1).reshape(width, lanes * units)
    attended_low, log_total = attention_call(
        attention_forward_kernel,
        [projected],
        [(part, BF16), (part, F32)],
        [BF16] * 3,
        places,
        lengths,
        2,
    )
    cot_others = [*cot_others, *[flip_core(piece) for piece in cot_across]]
    attended_low, up_part, cot_others = seal(attended_low, up_part, cot_others)

    def start_sum(left, multiply, *beside):
        left = enter(left)
        far, near = [
            flip_core(multiply(rows_of(left, *run)).astype(BF16)) for run in ((12, 16), (8, 12))
        ]
        middle = far.shape[0] // 2
        to_x = (multiply(rows_of(left, 4, 6)) + far[:middle].astype(F32)).astype(BF16)
        to_y = (multiply(rows_of(left, 6, 8)) + far[middle:].astype(F32)).astype(BF16)
        to_x, to_y, near, beside = seal(to_x, to_y, near, beside)
        return enter(to_x), enter(to_y), near, beside

    to_x, to_y, near, _ = start_sum(attended_low, lambda v: times(v, out_full))
    own = times(rows_of(enter(attended_low), 0, 4), out_full)
    cot_all = assemble(enter(*[cot_low, cot_x, cot_y, *cot_others[:3]]), MOST)
    cot_all = assemble(enter(*[*cot_across, *cot_others[3:]]), REST, cot_all)
    from_x, from_y, own, cot_all, down_full = seal(
        flip_x(to_x), flip_y(to_y), own, cot_all, down_full
    )
    sums = enter(own, near, from_x, from_y)
    to_x, to_y = last_sends(*sums)
    last_x, last_y, own = seal(flip_x(to_x), flip_y(to_y), own_rows(*after(sums, to_x, to_y)))
    mixed = x + add_last(*enter(own, last_x, last_y))
    second, second_pull = jax.vjp(layer_norm, mixed, norm_gains[1], norm_biases[1])
    second_low = seal(second.astype(BF16))

    def gather_rows(part_low, beside, also):
        part_low = enter(part_low)
        from_x, from_y, from_core = flip_x(part_low), flip_y(part_low), flip_core(part_low)
        from_x, from_y, from_core, beside = seal(from_x, from_y, from_core, beside())
        part_low, from_x, from_y, from_core = enter(part_low, from_x, from_y, from_core)
        across = diagonal_of(from_x, from_y)
        others = from_core, flip_core(from_x), flip_core(from_y)
        across, whole, also = seal(
            across, assemble([part_low, from_x, from_y, *others], MOST), also(beside)
        )
        across, whole = enter(across, whole)
        whole = assemble([*across, *[flip_core(piece) for piece in across]], REST, whole)
        return seal(whole), beside, also

    second_all, grad_activated, up_full = gather_rows(
        second_low, lambda: contract_last(enter(cot_all), down_full), lambda beside: up_full
    )
    bias_part = lax.dynamic_slice_in_dim(hidden_bias.reshape(blk, lanes, 2, units), b, 1, 0)
    bias_part = lax.dynamic_index_in_dim(bias_part, y, 2, keepdims=False).reshape(-1)
    activated_low, grad_hidden_low = seal(
        *hidden_call(enter(second_all), up_full, bias_part, grad_activated)
    )

    to_x, to_y, near, _ = start_sum(grad_hidden_low, lambda v: contract_last(v, up_full))
    down_term = contract_first(enter(activated_low), cot_all).astype(BF16)
    down_sum = scatter_z(down_term, 0)
    own = contract_last(rows_of(enter(grad_hidden_low), 0, 4), up_full)
    from_x, from_y, own, down_term = seal(flip_x(to_x), flip_y(to_y), own, down_term)
    sums = enter(own, near, from_x, from_y)
    to_x, to_y = last_sends(*sums)
    result_low = times(rows_of(enter(activated_low), 0, 8), down_full).astype(BF16)
    last_x, last_y, own, result_low = seal(
        flip_x(to_x), flip_y(to_y), own_rows(*after(sums, to_x, to_y)), result_low
    )
    grad_mixed_norm, gain_two, bias_two = second_pull(add_last(*enter(own, last_x, last_y)))
    grad_mixed = cot_low.astype(F32) + grad_mixed_norm
    mixed_low, gain_two, bias_two = seal(grad_mixed.astype(BF16), gain_two, bias_two)

    def beside_gather():
        up_term = contract_first(second_all, enter(grad_hidden_low)).astype(BF16)
        result_near = times(rows_of(enter(activated_low), 8, 12), down_full).astype(BF16)
        return up_term, result_near

    def beside_second(beside):
        far = times(rows_of(enter(activated_low), 12, 16), down_full).astype(BF16)
        return far, flip_core(enter(beside[1])), down_sum

    mixed_all, (up_term, _), (result_far, got_near, down_sum) = gather_rows(
        mixed_low, beside_gather, beside_second
    )
    up_sum = scatter_z(up_term.reshape(blk, -1, lanes * units), 1)
    mixed_all, result_far = enter(mixed_all, result_far)
    got_far, grad_attended = seal(
        flip_core(result_far), contract_last(mixed_all, out_full).astype(BF16)
    )
    got_far, grad_attended = enter(got_far, grad_attended)
    to_x = rows_of(result_low, 4, 6).astype(F32) + got_far[: 2 * half].astype(F32)
    to_y = rows_of(result_low, 6, 8).astype(F32) + got_far[2 * half :].astype(F32)
    to_x, to_y = to_x.astype(BF16), to_y.astype(BF16)
    from_x, from_y = flip_x(to_x), flip_y(to_y)
    grad_attended = after(grad_attended, to_x, to_y)
    (grad_projected,) = attention_call(
        attention_backward_kernel,
        [projected, grad_attended, log_total],
        [(3 * part, BF16)],
        [BF16] * 4 + [F32] * 3,
        places,
        lengths,
        5,
    )
    qkv_term = contract_first(normed_all, grad_projected).astype(BF16)
    from_x, from_y, grad_projected, qkv_term = seal(from_x, from_y, grad_projected, qkv_term)

    def split_sum(total):
        parts = total.reshape(blk, 2, shard, -1)
        other = flip_y(lax.dynamic_index_in_dim(parts, 1 - y, 1, keepdims=False))
        return lax.dynamic_index_in_dim(parts, y, 1, keepdims=False), other

    qkv_sum = scatter_z(qkv_term.reshape(blk, -1, 3 * part), 1)
    result_sums = enter(rows_of(result_low, 0, 4), got_near, from_x, from_y)
    to_x, to_y = last_sends(*result_sums)
    left = after(grad_projected, to_x, to_y)
    far, near = [
        contract_last(rows_of(left, *run), qkv_full).astype(BF16) for run in ((12, 16), (8, 12))
    ]
    far, near, last_x, last_y = seal(far, near, flip_x(to_x), flip_y(to_y))
    left, far, near = enter(grad_projected, far, near)
    far, near = flip_core(far), flip_core(near)
    up_pair = split_sum(enter(up_sum))
    to_x = contract_last(rows_of(left, 4, 6), qkv_full) + far[: 2 * half].astype(F32)
    to_y = contract_last(rows_of(left, 6, 8), qkv_full) + far[2 * half :].astype(F32)
    to_x, to_y, up_pair = seal(to_x.astype(BF16), to_y.astype(BF16), up_pair)
    to_x, to_y = enter(to_x, to_y)
    hidden_sum = jnp.sum(enter(grad_hidden_low).astype(F32), axis=0)
    own = contract_last(rows_of(enter(grad_projected), 0, 4), qkv_full)
    result = mixed + add_last(own_rows(*enter(*result_sums)), last_x, last_y)
    out_term = contract_first(enter(attended_low), mixed_all).astype(BF16)
    from_x, from_y, own, result, out_term, hidden_sum = seal(
        flip_x(to_x), flip_y(to_y), own, result, out_term, hidden_sum
    )
    sums = enter(own, near, from_x, from_y)
    to_x, to_y = last_sends(*sums)
    last_x, last_y, own, qkv_sum = seal(
        flip_x(to_x), flip_y(to_y), own_rows(*after(sums, to_x, to_y)), qkv_sum
    )

    grad_input_norm, gain_one, bias_one = first_pull(add_last(*enter(own, last_x, last_y)))
    grad_input = (grad_mixed + grad_input_norm).astype(BF16)
    up_got = exchange(*enter(*up_pair))
    qkv_pair = split_sum(enter(qkv_sum))
    up_got, qkv_pair, gain_one, bias_one, grad_input, result = seal(
        up_got, qkv_pair, gain_one, bias_one, grad_input, result.astype(BF16)
    )

    norms = sum_blk(enter(jnp.stack([gain_one, gain_two, bias_one, bias_two])))
    qkv_got = exchange(*enter(*qkv_pair))
    out_sum = scatter_z(after(out_term, qkv_sum), 0)
    grad_up = merge_columns(enter(up_got), *up_cut)
    norms, hidden_sum = sum_dp(norms, hidden_sum)
    grad_qkv = merge_columns(qkv_got, *qkv_cut)
    out_sum = after(out_sum, norms)
    grad_out = lax.ppermute(out_sum, "dp", [(j, i) for i, j in route]).astype(F32)
    return (
        result.reshape(1, 1, rows, width),
        grad_input.reshape(1, 1, rows, width),
        grad_qkv,
        grad_out,
        grad_up,
        down_sum.astype(F32),
        norms[:2],
        norms[2:],
        hidden_sum,
    )


def solution(mesh):
    return jax.shard_map(
        body,
        mesh=mesh,
        in_specs=(
            P("dp", "blk", None, None),
            P("dp", "blk", None, None),
            P("dp", None),
            P(),
            P(("blk", "dp"), None),
            P(("blk", "dp"), None),
            P(("blk", "dp"), None),
            P(("blk", "dp"), None),
            P(),
            P(),
            P(),
        ),
        out_specs=(
            P("dp", "blk", None, None),
            P("dp", "blk", None, None),
            P(("blk", "dp"), None),
            P(("blk", "dp"), None),
            P(("blk", "dp"), None),
            P(("blk", "dp"), None),
            P(None, ("blk", "dp")),
            P(None, ("blk", "dp")),
            P(("blk", "dp")),
        ),
        check_vma=False,
    )
```
